256 devices in a mesh: prow: 16 (over z, core), pcol: 16 (over y, x).
Axes of the slice: x: 4, y: 4, z: 8, core: 2. Of those that a mesh axis runs over, the one named last changes fastest.
Arguments:
- log_derivs: bfloat16 [512, 16384], P('pcol', 'prow'), may hold values from -12 to 12
- energy_derivs: bfloat16 [512, 16384], P('pcol', 'prow'), may hold values from -6 to 6
- start_block: float32 [16384, 32], P(('prow', 'pcol')), may hold values from -6 to 6
Outputs:
- block_one: float32 [16384, 32], P(('prow', 'pcol'))
- block_two: float32 [16384, 32], P(('prow', 'pcol'))
- rayleigh: float32 [32, 32], replicated
- correlation_tiles: float32 [16, 16384, 1024], P('pcol', 'prow')
- hamiltonian_tiles: float32 [16, 16384, 1024], P('pcol', 'prow')
The draws below stay inside these ranges and needn't reach their ends.
All inputs are finite; a program needn't handle non-finite values.
Results may differ from the reference program's by a relative error of at most 0.0003.
Values may be sent and summed in bfloat16 or wider, within the bound.
A program may use at most 64 MiB of HBM per device.

```python
import math
import jax
import jax.numpy as jnp
from jax import lax

PARAMS = 16384
VECS = 32
WALKERS = 512
N_PROW = 16
N_PCOL = 16


def draw_log_derivs(key, part):
    key = jax.random.fold_in(key, 11)
    key_base, key_cols = jax.random.split(key, 2)
    col_scale = jnp.exp(jax.random.uniform(key_cols, (1, PARAMS), jnp.float32, math.log(0.3), math.log(3.0)))
    values = jnp.clip(jax.random.normal(key_base, (WALKERS, PARAMS), jnp.float32), -4.0, 4.0) * col_scale
    return values.astype(jnp.bfloat16)


def block_levels(own_key, shape, cuts, smallest, largest):
    loudness, own = 1.0, jax.random.fold_in(own_key, 6)
    for axis_at, shards_of in cuts:
        draws = jnp.exp(jax.random.uniform(jax.random.fold_in(own, axis_at), (shards_of,), jnp.float32, smallest / len(cuts), largest / len(cuts)))
        loudness = loudness * jnp.repeat(draws, shape[axis_at] // shards_of).reshape([-1 if axis == axis_at else 1 for axis in range(len(shape))])
    return loudness


def centred(rng, extent, width, bound, shards=(), kind=jnp.bfloat16):
    level = block_levels(rng, extent, shards, -0.22, 0.18) if shards else 1.0
    entries = jax.random.normal(rng, extent, jnp.float32) * width * level
    return jnp.minimum(jnp.maximum(entries, -bound), bound).astype(kind)


def setup_inputs(seed: int = 0) -> dict:
    streams_of = jax.random.split(jax.random.key(seed), 4)
    return {
        "log_derivs": draw_log_derivs(jax.random.fold_in(streams_of[3], 71), 0),
        "energy_derivs": centred(streams_of[1], (WALKERS, PARAMS), 1.0, 6.0, ((0, 16), (1, 16))),
        "start_block": centred(streams_of[2], (PARAMS, VECS), 1.0, 6.0, ((0, 256),), jnp.float32),
    }


stabilizer = 0.5
epsilon = 1e-06
highest = lax.Precision.HIGHEST

def expansion(log_values, energy_values, diagonal_s, basis):
    walkers = log_values.shape[0]
    image_s = jnp.dot(log_values.T, jnp.dot(log_values, basis, precision=highest), precision=highest) / walkers + stabilizer * basis
    image_h = jnp.dot(log_values.T, jnp.dot(energy_values, basis, precision=highest), precision=highest) / walkers
    rayleigh_s = jnp.dot(basis.T, image_s, precision=highest)
    rayleigh_h = jnp.dot(basis.T, image_h, precision=highest)
    lower_factor = jnp.linalg.cholesky(rayleigh_s)
    coeffs = jax.scipy.linalg.cho_solve((lower_factor, True), rayleigh_h)
    residual = (image_h - jnp.dot(image_s, coeffs, precision=highest)) / diagonal_s[:, None]
    sum_squares = lax.optimization_barrier(jnp.sum(residual * residual, axis=0))
    return (residual / jnp.sqrt(sum_squares / PARAMS + epsilon), coeffs)

def arrange(matrix):
    fine_cols = PARAMS // (N_PROW * N_PCOL)
    split_view = matrix.reshape(PARAMS, N_PROW, N_PCOL, fine_cols)
    return jnp.transpose(split_view, (2, 0, 1, 3)).reshape(N_PCOL, PARAMS, PARAMS // N_PCOL)

def reference(log_derivs, energy_derivs, start_block):
    log_values = log_derivs.astype(jnp.float32)
    energy_values = energy_derivs.astype(jnp.float32)
    walkers = log_derivs.shape[0]
    diagonal_s = lax.optimization_barrier(jnp.sum(log_values * log_values, axis=0)) / walkers + stabilizer
    block_one, first_coeffs = expansion(log_values, energy_values, diagonal_s, start_block)
    block_two, rayleigh = expansion(log_values, energy_values, diagonal_s, block_one)
    correlation = jnp.dot(log_derivs.T.astype(jnp.float32), log_derivs.astype(jnp.float32), preferred_element_type=jnp.float32) / walkers
    positions = jnp.arange(PARAMS, dtype=jnp.int32)
    correlation = correlation.at[positions, positions].add(stabilizer)
    correlation_tiles = arrange(correlation)
    hamiltonian = jnp.dot(log_derivs.T.astype(jnp.float32), energy_derivs.astype(jnp.float32), preferred_element_type=jnp.float32) / walkers
    hamiltonian_tiles = arrange(hamiltonian)
    return (block_one, block_two, rayleigh, correlation_tiles, hamiltonian_tiles)
```

```python
import functools

import jax
import jax.numpy as jnp
from jax import lax
from jax.experimental import pallas as pl
from jax.experimental.pallas import tpu as pltpu
from jax.sharding import PartitionSpec as P

STABILIZER = 0.5
EPSILON = 1e-6
F32 = jnp.float32
BF16 = jnp.bfloat16
HIGHEST = lax.Precision.HIGHEST
MESH = pl.DeviceIdType.MESH
NT = (((1,), (1,)), ((), ()))
TN = (((0,), (0,)), ((), ()))


def pieces(x):
    high = x.astype(BF16)
    rest = x - high.astype(F32)
    middle = rest.astype(BF16)
    low = (rest - middle.astype(F32)).astype(BF16)
    return jnp.concatenate([high, middle, low], axis=0)


def sum_rows(x, n):
    return x[:n] + x[n : 2 * n] + x[2 * n : 3 * n]


def to_row(column, eye):
    return jnp.sum(jnp.where(eye, column, 0.0), axis=0, keepdims=True)


def to_column(row, eye):
    return jnp.sum(jnp.where(eye, row, 0.0), axis=1, keepdims=True)


def pack_image(x):
    tail = x[24:32]
    side = jnp.concatenate([tail[:, 0:32], tail[:, 32:64], tail[:, 64:96]], axis=0)
    return jnp.concatenate([x[:24], side], axis=1)


def unpack_image(x):
    tail = jnp.concatenate([x[0:8, 96:], x[8:16, 96:], x[16:24, 96:]], axis=1)
    return jnp.concatenate([x[:, :96], tail], axis=0)


def fold(x):
    return jnp.concatenate([x[8 * g : 8 * g + 8] for g in range(4)], axis=1)


def unfold(folded):
    return jnp.concatenate(
        [
            jnp.concatenate([x[:, 32 * g : 32 * g + 32] for x in folded], axis=1)
            for g in range(4)
        ],
        axis=0,
    )


def eliminate(matrix, right):
    n = matrix.shape[0]
    both = jnp.concatenate([matrix, right], axis=1)
    rows = lax.broadcasted_iota(jnp.int32, both.shape, 0)
    for k in range(n):
        row = both[k : k + 1] / both[k : k + 1, k : k + 1]
        both = jnp.where(rows == k, row, both - both[:, k : k + 1] * row)
    return both[:, n:]


def davidson(
    nr,
    nc,
    l_ref,
    e_ref,
    v_ref,
    own_t_ref,
    cols_ref,
    one_ref,
    two_ref,
    ray_ref,
    block,
    slabs,
    gathered,
    v_send,
    v_recv,
    stacked,
    basis,
    pair_send,
    pair_recv,
    image_send,
    image_recv,
    walk_send,
    walk_recv,
    norm_send,
    norm_recv,
    sends,
    recvs,
    ring_sems,
):
    p = lax.axis_index("prow")
    q = lax.axis_index("pcol")
    z = p // 2
    core = p % 2
    nz = nr // 2
    wide = 64 * nc
    walkers = 32 * nc
    params = wide * nr

    def row_of(zz, cc):
        return lax.rem(zz + nz, nz) * 2 + cc

    sibling = z * 2 + 1 - core

    def push(src, dst, send_sem, recv_sem, device):
        pltpu.make_async_remote_copy(
            src_ref=src,
            dst_ref=dst,
            send_sem=send_sem,
            recv_sem=recv_sem,
            device_id=device,
            device_id_type=MESH,
        ).start()

    def sent(ref, sem):
        pltpu.make_async_remote_copy(
            src_ref=ref,
            dst_ref=ref,
            send_sem=sem,
            recv_sem=sem,
            device_id={"prow": sibling},
            device_id_type=MESH,
        ).wait_send()

    def landed(ref, sem):
        pltpu.make_async_remote_copy(
            src_ref=ref,
            dst_ref=ref,
            send_sem=sem,
            recv_sem=sem,
            device_id={"prow": sibling},
            device_id_type=MESH,
        ).wait_recv()

    barrier = pltpu.get_barrier_semaphore()

    def greet_col(i, carry):
        pl.semaphore_signal(
            barrier, inc=1, device_id={"pcol": lax.rem(q + i, nc)}, device_id_type=MESH
        )
        return carry

    def greet_row(i, carry):
        pl.semaphore_signal(
            barrier, inc=1, device_id={"prow": lax.rem(p + i, nr)}, device_id_type=MESH
        )
        return carry

    lax.fori_loop(1, nc, greet_col, 0)
    lax.fori_loop(1, nr, greet_row, 0)
    v_own = v_ref[...]
    v_send[...] = jnp.concatenate([v_own[:16], v_own[16:]], axis=1)
    v_recv[pl.ds(q, 1)] = v_send[...][None]
    l_own = l_ref[...]
    e_own = e_ref[...]
    for j in range(nc):
        slabs[j] = jnp.concatenate(
            [l_own[:, 64 * j : 64 * j + 64], e_own[:, 64 * j : 64 * j + 64]], axis=1
        )
    own_rows = pl.ds(pl.multiple_of(q * 32, 32), 32)
    gathered[pl.ds(p, 1), own_rows, :] = slabs[pl.ds(q, 1)]
    block[own_rows, :] = l_own
    stacked[0:32] = l_own
    stacked[32:64] = e_own
    pl.semaphore_wait(barrier, nc - 1 + nr - 1)

    def to_plane(copy):
        def body(i, carry):
            copy(lax.rem(q + i, nc))
            return carry

        lax.fori_loop(1, nc, body, 0)

    to_plane(
        lambda peer: push(
            v_send, v_recv.at[q], sends.at[0], recvs.at[0], {"pcol": peer}
        )
    )
    to_plane(
        lambda peer: push(
            slabs.at[peer],
            gathered.at[p, own_rows],
            sends.at[1],
            recvs.at[1],
            {"pcol": peer},
        )
    )
    to_plane(
        lambda peer: push(
            l_ref, block.at[own_rows], sends.at[2], recvs.at[2], {"pcol": peer}
        )
    )

    eye = lax.broadcasted_iota(jnp.int32, (32, 32), 0) == lax.broadcasted_iota(
        jnp.int32, (32, 32), 1
    )
    far = pl.ds(0, nc - 1)

    full = nz // 2 - 1
    half = walkers // 2
    everything, lower, upper = pl.ds(0, walkers), pl.ds(0, half), pl.ds(half, half)

    def ring_send(step):
        for way, sign in ((0, 1), (1, -1)):
            chunk = row_of(z - sign * step, core)
            part = everything if step < full else (lower, upper)[way]
            ref = gathered.at[chunk, part]
            push(
                ref,
                ref,
                ring_sems.at[0, way, step],
                ring_sems.at[1, way, step],
                {"prow": row_of(z + sign, core)},
            )

    def ring_landed(step):
        for way, sign in ((0, 1), (1, -1)):
            chunk = row_of(z - sign * (step + 1), core)
            part = everything if step < full else (lower, upper)[way]
            ref = gathered.at[chunk, part]
            landed(ref, ring_sems.at[1, way, step])
            push(
                ref,
                ref,
                ring_sems.at[2, way, step],
                ring_sems.at[3, way, step],
                {"prow": sibling},
            )

    def ring_finish():
        own = gathered.at[p]
        sent(own, ring_sems.at[2, 0, full + 1])
        landed(gathered.at[sibling], ring_sems.at[3, 0, full + 1])
        for step in range(full + 1):
            for way, sign in ((0, 1), (1, -1)):
                part = everything if step < full else (lower, upper)[way]
                chunk = row_of(z - sign * (step + 1), 1 - core)
                ref = gathered.at[chunk, part]
                sent(ref, ring_sems.at[0, way, step])
                sent(ref, ring_sems.at[2, way, step])
                landed(ref, ring_sems.at[3, way, step])

    def ring_at(point):
        if point == 0:
            landed(gathered.at[0, pl.ds(0, 32 * (nc - 1))], recvs.at[1])
            ring_send(0)
            own = gathered.at[p]
            push(
                own,
                own,
                ring_sems.at[2, 0, full + 1],
                ring_sems.at[3, 0, full + 1],
                {"prow": sibling},
            )
        elif point <= full + 1:
            ring_landed(point - 1)
            if point <= full:
                ring_send(point)

    def image(vec, turn, first):
        split = pieces(vec)
        stacked[64:160] = split
        out = lax.dot_general(split, stacked[...], NT, preferred_element_type=F32)
        out = sum_rows(out, 32)
        gram = out[:, 64:96] + out[:, 96:128] + out[:, 128:160]
        pair_send[turn] = pack_image(jnp.concatenate([out[:, :64], gram], axis=1))
        push(
            pair_send.at[turn],
            pair_recv.at[turn],
            sends.at[4 + turn],
            recvs.at[4 + turn],
            {"prow": sibling},
        )
        landed(pair_recv.at[turn], recvs.at[4 + turn])
        mine = pair_send[turn] + pair_recv[turn]
        image_send[turn] = mine
        image_recv[turn, pl.ds(z, 1)] = mine[None]

        def body(i, carry):
            push(
                image_send.at[turn],
                image_recv.at[turn, z],
                sends.at[6 + turn],
                recvs.at[6 + turn],
                {"prow": row_of(z + i, core)},
            )
            return carry

        lax.fori_loop(1, nz, body, 0)
        ring_at(first)
        landed(image_recv.at[turn, pl.ds(0, nz - 1)], recvs.at[6 + turn])
        total = image_recv[turn, 0]
        for k in range(1, nz):
            total = total + image_recv[turn, k]
        total = unpack_image(total)
        gram = total[:, 64:96]
        mine = jnp.concatenate([fold(total[:, :32]), fold(total[:, 32:64])], axis=0)
        walk_send[turn] = mine
        walk_recv[turn, pl.ds(q, 1)] = mine[None]
        to_plane(
            lambda peer: push(
                walk_send.at[turn],
                walk_recv.at[turn, q],
                sends.at[8 + turn],
                recvs.at[8 + turn],
                {"pcol": peer},
            )
        )
        ring_at(first + 1)
        landed(walk_recv.at[turn, far], recvs.at[8 + turn])
        values = []
        for rows in (slice(0, 8), slice(8, 16)):
            values.append(
                jnp.concatenate(
                    [
                        unfold([walk_recv[turn, k + j, rows] for j in range(4)])
                        for k in range(0, nc, 4)
                    ],
                    axis=1,
                )
            )
        return values[0], values[1], gram

    def residual(vec, l_val, e_val, gram, inverse_diag):
        l_split = pieces(l_val)
        both = jnp.concatenate([l_split, pieces(e_val)], axis=0)
        out = sum_rows(
            lax.dot_general(l_split, both, NT, preferred_element_type=F32), 32
        )
        ray_s = out[:, :32] + out[:, 32:64] + out[:, 64:96]
        ray_h = out[:, 96:128] + out[:, 128:160] + out[:, 160:192]
        coeffs = eliminate(
            ray_s * (1.0 / walkers) + STABILIZER * gram, ray_h * (1.0 / walkers)
        )
        mixed = lax.dot_general(
            coeffs,
            jnp.concatenate([l_val, vec], axis=1),
            TN,
            precision=HIGHEST,
            preferred_element_type=F32,
        )
        rest = (e_val - mixed[:, :walkers]) * (1.0 / walkers)
        out = jnp.dot(pieces(rest), block[...], preferred_element_type=F32)
        out = sum_rows(out, 32) - STABILIZER * mixed[:, walkers:]
        return out * inverse_diag, coeffs

    def own_part(vec):
        for k in range(nc // 2):
            basis[k] = vec[:, 128 * k : 128 * k + 128]
        chunk = basis[pl.ds(q // 2, 1)][0]
        return jnp.where(q % 2 == 0, chunk[:, :64], chunk[:, 64:])

    landed(v_recv.at[far], recvs.at[0])
    top, bottom = [], []
    for k in range(0, nc, 2):
        a, b = v_recv[k], v_recv[k + 1]
        top += [a[:, :64], b[:, :64]]
        bottom += [a[:, 64:], b[:, 64:]]
    vec = jnp.concatenate(
        [jnp.concatenate(top, axis=1), jnp.concatenate(bottom, axis=1)], axis=0
    )
    l_val, e_val, gram = image(vec, 0, 0)
    landed(block.at[pl.ds(0, 32 * (nc - 1))], recvs.at[2])
    squares = jnp.zeros((8, wide), F32)
    for k in range(0, walkers, 16):
        part = block[k : k + 16].astype(F32)
        part = part * part
        squares = squares + part[:8] + part[8:]
    inverse_diag = 1.0 / (
        jnp.sum(squares, axis=0, keepdims=True) * (1.0 / walkers) + STABILIZER
    )
    vec, _ = residual(vec, l_val, e_val, gram, inverse_diag)

    l_val, e_val, gram = image(vec, 1, 2)
    norms = jnp.sum(jnp.where(eye, gram, 0.0), axis=1, keepdims=True)
    scale = 1.0 / jnp.sqrt(norms * (1.0 / params) + EPSILON)
    scale_row = to_row(scale, eye)
    vec = vec * scale
    one_ref[...] = own_part(vec)
    vec, coeffs = residual(
        vec, l_val * scale, e_val * scale, gram * scale * scale_row, inverse_diag
    )
    ray_ref[...] = coeffs

    norms = to_row(jnp.sum(vec * vec, axis=1, keepdims=True), eye)
    norm_send[...] = jnp.concatenate([norms, jnp.zeros((1, 96), F32)], axis=1)
    norm_recv[pl.ds(p, 1)] = norm_send[...][None]

    def send_norm(i, carry):
        push(
            norm_send,
            norm_recv.at[p],
            sends.at[3],
            recvs.at[3],
            {"prow": lax.rem(p + i, nr)},
        )
        return carry

    lax.fori_loop(1, nr, send_norm, 0)
    for point in range(4, full + 2):
        ring_at(point)
    own_t_ref[...] = block[...].T
    landed(norm_recv.at[pl.ds(0, nr - 1)], recvs.at[3])
    norms = norm_recv[0]
    for k in range(1, nr):
        norms = norms + norm_recv[k]
    norms = to_column(norms[:, :32], eye)
    two_ref[...] = own_part(vec) * (1.0 / jnp.sqrt(norms * (1.0 / params) + EPSILON))

    ring_finish()
    for k in range(nr // 2):
        a, b = gathered[2 * k], gathered[2 * k + 1]
        cols_ref[:, 128 * k : 128 * k + 128] = jnp.concatenate(
            [a[:, :64], b[:, :64]], axis=1
        )
        cols_ref[:, 64 * nr + 128 * k : 64 * nr + 128 * k + 128] = jnp.concatenate(
            [a[:, 64:], b[:, 64:]], axis=1
        )

    sent(v_recv.at[far], sends.at[0])
    sent(gathered.at[0, pl.ds(0, 32 * (nc - 1))], sends.at[1])
    sent(block.at[pl.ds(0, 32 * (nc - 1))], sends.at[2])
    sent(norm_recv.at[pl.ds(0, nr - 1)], sends.at[3])
    for turn in range(2):
        sent(pair_send.at[turn], sends.at[4 + turn])
        sent(image_recv.at[turn, pl.ds(0, nz - 1)], sends.at[6 + turn])
        sent(walk_recv.at[turn, far], sends.at[8 + turn])


def tiles(
    walkers, own_t, cols, one, two, ray, corr_ref, ham_ref, one_out, two_out, ray_out
):
    step = pl.program_id(0)
    p = lax.axis_index("prow")
    q = lax.axis_index("pcol")
    rows, width = corr_ref.shape[1:]

    @pl.when(step == 0)
    def _():
        one_out[...] = one[...]
        two_out[...] = two[...]
        ray_out[...] = ray[...]

    left = own_t[...]
    corr_ref[0] = jnp.dot(
        left, cols[:, :width], preferred_element_type=F32
    ) * (1.0 / walkers)
    ham_ref[0] = jnp.dot(
        left, cols[:, width:], preferred_element_type=F32
    ) * (1.0 / walkers)

    @pl.when(step == q * 64 // rows)
    def _():
        row = lax.broadcasted_iota(jnp.int32, (rows, width), 0) + step * rows - q * 64
        column = lax.broadcasted_iota(jnp.int32, (rows, width), 1) - p * 64
        hit = (row == column) & (row >= 0) & (row < 64)
        corr_ref[0] += jnp.where(hit, STABILIZER, 0.0)


def local(nr, nc, log_derivs, energy_derivs, start_block):
    wide, walkers, narrow = 64 * nc, 32 * nc, 64 * nr
    nz = nr // 2
    vmem = pl.BlockSpec(memory_space=pltpu.VMEM)
    full = nz // 2 - 1
    own_t, cols, one, two, ray = pl.pallas_call(
        functools.partial(davidson, nr, nc),
        out_shape=(
            jax.ShapeDtypeStruct((wide, walkers), BF16),
            jax.ShapeDtypeStruct((walkers, 2 * narrow), BF16),
            jax.ShapeDtypeStruct((32, 64), F32),
            jax.ShapeDtypeStruct((32, 64), F32),
            jax.ShapeDtypeStruct((32, 32), F32),
        ),
        in_specs=[vmem] * 3,
        out_specs=(vmem,) * 5,
        scratch_shapes=[
            pltpu.VMEM((walkers, wide), BF16),
            pltpu.VMEM((nc, 32, 128), BF16),
            pltpu.VMEM((nr, walkers, 128), BF16),
            pltpu.VMEM((16, 128), F32),
            pltpu.VMEM((nc, 16, 128), F32),
            pltpu.VMEM((160, wide), BF16),
            pltpu.VMEM((nc // 2, 32, 128), F32),
            pltpu.VMEM((2, 24, 128), F32),
            pltpu.VMEM((2, 24, 128), F32),
            pltpu.VMEM((2, 24, 128), F32),
            pltpu.VMEM((2, nz, 24, 128), F32),
            pltpu.VMEM((2, 16, 128), F32),
            pltpu.VMEM((2, nc, 16, 128), F32),
            pltpu.VMEM((1, 128), F32),
            pltpu.VMEM((nr, 1, 128), F32),
            pltpu.SemaphoreType.DMA((10,)),
            pltpu.SemaphoreType.DMA((10,)),
            pltpu.SemaphoreType.DMA((4, 2, full + 2)),
        ],
        compiler_params=pltpu.CompilerParams(
            collective_id=0, has_side_effects=True, vmem_limit_bytes=40 * 1024 * 1024
        ),
        name="davidson",
    )(log_derivs, energy_derivs, start_block.T)

    rows = min(128, wide)
    small = lambda shape: pl.BlockSpec(shape, lambda i: (0, 0))
    corr, ham, one, two, ray = pl.pallas_call(
        functools.partial(tiles, walkers),
        grid=(wide // rows,),
        out_shape=(
            jax.ShapeDtypeStruct((1, wide, narrow), F32),
            jax.ShapeDtypeStruct((1, wide, narrow), F32),
            jax.ShapeDtypeStruct((32, 64), F32),
            jax.ShapeDtypeStruct((32, 64), F32),
            jax.ShapeDtypeStruct((32, 32), F32),
        ),
        in_specs=[
            pl.BlockSpec((rows, walkers), lambda i: (i, 0)),
            small((walkers, 2 * narrow)),
            small((32, 64)),
            small((32, 64)),
            small((32, 32)),
        ],
        out_specs=(
            pl.BlockSpec((1, rows, narrow), lambda i: (0, i, 0)),
            pl.BlockSpec((1, rows, narrow), lambda i: (0, i, 0)),
            small((32, 64)),
            small((32, 64)),
            small((32, 32)),
        ),
        compiler_params=pltpu.CompilerParams(vmem_limit_bytes=24 * 1024 * 1024),
        name="tiles",
    )(own_t, cols, one, two, ray)
    return one.T, two.T, ray, corr, ham


def solution(mesh):
    return jax.shard_map(
        functools.partial(local, mesh.shape["prow"], mesh.shape["pcol"]),
        mesh=mesh,
        in_specs=(P("pcol", "prow"), P("pcol", "prow"), P(("prow", "pcol"), None)),
        out_specs=(
            P(("prow", "pcol"), None),
            P(("prow", "pcol"), None),
            P(),
            P("pcol", "prow", None),
            P("pcol", "prow", None),
        ),
        check_vma=False,
    )
```

```python
import contextlib
import functools

import jax
import jax.numpy as jnp
from jax import lax
from jax.experimental import pallas as pl
from jax.experimental.pallas import tpu as pltpu
from jax.sharding import PartitionSpec as P

STABILIZER = 0.5
EPSILON = 1e-6
F32 = jnp.float32
BF16 = jnp.bfloat16
HIGHEST = lax.Precision.HIGHEST
MESH = pl.DeviceIdType.MESH
NT = (((1,), (1,)), ((), ()))
TN = (((0,), (0,)), ((), ()))


def scope(name):
    return contextlib.nullcontext()


def pieces(x):
    high = x.astype(BF16)
    rest = x - high.astype(F32)
    middle = rest.astype(BF16)
    low = (rest - middle.astype(F32)).astype(BF16)
    return jnp.concatenate([high, middle, low], axis=0)


def sum_rows(x, n):
    return x[:n] + x[n : 2 * n] + x[2 * n : 3 * n]


def to_row(column, eye):
    return jnp.sum(jnp.where(eye, column, 0.0), axis=0, keepdims=True)


def to_column(row, eye):
    return jnp.sum(jnp.where(eye, row, 0.0), axis=1, keepdims=True)


def pack_image(x):
    tail = x[24:32]
    side = jnp.concatenate([tail[:, 0:32], tail[:, 32:64], tail[:, 64:96]], axis=0)
    return jnp.concatenate([x[:24], side], axis=1)


def unpack_image(x):
    tail = jnp.concatenate([x[0:8, 96:], x[8:16, 96:], x[16:24, 96:]], axis=1)
    return jnp.concatenate([x[:, :96], tail], axis=0)


def fold(x):
    return jnp.concatenate([x[8 * g : 8 * g + 8] for g in range(4)], axis=1)


def unfold(folded):
    return jnp.concatenate(
        [
            jnp.concatenate([x[:, 32 * g : 32 * g + 32] for x in folded], axis=1)
            for g in range(4)
        ],
        axis=0,
    )


def inverse_of_two(a, b, d):
    scale = 1.0 / (a * d - b * b)
    return d * scale, -b * scale, a * scale


def eliminate(matrix, right, eye):
    n = matrix.shape[0]
    diagonal = jnp.where(eye, matrix, 0.0)
    unit = lax.rsqrt(jnp.sum(diagonal, axis=1, keepdims=True))
    unit_row = lax.rsqrt(jnp.sum(diagonal, axis=0, keepdims=True))
    both = jnp.concatenate([matrix * unit * unit_row, right * unit], axis=1)
    rows = lax.broadcasted_iota(jnp.int32, both.shape, 0)
    for k in range(0, n, 4):
        c = [jnp.broadcast_to(both[:, k + j : k + j + 1], both.shape) for j in range(4)]
        r = [both[k + i : k + i + 1] for i in range(4)]
        g = [[c[j][k + i : k + i + 1] for j in range(4)] for i in range(4)]
        p0, p1, p2 = inverse_of_two(g[0][0], g[1][0], g[1][1])
        u0, u1 = p0 * r[0] + p1 * r[1], p1 * r[0] + p2 * r[1]
        t02, t12 = p0 * g[2][0] + p1 * g[2][1], p1 * g[2][0] + p2 * g[2][1]
        t03, t13 = p0 * g[3][0] + p1 * g[3][1], p1 * g[3][0] + p2 * g[3][1]
        w0, w1, w2 = inverse_of_two(
            g[2][2] - g[2][0] * t02 - g[2][1] * t12,
            g[3][2] - g[3][0] * t02 - g[3][1] * t12,
            g[3][3] - g[3][0] * t03 - g[3][1] * t13,
        )
        v2 = r[2] - g[2][0] * u0 - g[2][1] * u1
        v3 = r[3] - g[3][0] * u0 - g[3][1] * u1
        x2, x3 = w0 * v2 + w1 * v3, w1 * v2 + w2 * v3
        x = (u0 - t02 * x2 - t03 * x3, u1 - t12 * x2 - t13 * x3, x2, x3)
        both = both - c[0] * x[0] - c[1] * x[1] - c[2] * x[2] - c[3] * x[3]
        for i in range(4):
            both = jnp.where(rows == k + i, x[i], both)
    return both[:, n:] * unit


def davidson(
    nr,
    nc,
    l_hbm,
    e_hbm,
    v_hbm,
    own_t_ref,
    cols_ref,
    one_ref,
    two_ref,
    ray_ref,
    l_ref,
    e_ref,
    v_ref,
    block,
    slabs,
    gathered,
    v_send,
    v_recv,
    stacked,
    basis,
    pair_send,
    pair_recv,
    image_send,
    image_recv,
    walk_send,
    walk_recv,
    norm_send,
    norm_recv,
    loads,
    sends,
    recvs,
    ring_sems,
):
    p = lax.axis_index("prow")
    q = lax.axis_index("pcol")
    z = p // 2
    core = p % 2
    nz = nr // 2
    wide = 64 * nc
    walkers = 32 * nc
    params = wide * nr

    def row_of(zz, cc):
        return lax.rem(zz + nz, nz) * 2 + cc

    sibling = z * 2 + 1 - core

    def push(src, dst, send_sem, recv_sem, device):
        pltpu.make_async_remote_copy(
            src_ref=src,
            dst_ref=dst,
            send_sem=send_sem,
            recv_sem=recv_sem,
            device_id=device,
            device_id_type=MESH,
        ).start()

    def sent(ref, sem):
        pltpu.make_async_remote_copy(
            src_ref=ref,
            dst_ref=ref,
            send_sem=sem,
            recv_sem=sem,
            device_id={"prow": sibling},
            device_id_type=MESH,
        ).wait_send()

    def landed(ref, sem):
        pltpu.make_async_remote_copy(
            src_ref=ref,
            dst_ref=ref,
            send_sem=sem,
            recv_sem=sem,
            device_id={"prow": sibling},
            device_id_type=MESH,
        ).wait_recv()

    reads = [
        pltpu.make_async_copy(src, dst, loads.at[i])
        for i, (src, dst) in enumerate(((v_hbm, v_ref), (l_hbm, l_ref), (e_hbm, e_ref)))
    ]
    for read in reads:
        read.start()

    barrier = pltpu.get_barrier_semaphore()

    def greet_col(i, carry):
        pl.semaphore_signal(
            barrier, inc=1, device_id={"pcol": lax.rem(q + i, nc)}, device_id_type=MESH
        )
        return carry

    def greet_row(i, carry):
        pl.semaphore_signal(
            barrier, inc=1, device_id={"prow": lax.rem(p + i, nr)}, device_id_type=MESH
        )
        return carry

    lax.fori_loop(1, nc, greet_col, 0)
    lax.fori_loop(1, nr, greet_row, 0)

    def to_plane(copy):
        def body(i, carry):
            copy(lax.rem(q + i, nc))
            return carry

        lax.fori_loop(1, nc, body, 0)

    reads[0].wait()
    v_own = v_ref[...]
    v_send[...] = jnp.concatenate([v_own[:16], v_own[16:]], axis=1)
    v_recv[pl.ds(q, 1)] = v_send[...][None]
    reads[1].wait()
    reads[2].wait()
    l_own = l_ref[...]
    e_own = e_ref[...]
    for j in range(nc):
        slabs[j] = jnp.concatenate(
            [l_own[:, 64 * j : 64 * j + 64], e_own[:, 64 * j : 64 * j + 64]], axis=1
        )
    own_rows = pl.ds(pl.multiple_of(q * 32, 32), 32)
    gathered[pl.ds(p, 1), own_rows, :] = slabs[pl.ds(q, 1)]
    block[own_rows, :] = l_own
    stacked[0:32] = l_own
    stacked[32:64] = e_own
    with scope("loaded"):
        pass
    with scope("barrier"):
        pl.semaphore_wait(barrier, nc - 1 + nr - 1)
    to_plane(
        lambda peer: push(
            v_send, v_recv.at[q], sends.at[0], recvs.at[0], {"pcol": peer}
        )
    )
    to_plane(
        lambda peer: push(
            slabs.at[peer],
            gathered.at[p, own_rows],
            sends.at[1],
            recvs.at[1],
            {"pcol": peer},
        )
    )

    nx = 4
    ny = nc // nx
    x, y = q % nx, q // nx

    def along_x(i):
        return y * nx + lax.rem(x + i, nx)

    def along_y(i):
        return lax.rem(y + i, ny) * nx + x

    def half_of(member, part):
        return block.at[pl.ds(pl.multiple_of(member * 32 + 16 * part, 16), 16)]

    def block_first():
        for i in range(1, nx):
            ref = half_of(q, 0)
            push(ref, ref, sends.at[2], recvs.at[2], {"pcol": along_x(i)})
        for i in range(1, ny):
            ref = half_of(q, 1)
            push(ref, ref, sends.at[10], recvs.at[10], {"pcol": along_y(i)})

    def block_second():
        landed(block.at[pl.ds(0, 16 * (nx - 1))], recvs.at[2])
        landed(block.at[pl.ds(0, 16 * (ny - 1))], recvs.at[10])

        def forward_y(i, carry):
            for k in range(nx):
                ref = half_of(along_x(k), 0)
                push(ref, ref, sends.at[11], recvs.at[11], {"pcol": along_y(i)})
            return carry

        def forward_x(i, carry):
            for k in range(ny):
                ref = half_of(along_y(k), 1)
                push(ref, ref, sends.at[12], recvs.at[12], {"pcol": along_x(i)})
            return carry

        lax.fori_loop(1, ny, forward_y, 0)
        lax.fori_loop(1, nx, forward_x, 0)

    counts = (nx - 1, ny - 1, nx * (ny - 1), ny * (nx - 1))

    def block_landed():
        for sem, count in zip((11, 12), counts[2:], strict=True):
            landed(block.at[pl.ds(0, 16 * count)], recvs.at[sem])

    def block_sent():
        for sem, count in zip((2, 10, 11, 12), counts, strict=True):
            sent(block.at[pl.ds(0, 16 * count)], sends.at[sem])

    block_first()

    eye = lax.broadcasted_iota(jnp.int32, (32, 32), 0) == lax.broadcasted_iota(
        jnp.int32, (32, 32), 1
    )
    far = pl.ds(0, nc - 1)

    full = nz // 2 - 1
    half = walkers // 2
    everything, lower, upper = pl.ds(0, walkers), pl.ds(0, half), pl.ds(half, half)

    def ring_send(step):
        for way, sign in ((0, 1), (1, -1)):
            chunk = row_of(z - sign * step, core)
            part = everything if step < full else (lower, upper)[way]
            ref = gathered.at[chunk, part]
            push(
                ref,
                ref,
                ring_sems.at[0, way, step],
                ring_sems.at[1, way, step],
                {"prow": row_of(z + sign, core)},
            )

    def ring_landed(step):
        for way, sign in ((0, 1), (1, -1)):
            chunk = row_of(z - sign * (step + 1), core)
            part = everything if step < full else (lower, upper)[way]
            ref = gathered.at[chunk, part]
            landed(ref, ring_sems.at[1, way, step])
            push(
                ref,
                ref,
                ring_sems.at[2, way, step],
                ring_sems.at[3, way, step],
                {"prow": sibling},
            )

    def ring_finish():
        own = gathered.at[p]
        sent(own, ring_sems.at[2, 0, full + 1])
        landed(gathered.at[sibling], ring_sems.at[3, 0, full + 1])
        for step in range(full + 1):
            for way, sign in ((0, 1), (1, -1)):
                part = everything if step < full else (lower, upper)[way]
                chunk = row_of(z - sign * (step + 1), 1 - core)
                ref = gathered.at[chunk, part]
                sent(ref, ring_sems.at[0, way, step])
                sent(ref, ring_sems.at[2, way, step])
                landed(ref, ring_sems.at[3, way, step])

    def ring_at(point):
        if point == 0:
            landed(gathered.at[0, pl.ds(0, 32 * (nc - 1))], recvs.at[1])
            ring_send(0)
            own = gathered.at[p]
            push(
                own,
                own,
                ring_sems.at[2, 0, full + 1],
                ring_sems.at[3, 0, full + 1],
                {"prow": sibling},
            )
        elif point <= full + 1:
            ring_landed(point - 1)
            if point <= full:
                ring_send(point)

    def image(vec, turn, first):
        split = pieces(vec)
        stacked[64:160] = split
        out = lax.dot_general(split, stacked[...], NT, preferred_element_type=F32)
        out = sum_rows(out, 32)
        gram = out[:, 64:96] + out[:, 96:128] + out[:, 128:160]
        pair_send[turn] = pack_image(jnp.concatenate([out[:, :64], gram], axis=1))
        push(
            pair_send.at[turn],
            pair_recv.at[turn],
            sends.at[4 + turn],
            recvs.at[4 + turn],
            {"prow": sibling},
        )
        if turn == 0:
            with scope("block_second"):
                block_second()
        with scope("wait_pair"):
            landed(pair_recv.at[turn], recvs.at[4 + turn])
        mine = pair_send[turn] + pair_recv[turn]
        image_send[turn] = mine
        image_recv[turn, pl.ds(z, 1)] = mine[None]

        def body(i, carry):
            push(
                image_send.at[turn],
                image_recv.at[turn, z],
                sends.at[6 + turn],
                recvs.at[6 + turn],
                {"prow": row_of(z + i, core)},
            )
            return carry

        lax.fori_loop(1, nz, body, 0)
        with scope("ring_a"):
            ring_at(first)
        with scope("wait_image"):
            landed(image_recv.at[turn, pl.ds(0, nz - 1)], recvs.at[6 + turn])
        total = image_recv[turn, 0]
        for k in range(1, nz):
            total = total + image_recv[turn, k]
        total = unpack_image(total)
        gram = total[:, 64:96]
        mine = jnp.concatenate([fold(total[:, :32]), fold(total[:, 32:64])], axis=0)
        walk_send[turn] = mine
        walk_recv[turn, pl.ds(q, 1)] = mine[None]
        to_plane(
            lambda peer: push(
                walk_send.at[turn],
                walk_recv.at[turn, q],
                sends.at[8 + turn],
                recvs.at[8 + turn],
                {"pcol": peer},
            )
        )
        with scope("ring_b"):
            ring_at(first + 1)
        with scope("wait_walk"):
            landed(walk_recv.at[turn, far], recvs.at[8 + turn])
        values = []
        for rows in (slice(0, 8), slice(8, 16)):
            values.append(
                jnp.concatenate(
                    [
                        unfold([walk_recv[turn, k + j, rows] for j in range(4)])
                        for k in range(0, nc, 4)
                    ],
                    axis=1,
                )
            )
        return values[0], values[1], gram

    def residual(vec, l_val, e_val, gram, inverse_diag):
        l_split = pieces(l_val)
        both = jnp.concatenate([l_split, pieces(e_val)], axis=0)
        out = sum_rows(
            lax.dot_general(l_split, both, NT, preferred_element_type=F32), 32
        )
        ray_s = out[:, :32] + out[:, 32:64] + out[:, 64:96]
        ray_h = out[:, 96:128] + out[:, 128:160] + out[:, 160:192]
        with scope("eliminate"):
            coeffs = eliminate(
                ray_s * (1.0 / walkers) + STABILIZER * gram, ray_h * (1.0 / walkers), eye
            )
        mixed = lax.dot_general(
            coeffs,
            jnp.concatenate([l_val, vec], axis=1),
            TN,
            precision=HIGHEST,
            preferred_element_type=F32,
        )
        rest = (e_val - mixed[:, :walkers]) * (1.0 / walkers)
        out = jnp.dot(pieces(rest), block[...], preferred_element_type=F32)
        out = sum_rows(out, 32) - STABILIZER * mixed[:, walkers:]
        return out * inverse_diag, coeffs

    def own_part(vec):
        for k in range(nc // 2):
            basis[k] = vec[:, 128 * k : 128 * k + 128]
        chunk = basis[pl.ds(q // 2, 1)][0]
        return jnp.where(q % 2 == 0, chunk[:, :64], chunk[:, 64:])

    with scope("wait_v"):
        landed(v_recv.at[far], recvs.at[0])
    top, bottom = [], []
    for k in range(0, nc, 2):
        a, b = v_recv[k], v_recv[k + 1]
        top += [a[:, :64], b[:, :64]]
        bottom += [a[:, 64:], b[:, 64:]]
    vec = jnp.concatenate(
        [jnp.concatenate(top, axis=1), jnp.concatenate(bottom, axis=1)], axis=0
    )
    l_val, e_val, gram = image(vec, 0, 0)
    with scope("wait_block"):
        block_landed()
    squares = jnp.zeros((8, wide), F32)
    for k in range(0, walkers, 16):
        part = block[k : k + 16].astype(F32)
        part = part * part
        squares = squares + part[:8] + part[8:]
    inverse_diag = 1.0 / (
        jnp.sum(squares, axis=0, keepdims=True) * (1.0 / walkers) + STABILIZER
    )
    vec, _ = residual(vec, l_val, e_val, gram, inverse_diag)

    l_val, e_val, gram = image(vec, 1, 2)
    norms = jnp.sum(jnp.where(eye, gram, 0.0), axis=1, keepdims=True)
    scale = 1.0 / jnp.sqrt(norms * (1.0 / params) + EPSILON)
    scale_row = to_row(scale, eye)
    vec = vec * scale
    one_ref[...] = own_part(vec)
    vec, coeffs = residual(
        vec, l_val * scale, e_val * scale, gram * scale * scale_row, inverse_diag
    )
    ray_ref[...] = coeffs

    norms = to_row(jnp.sum(vec * vec, axis=1, keepdims=True), eye)
    norm_send[...] = jnp.concatenate([norms, jnp.zeros((1, 96), F32)], axis=1)
    norm_recv[pl.ds(p, 1)] = norm_send[...][None]

    def send_norm(i, carry):
        push(
            norm_send,
            norm_recv.at[p],
            sends.at[3],
            recvs.at[3],
            {"prow": lax.rem(p + i, nr)},
        )
        return carry

    lax.fori_loop(1, nr, send_norm, 0)
    with scope("ring_c"):
        for point in range(4, full + 2):
            ring_at(point)
    with scope("own_t"):
        own_t_ref[...] = block[...].T
    with scope("ring_finish"):
        ring_finish()
    with scope("columns"):
        for k in range(nr // 2):
            a, b = gathered[2 * k], gathered[2 * k + 1]
            at = 128 * k
            cols_ref[:, at : at + 128] = jnp.concatenate([a[:, :64], b[:, :64]], axis=1)
            at += 64 * nr
            cols_ref[:, at : at + 128] = jnp.concatenate([a[:, 64:], b[:, 64:]], axis=1)
    with scope("wait_norm"):
        landed(norm_recv.at[pl.ds(0, nr - 1)], recvs.at[3])
    norms = norm_recv[0]
    for k in range(1, nr):
        norms = norms + norm_recv[k]
    norms = to_column(norms[:, :32], eye)
    two_ref[...] = own_part(vec) * (1.0 / jnp.sqrt(norms * (1.0 / params) + EPSILON))

    with scope("finish"):
        pass
    sent(v_recv.at[far], sends.at[0])
    sent(gathered.at[0, pl.ds(0, 32 * (nc - 1))], sends.at[1])
    block_sent()
    sent(norm_recv.at[pl.ds(0, nr - 1)], sends.at[3])
    for turn in range(2):
        sent(pair_send.at[turn], sends.at[4 + turn])
        sent(image_recv.at[turn, pl.ds(0, nz - 1)], sends.at[6 + turn])
        sent(walk_recv.at[turn, far], sends.at[8 + turn])


def tiles(
    walkers,
    own_t,
    cols,
    one,
    two,
    ray,
    corr_ref,
    ham_ref,
    one_out,
    two_out,
    ray_out,
    both,
    sems,
):
    p = lax.axis_index("prow")
    q = lax.axis_index("pcol")
    width = corr_ref.shape[2]
    step = min(256, width)
    one_out[...] = one[...]
    two_out[...] = two[...]
    ray_out[...] = ray[...]
    writes = []
    for k in range(2 * width // step):
      with scope("chunk"):
        which, at = divmod(k * step, width)
        columns = pl.ds(at, step)
        both[which, :, columns] = jnp.dot(
            own_t[...], cols[:, k * step : k * step + step], preferred_element_type=F32
        ) * (1.0 / walkers)
        if which == 0:

            @pl.when(p * 64 // step == at // step)
            def _():
                row = lax.broadcasted_iota(jnp.int32, (64, step), 0)
                column = lax.broadcasted_iota(jnp.int32, (64, step), 1)
                hit = row == column - (p * 64 - at)
                mine = pl.ds(pl.multiple_of(q * 64, 64), 64)
                both[0, mine, columns] += jnp.where(hit, STABILIZER, 0.0)

        out = (corr_ref, ham_ref)[which]
        writes.append(
            pltpu.make_async_copy(
                both.at[which, :, columns], out.at[0, :, columns], sems.at[k]
            )
        )
        writes[-1].start()
    with scope("writes"):
        for write in writes:
            write.wait()


def local(nr, nc, log_derivs, energy_derivs, start_block):
    wide, walkers, narrow = 64 * nc, 32 * nc, 64 * nr
    nz = nr // 2
    vmem = pl.BlockSpec(memory_space=pltpu.VMEM)
    full = nz // 2 - 1
    own_t, cols, one, two, ray = pl.pallas_call(
        functools.partial(davidson, nr, nc),
        out_shape=(
            jax.ShapeDtypeStruct((wide, walkers), BF16),
            jax.ShapeDtypeStruct((walkers, 2 * narrow), BF16),
            jax.ShapeDtypeStruct((32, 64), F32),
            jax.ShapeDtypeStruct((32, 64), F32),
            jax.ShapeDtypeStruct((32, 32), F32),
        ),
        in_specs=[pl.BlockSpec(memory_space=pltpu.HBM)] * 3,
        out_specs=(vmem,) * 5,
        scratch_shapes=[
            pltpu.VMEM((32, wide), BF16),
            pltpu.VMEM((32, wide), BF16),
            pltpu.VMEM((32, 64), F32),
            pltpu.VMEM((walkers, wide), BF16),
            pltpu.VMEM((nc, 32, 128), BF16),
            pltpu.VMEM((nr, walkers, 128), BF16),
            pltpu.VMEM((16, 128), F32),
            pltpu.VMEM((nc, 16, 128), F32),
            pltpu.VMEM((160, wide), BF16),
            pltpu.VMEM((nc // 2, 32, 128), F32),
            pltpu.VMEM((2, 24, 128), F32),
            pltpu.VMEM((2, 24, 128), F32),
            pltpu.VMEM((2, 24, 128), F32),
            pltpu.VMEM((2, nz, 24, 128), F32),
            pltpu.VMEM((2, 16, 128), F32),
            pltpu.VMEM((2, nc, 16, 128), F32),
            pltpu.VMEM((1, 128), F32),
            pltpu.VMEM((nr, 1, 128), F32),
            pltpu.SemaphoreType.DMA((3,)),
            pltpu.SemaphoreType.DMA((13,)),
            pltpu.SemaphoreType.DMA((13,)),
            pltpu.SemaphoreType.DMA((4, 2, full + 2)),
        ],
        compiler_params=pltpu.CompilerParams(
            collective_id=0, has_side_effects=True, vmem_limit_bytes=40 * 1024 * 1024
        ),
        name="davidson",
    )(*(pltpu.with_memory_space_constraint(x, pltpu.HBM) for x in (log_derivs, energy_derivs, start_block.T)))

    hbm = pl.BlockSpec(memory_space=pltpu.HBM)
    corr, ham, one, two, ray = pl.pallas_call(
        functools.partial(tiles, walkers),
        out_shape=(
            jax.ShapeDtypeStruct((1, wide, narrow), F32),
            jax.ShapeDtypeStruct((1, wide, narrow), F32),
            jax.ShapeDtypeStruct((32, 64), F32),
            jax.ShapeDtypeStruct((32, 64), F32),
            jax.ShapeDtypeStruct((32, 32), F32),
        ),
        in_specs=[vmem] * 5,
        out_specs=(hbm, hbm, vmem, vmem, vmem),
        scratch_shapes=[
            pltpu.VMEM((2, wide, narrow), F32),
            pltpu.SemaphoreType.DMA((2 * narrow // min(256, narrow),)),
        ],
        compiler_params=pltpu.CompilerParams(vmem_limit_bytes=24 * 1024 * 1024),
        name="tiles",
    )(own_t, cols, one, two, ray)
    return one.T, two.T, ray, corr, ham


def solution(mesh):
    return jax.shard_map(
        functools.partial(local, mesh.shape["prow"], mesh.shape["pcol"]),
        mesh=mesh,
        in_specs=(P("pcol", "prow"), P("pcol", "prow"), P(("prow", "pcol"), None)),
        out_specs=(
            P(("prow", "pcol"), None),
            P(("prow", "pcol"), None),
            P(),
            P("pcol", "prow", None),
            P("pcol", "prow", None),
        ),
        check_vma=False,
    )
```

```python
import contextlib
import functools

import jax
import jax.numpy as jnp
from jax import lax
from jax.experimental import pallas as pl
from jax.experimental.pallas import tpu as pltpu
from jax.sharding import PartitionSpec as P

STABILIZER = 0.5
EPSILON = 1e-6
F32 = jnp.float32
BF16 = jnp.bfloat16
HIGHEST = lax.Precision.HIGHEST
MESH = pl.DeviceIdType.MESH
NT = (((1,), (1,)), ((), ()))
TN = (((0,), (0,)), ((), ()))


def scope(name):
    return contextlib.nullcontext()


def pieces(x):
    high = x.astype(BF16)
    rest = x - high.astype(F32)
    middle = rest.astype(BF16)
    low = (rest - middle.astype(F32)).astype(BF16)
    return jnp.concatenate([high, middle, low], axis=0)


def sum_rows(x, n):
    return x[:n] + x[n : 2 * n] + x[2 * n : 3 * n]


def to_row(column, eye):
    return jnp.sum(jnp.where(eye, column, 0.0), axis=0, keepdims=True)


def to_column(row, eye):
    return jnp.sum(jnp.where(eye, row, 0.0), axis=1, keepdims=True)


def fold(x):
    return jnp.concatenate([x[8 * g : 8 * g + 8] for g in range(4)], axis=1)


def unfold(folded):
    return jnp.concatenate(
        [
            jnp.concatenate([x[:, 32 * g : 32 * g + 32] for x in folded], axis=1)
            for g in range(4)
        ],
        axis=0,
    )


def inverse_of_two(a, b, d):
    scale = 1.0 / (a * d - b * b)
    return d * scale, -b * scale, a * scale


def eliminate(matrix, right, eye):
    n = matrix.shape[0]
    diagonal = jnp.where(eye, matrix, 0.0)
    unit = lax.rsqrt(jnp.sum(diagonal, axis=1, keepdims=True))
    unit_row = lax.rsqrt(jnp.sum(diagonal, axis=0, keepdims=True))
    both = jnp.concatenate([matrix * unit * unit_row, right * unit], axis=1)
    rows = lax.broadcasted_iota(jnp.int32, both.shape, 0)
    for k in range(0, n, 4):
        c = [jnp.broadcast_to(both[:, k + j : k + j + 1], both.shape) for j in range(4)]
        r = [both[k + i : k + i + 1] for i in range(4)]
        g = [[c[j][k + i : k + i + 1] for j in range(4)] for i in range(4)]
        p0, p1, p2 = inverse_of_two(g[0][0], g[1][0], g[1][1])
        u0, u1 = p0 * r[0] + p1 * r[1], p1 * r[0] + p2 * r[1]
        t02, t12 = p0 * g[2][0] + p1 * g[2][1], p1 * g[2][0] + p2 * g[2][1]
        t03, t13 = p0 * g[3][0] + p1 * g[3][1], p1 * g[3][0] + p2 * g[3][1]
        w0, w1, w2 = inverse_of_two(
            g[2][2] - g[2][0] * t02 - g[2][1] * t12,
            g[3][2] - g[3][0] * t02 - g[3][1] * t12,
            g[3][3] - g[3][0] * t03 - g[3][1] * t13,
        )
        v2 = r[2] - g[2][0] * u0 - g[2][1] * u1
        v3 = r[3] - g[3][0] * u0 - g[3][1] * u1
        x2, x3 = w0 * v2 + w1 * v3, w1 * v2 + w2 * v3
        x = (u0 - t02 * x2 - t03 * x3, u1 - t12 * x2 - t13 * x3, x2, x3)
        both = both - c[0] * x[0] - c[1] * x[1] - c[2] * x[2] - c[3] * x[3]
        for i in range(4):
            both = jnp.where(rows == k + i, x[i], both)
    return both[:, n:] * unit


def davidson(
    nr,
    nc,
    l_hbm,
    e_hbm,
    v_hbm,
    tiles_ref,
    one_ref,
    two_ref,
    ray_ref,
    l_ref,
    e_ref,
    v_ref,
    block,
    own_t,
    slabs,
    gathered,
    v_send,
    v_recv,
    stacked,
    basis,
    pair_send,
    pair_recv,
    image_send,
    image_recv,
    gram_send,
    gram_recv,
    walk_send,
    walk_recv,
    norm_send,
    norm_recv,
    loads,
    sends,
    recvs,
    ring_sems,
):
    p = lax.axis_index("prow")
    q = lax.axis_index("pcol")
    z = p // 2
    core = p % 2
    nz = nr // 2
    wide = 64 * nc
    walkers = 32 * nc
    params = wide * nr

    def row_of(zz, cc):
        return lax.rem(zz + nz, nz) * 2 + cc

    sibling = z * 2 + 1 - core

    def push(src, dst, send_sem, recv_sem, device):
        pltpu.make_async_remote_copy(
            src_ref=src,
            dst_ref=dst,
            send_sem=send_sem,
            recv_sem=recv_sem,
            device_id=device,
            device_id_type=MESH,
        ).start()

    def sent(ref, sem):
        pltpu.make_async_remote_copy(
            src_ref=ref,
            dst_ref=ref,
            send_sem=sem,
            recv_sem=sem,
            device_id={"prow": sibling},
            device_id_type=MESH,
        ).wait_send()

    def landed(ref, sem):
        pltpu.make_async_remote_copy(
            src_ref=ref,
            dst_ref=ref,
            send_sem=sem,
            recv_sem=sem,
            device_id={"prow": sibling},
            device_id_type=MESH,
        ).wait_recv()

    reads = [
        pltpu.make_async_copy(src, dst, loads.at[i])
        for i, (src, dst) in enumerate(((v_hbm, v_ref), (l_hbm, l_ref), (e_hbm, e_ref)))
    ]
    for read in reads:
        read.start()

    barrier = pltpu.get_barrier_semaphore()

    def greet_col(i, carry):
        pl.semaphore_signal(
            barrier, inc=1, device_id={"pcol": lax.rem(q + i, nc)}, device_id_type=MESH
        )
        return carry

    def greet_row(i, carry):
        pl.semaphore_signal(
            barrier, inc=1, device_id={"prow": lax.rem(p + i, nr)}, device_id_type=MESH
        )
        return carry

    lax.fori_loop(1, nc, greet_col, 0)
    lax.fori_loop(1, nr, greet_row, 0)

    def to_plane(copy):
        def body(i, carry):
            copy(lax.rem(q + i, nc))
            return carry

        lax.fori_loop(1, nc, body, 0)

    reads[0].wait()
    v_own = v_ref[...]
    v_send[...] = jnp.concatenate([v_own[:16], v_own[16:]], axis=1)
    v_recv[pl.ds(q, 1)] = v_send[...][None]
    reads[1].wait()
    reads[2].wait()
    l_own = l_ref[...]
    e_own = e_ref[...]
    for j in range(nc):
        slabs[j] = jnp.concatenate(
            [l_own[:, 64 * j : 64 * j + 64], e_own[:, 64 * j : 64 * j + 64]], axis=1
        )
    own_rows = pl.ds(pl.multiple_of(q * 32, 32), 32)
    gathered[pl.ds(p, 1), own_rows, :] = slabs[pl.ds(q, 1)]
    block[own_rows, :] = l_own
    stacked[0:32] = l_own
    stacked[32:64] = e_own
    with scope("loaded"):
        pass
    with scope("barrier"):
        pl.semaphore_wait(barrier, nc - 1 + nr - 1)
    to_plane(
        lambda peer: push(
            v_send, v_recv.at[q], sends.at[0], recvs.at[0], {"pcol": peer}
        )
    )
    nx = 4
    ny = nc // nx
    x, y = q % nx, q // nx

    def along_x(i):
        return y * nx + lax.rem(x + i, nx)

    def along_y(i):
        return lax.rem(y + i, ny) * nx + x

    def half_of(member, part):
        return block.at[pl.ds(pl.multiple_of(member * 32 + 16 * part, 16), 16)]

    def block_first():
        for i in range(1, nx):
            ref = half_of(q, 0)
            push(ref, ref, sends.at[2], recvs.at[2], {"pcol": along_x(i)})
        for i in range(1, ny):
            ref = half_of(q, 1)
            push(ref, ref, sends.at[10], recvs.at[10], {"pcol": along_y(i)})

    def block_second():
        landed(block.at[pl.ds(0, 16 * (nx - 1))], recvs.at[2])
        landed(block.at[pl.ds(0, 16 * (ny - 1))], recvs.at[10])

        def forward_y(i, carry):
            for k in range(nx):
                ref = half_of(along_x(k), 0)
                push(ref, ref, sends.at[11], recvs.at[11], {"pcol": along_y(i)})
            return carry

        def forward_x(i, carry):
            for k in range(ny):
                ref = half_of(along_y(k), 1)
                push(ref, ref, sends.at[12], recvs.at[12], {"pcol": along_x(i)})
            return carry

        lax.fori_loop(1, ny, forward_y, 0)
        lax.fori_loop(1, nx, forward_x, 0)

    counts = (nx - 1, ny - 1, nx * (ny - 1), ny * (nx - 1))

    def block_landed():
        for sem, count in zip((11, 12), counts[2:], strict=True):
            landed(block.at[pl.ds(0, 16 * count)], recvs.at[sem])

    def block_sent():
        for sem, count in zip((2, 10, 11, 12), counts, strict=True):
            sent(block.at[pl.ds(0, 16 * count)], sends.at[sem])

    block_first()
    to_plane(
        lambda peer: push(
            slabs.at[peer],
            gathered.at[p, own_rows],
            sends.at[1],
            recvs.at[1],
            {"pcol": peer},
        )
    )

    eye = lax.broadcasted_iota(jnp.int32, (32, 32), 0) == lax.broadcasted_iota(
        jnp.int32, (32, 32), 1
    )
    far = pl.ds(0, nc - 1)

    full = nz // 2 - 1
    half = walkers // 2
    everything, lower, upper = pl.ds(0, walkers), pl.ds(0, half), pl.ds(half, half)

    def part_of(way, step):
        return everything if step < full else (lower, upper)[way]

    def ring_start():
        landed(gathered.at[0, pl.ds(0, 32 * (nc - 1))], recvs.at[1])
        ring_send(0)
        own = gathered.at[p]
        push(
            own,
            own,
            ring_sems.at[2, 0, full + 1],
            ring_sems.at[3, 0, full + 1],
            {"prow": sibling},
        )

    def ring_send(step):
        for way, sign in ((0, 1), (1, -1)):
            ref = gathered.at[row_of(z - sign * step, core), part_of(way, step)]
            push(
                ref,
                ref,
                ring_sems.at[0, way, step],
                ring_sems.at[1, way, step],
                {"prow": row_of(z + sign, core)},
            )

    def ring_landed(step):
        for way, sign in ((0, 1), (1, -1)):
            ref = gathered.at[row_of(z - sign * (step + 1), core), part_of(way, step)]
            landed(ref, ring_sems.at[1, way, step])
            push(
                ref,
                ref,
                ring_sems.at[2, way, step],
                ring_sems.at[3, way, step],
                {"prow": sibling},
            )

    def sibling_landed(step):
        for way, sign in ((0, 1), (1, -1)):
            chunk = row_of(z - sign * (step + 1), 1 - core)
            landed(gathered.at[chunk, part_of(way, step)], ring_sems.at[3, way, step])

    def ring_sent():
        sent(gathered.at[p], ring_sems.at[2, 0, full + 1])
        for step in range(full + 1):
            for way in range(2):
                ref = gathered.at[p, part_of(way, step)]
                sent(ref, ring_sems.at[0, way, step])
                sent(ref, ring_sems.at[2, way, step])

    def multiply(chunk):
        a = gathered[pl.ds(2 * chunk, 1)][0]
        b = gathered[pl.ds(2 * chunk + 1, 1)][0]
        right = jnp.concatenate(
            [a[:, :64], b[:, :64], a[:, 64:], b[:, 64:]], axis=1
        )
        out = jnp.dot(own_t[...], right, preferred_element_type=F32) * (1.0 / walkers)
        columns = pl.ds(pl.multiple_of(chunk * 128, 128), 128)
        tiles_ref[0, :, columns] = out[:, :128]
        tiles_ref[1, :, columns] = out[:, 128:]

    def multiply_own():
        own_t[...] = block[...].T
        landed(gathered.at[sibling], ring_sems.at[3, 0, full + 1])
        multiply(z)
        row = lax.broadcasted_iota(jnp.int32, (64, 128), 0)
        column = lax.broadcasted_iota(jnp.int32, (64, 128), 1)
        mine = pl.ds(pl.multiple_of(q * 64, 64), 64)
        columns = pl.ds(pl.multiple_of(z * 128, 128), 128)
        tiles_ref[0, mine, columns] += jnp.where(
            column == row + core * 64, STABILIZER, 0.0
        )

    def multiply_step(step):
        sibling_landed(step)

        def body(way, carry):
            multiply(lax.rem(z + (2 * way - 1) * (step + 1) + nz, nz))
            return carry

        lax.fori_loop(0, 2 if step < full else 1, body, 0)

    def image_start(vec, turn):
        split = pieces(vec)
        stacked[64:160] = split
        out = lax.dot_general(split, stacked[...], NT, preferred_element_type=F32)
        out = sum_rows(out, 32)
        gram = out[:, 64:96] + out[:, 96:128] + out[:, 128:160]
        pair_send[turn] = jnp.concatenate(
            [fold(out[:, :32]), fold(out[:, 32:64]), fold(gram)], axis=0
        )
        push(
            pair_send.at[turn],
            pair_recv.at[turn],
            sends.at[4 + turn],
            recvs.at[4 + turn],
            {"prow": sibling},
        )
        if turn == 0:
            with scope("block_second"):
                block_second()
        with scope("wait_pair"):
            landed(pair_recv.at[turn], recvs.at[4 + turn])
        mine = pair_send[turn] + pair_recv[turn]
        image_send[turn] = mine[:16]
        gram_send[turn] = mine[16:]
        image_recv[turn, pl.ds(z, 1)] = mine[None, :16]
        gram_recv[turn, pl.ds(z, 1)] = mine[None, 16:]
        for src, dst, sem in (
            (image_send, image_recv, 6 + turn),
            (gram_send, gram_recv, 13 + turn),
        ):

            def body(i, carry):
                push(
                    src.at[turn],
                    dst.at[turn, z],
                    sends.at[sem],
                    recvs.at[sem],
                    {"prow": row_of(z + i, core)},
                )
                return carry

            lax.fori_loop(1, nz, body, 0)

    def walk_start(turn):
        with scope("wait_image"):
            landed(image_recv.at[turn, pl.ds(0, nz - 1)], recvs.at[6 + turn])
        mine = jnp.sum(image_recv[turn], axis=0)
        walk_send[turn] = mine
        walk_recv[turn, pl.ds(q, 1)] = mine[None]
        to_plane(
            lambda peer: push(
                walk_send.at[turn],
                walk_recv.at[turn, q],
                sends.at[8 + turn],
                recvs.at[8 + turn],
                {"pcol": peer},
            )
        )

    def gram_landed(turn):
        landed(gram_recv.at[turn, pl.ds(0, nz - 1)], recvs.at[13 + turn])
        return unfold([jnp.sum(gram_recv[turn], axis=0)])

    def walk_landed(turn):
        with scope("wait_walk"):
            landed(walk_recv.at[turn, far], recvs.at[8 + turn])
        return [
            jnp.concatenate(
                [
                    unfold([walk_recv[turn, k + j, rows] for j in range(4)])
                    for k in range(0, nc, 4)
                ],
                axis=1,
            )
            for rows in (slice(0, 8), slice(8, 16))
        ]

    def residual(vec, l_val, e_val, gram, inverse_diag):
        l_split = pieces(l_val)
        both = jnp.concatenate([l_split, pieces(e_val)], axis=0)
        out = sum_rows(
            lax.dot_general(l_split, both, NT, preferred_element_type=F32), 32
        )
        ray_s = out[:, :32] + out[:, 32:64] + out[:, 64:96]
        ray_h = out[:, 96:128] + out[:, 128:160] + out[:, 160:192]
        image = jnp.dot(both, block[...], preferred_element_type=F32)
        image_s = sum_rows(image[:96], 32) * (1.0 / walkers) + STABILIZER * vec
        image_h = sum_rows(image[96:], 32) * (1.0 / walkers) * inverse_diag
        s = pieces(image_s * inverse_diag)
        right = jnp.concatenate(
            [s[:32], s[32:64], s[:32], s[64:], s[32:64], s[:32]], axis=0
        )
        with scope("eliminate"):
            coeffs = eliminate(
                ray_s * (1.0 / walkers) + STABILIZER * gram,
                ray_h * (1.0 / walkers),
                eye,
            )
        c = pieces(coeffs)
        left = jnp.concatenate([c[:32], c[:32], c[32:64], c[:32], c[32:64], c[64:]], axis=0)
        out = lax.dot_general(left, right, TN, preferred_element_type=F32)
        return image_h - out, coeffs

    def own_part(vec):
        for k in range(nc // 2):
            basis[k] = vec[:, 128 * k : 128 * k + 128]
        chunk = basis[pl.ds(q // 2, 1)][0]
        return jnp.where(q % 2 == 0, chunk[:, :64], chunk[:, 64:])

    with scope("wait_v"):
        landed(v_recv.at[far], recvs.at[0])
    top, bottom = [], []
    for k in range(0, nc, 2):
        a, b = v_recv[k], v_recv[k + 1]
        top += [a[:, :64], b[:, :64]]
        bottom += [a[:, 64:], b[:, 64:]]
    vec = jnp.concatenate(
        [jnp.concatenate(top, axis=1), jnp.concatenate(bottom, axis=1)], axis=0
    )
    image_start(vec, 0)
    walk_start(0)
    with scope("ring_start"):
        ring_start()
    with scope("wait_block"):
        block_landed()
    squares = jnp.zeros((8, wide), F32)
    for k in range(0, walkers, 16):
        part = block[k : k + 16].astype(F32)
        part = part * part
        squares = squares + part[:8] + part[8:]
    inverse_diag = 1.0 / (
        jnp.sum(squares, axis=0, keepdims=True) * (1.0 / walkers) + STABILIZER
    )
    gram = gram_landed(0)
    l_val, e_val = walk_landed(0)
    with scope("ring_0"):
        if full >= 1:
            ring_landed(0)
            ring_send(1)
    vec, _ = residual(vec, l_val, e_val, gram, inverse_diag)

    image_start(vec, 1)
    with scope("tiles_a"):
        multiply_own()
        if full >= 1:
            multiply_step(0)
    with scope("ring_1"):
        if full >= 2:
            ring_landed(1)
    walk_start(1)
    with scope("tiles_b"):
        if full >= 2:
            ring_send(2)
            multiply_step(1)
    gram = gram_landed(1)
    norms = jnp.sum(jnp.where(eye, gram, 0.0), axis=1, keepdims=True)
    scale = 1.0 / jnp.sqrt(norms * (1.0 / params) + EPSILON)
    gram = gram * scale * to_row(scale, eye)
    vec = vec * scale
    one_ref[...] = own_part(vec)
    l_val, e_val = walk_landed(1)
    with scope("ring_2"):
        if full >= 3:
            ring_landed(2)
            ring_send(3)
    vec, coeffs = residual(vec, l_val * scale, e_val * scale, gram, inverse_diag)
    norms = to_row(jnp.sum(vec * vec, axis=1, keepdims=True), eye)
    norm_send[...] = jnp.concatenate([norms, jnp.zeros((1, 96), F32)], axis=1)
    norm_recv[pl.ds(p, 1)] = norm_send[...][None]

    def send_norm(i, carry):
        push(
            norm_send,
            norm_recv.at[p],
            sends.at[3],
            recvs.at[3],
            {"prow": lax.rem(p + i, nr)},
        )
        return carry

    lax.fori_loop(1, nr, send_norm, 0)
    ray_ref[...] = coeffs
    two = own_part(vec)
    with scope("tiles_c"):
        if full >= 3:
            multiply_step(2)
    with scope("ring_3"):
        ring_landed(full)
    with scope("tiles_d"):
        multiply_step(full)
    ring_sent()
    sent(v_recv.at[far], sends.at[0])
    sent(gathered.at[0, pl.ds(0, 32 * (nc - 1))], sends.at[1])
    block_sent()
    for turn in range(2):
        sent(pair_send.at[turn], sends.at[4 + turn])
        sent(image_recv.at[turn, pl.ds(0, nz - 1)], sends.at[6 + turn])
        sent(gram_recv.at[turn, pl.ds(0, nz - 1)], sends.at[13 + turn])
        sent(walk_recv.at[turn, far], sends.at[8 + turn])
    with scope("wait_norm"):
        landed(norm_recv.at[pl.ds(0, nr - 1)], recvs.at[3])
    norms = to_column(jnp.sum(norm_recv[...], axis=0)[:, :32], eye)
    two_ref[...] = two * (1.0 / jnp.sqrt(norms * (1.0 / params) + EPSILON))
    sent(norm_recv.at[pl.ds(0, nr - 1)], sends.at[3])
    with scope("end"):
        pass


def write(tiles, one, two, ray, corr_ref, ham_ref, one_ref, two_ref, ray_ref, sems):
    pairs = (
        (tiles.at[0], corr_ref.at[0]),
        (tiles.at[1], ham_ref.at[0]),
        (one, one_ref),
        (two, two_ref),
        (ray, ray_ref),
    )
    writes = [
        pltpu.make_async_copy(src, dst, sems.at[i])
        for i, (src, dst) in enumerate(pairs)
    ]
    for copy in writes:
        copy.start()
    for copy in writes:
        copy.wait()


def local(nr, nc, log_derivs, energy_derivs, start_block):
    wide, walkers, narrow = 64 * nc, 32 * nc, 64 * nr
    nz = nr // 2
    vmem = pl.BlockSpec(memory_space=pltpu.VMEM)
    full = nz // 2 - 1
    hbm = pl.BlockSpec(memory_space=pltpu.HBM)
    small = (
        jax.ShapeDtypeStruct((32, 64), F32),
        jax.ShapeDtypeStruct((32, 64), F32),
        jax.ShapeDtypeStruct((32, 32), F32),
    )
    arguments = (log_derivs, energy_derivs, start_block.T)
    results = pl.pallas_call(
        functools.partial(davidson, nr, nc),
        out_shape=(
            pltpu.VMEM((2, wide, narrow), F32),
            *(pltpu.VMEM(x.shape, F32) for x in small),
        ),
        in_specs=[hbm] * 3,
        out_specs=(vmem,) * 4,
        scratch_shapes=[
            pltpu.VMEM((32, wide), BF16),
            pltpu.VMEM((32, wide), BF16),
            pltpu.VMEM((32, 64), F32),
            pltpu.VMEM((walkers, wide), BF16),
            pltpu.VMEM((wide, walkers), BF16),
            pltpu.VMEM((nc, 32, 128), BF16),
            pltpu.VMEM((nr, walkers, 128), BF16),
            pltpu.VMEM((16, 128), F32),
            pltpu.VMEM((nc, 16, 128), F32),
            pltpu.VMEM((160, wide), BF16),
            pltpu.VMEM((nc // 2, 32, 128), F32),
            pltpu.VMEM((2, 24, 128), F32),
            pltpu.VMEM((2, 24, 128), F32),
            pltpu.VMEM((2, 16, 128), F32),
            pltpu.VMEM((2, nz, 16, 128), F32),
            pltpu.VMEM((2, 8, 128), F32),
            pltpu.VMEM((2, nz, 8, 128), F32),
            pltpu.VMEM((2, 16, 128), F32),
            pltpu.VMEM((2, nc, 16, 128), F32),
            pltpu.VMEM((1, 128), F32),
            pltpu.VMEM((nr, 1, 128), F32),
            pltpu.SemaphoreType.DMA((3,)),
            pltpu.SemaphoreType.DMA((15,)),
            pltpu.SemaphoreType.DMA((15,)),
            pltpu.SemaphoreType.DMA((4, 2, full + 2)),
        ],
        compiler_params=pltpu.CompilerParams(
            collective_id=0, has_side_effects=True, vmem_limit_bytes=24 * 1024 * 1024
        ),
        name="davidson",
    )(*(pltpu.with_memory_space_constraint(x, pltpu.HBM) for x in arguments))

    corr, ham, one, two, ray = pl.pallas_call(
        write,
        out_shape=(
            jax.ShapeDtypeStruct((1, wide, narrow), F32),
            jax.ShapeDtypeStruct((1, wide, narrow), F32),
            *small,
        ),
        in_specs=[vmem] * 4,
        out_specs=(hbm,) * 5,
        scratch_shapes=[pltpu.SemaphoreType.DMA((5,))],
        compiler_params=pltpu.CompilerParams(vmem_limit_bytes=24 * 1024 * 1024),
        name="tiles",
    )(*(pltpu.with_memory_space_constraint(x, pltpu.VMEM) for x in results))
    return one.T, two.T, ray, corr, ham


def solution(mesh):
    return jax.shard_map(
        functools.partial(local, mesh.shape["prow"], mesh.shape["pcol"]),
        mesh=mesh,
        in_specs=(P("pcol", "prow"), P("pcol", "prow"), P(("prow", "pcol"), None)),
        out_specs=(
            P(("prow", "pcol"), None),
            P(("prow", "pcol"), None),
            P(),
            P("pcol", "prow", None),
            P("pcol", "prow", None),
        ),
        check_vma=False,
    )
```

```python
import contextlib
import functools

import jax
import jax.numpy as jnp
from jax import lax
from jax.experimental import pallas as pl
from jax.experimental.pallas import tpu as pltpu
from jax.sharding import PartitionSpec as P

STABILIZER = 0.5
EPSILON = 1e-6
F32 = jnp.float32
BF16 = jnp.bfloat16
HIGHEST = lax.Precision.HIGHEST
MESH = pl.DeviceIdType.MESH
NT = (((1,), (1,)), ((), ()))
TN = (((0,), (0,)), ((), ()))


def scope(name):
    return contextlib.nullcontext()


def pieces(x):
    high = x.astype(BF16)
    rest = x - high.astype(F32)
    middle = rest.astype(BF16)
    low = (rest - middle.astype(F32)).astype(BF16)
    return jnp.concatenate([high, middle, low], axis=0)


def sum_rows(x, n):
    return x[:n] + x[n : 2 * n] + x[2 * n : 3 * n]


def to_row(column, eye):
    return jnp.sum(jnp.where(eye, column, 0.0), axis=0, keepdims=True)


def to_column(row, eye):
    return jnp.sum(jnp.where(eye, row, 0.0), axis=1, keepdims=True)


def fold(x):
    return jnp.concatenate([x[8 * g : 8 * g + 8] for g in range(4)], axis=1)


def unfold(folded):
    return jnp.concatenate(
        [
            jnp.concatenate([x[:, 32 * g : 32 * g + 32] for x in folded], axis=1)
            for g in range(4)
        ],
        axis=0,
    )


def inverse_of_two(a, b, d):
    scale = 1.0 / (a * d - b * b)
    return d * scale, -b * scale, a * scale


def eliminate(matrix, right, eye):
    n = matrix.shape[0]
    diagonal = jnp.where(eye, matrix, 0.0)
    unit = lax.rsqrt(jnp.sum(diagonal, axis=1, keepdims=True))
    unit_row = lax.rsqrt(jnp.sum(diagonal, axis=0, keepdims=True))
    both = jnp.concatenate([matrix * unit * unit_row, right * unit], axis=1)
    rows = lax.broadcasted_iota(jnp.int32, both.shape, 0)
    for k in range(0, n, 4):
        c = [jnp.broadcast_to(both[:, k + j : k + j + 1], both.shape) for j in range(4)]
        r = [both[k + i : k + i + 1] for i in range(4)]
        g = [[c[j][k + i : k + i + 1] for j in range(4)] for i in range(4)]
        p0, p1, p2 = inverse_of_two(g[0][0], g[1][0], g[1][1])
        u0, u1 = p0 * r[0] + p1 * r[1], p1 * r[0] + p2 * r[1]
        t02, t12 = p0 * g[2][0] + p1 * g[2][1], p1 * g[2][0] + p2 * g[2][1]
        t03, t13 = p0 * g[3][0] + p1 * g[3][1], p1 * g[3][0] + p2 * g[3][1]
        w0, w1, w2 = inverse_of_two(
            g[2][2] - g[2][0] * t02 - g[2][1] * t12,
            g[3][2] - g[3][0] * t02 - g[3][1] * t12,
            g[3][3] - g[3][0] * t03 - g[3][1] * t13,
        )
        v2 = r[2] - g[2][0] * u0 - g[2][1] * u1
        v3 = r[3] - g[3][0] * u0 - g[3][1] * u1
        x2, x3 = w0 * v2 + w1 * v3, w1 * v2 + w2 * v3
        x = (u0 - t02 * x2 - t03 * x3, u1 - t12 * x2 - t13 * x3, x2, x3)
        pivots = (rows >= k) & (rows < k + 4)
        c = [
            jnp.where(rows == k + j, -1.0, jnp.where(pivots, 0.0, c[j]))
            for j in range(4)
        ]
        both = jnp.where(pivots, 0.0, both)
        both = (both - c[0] * x[0] - c[1] * x[1]) - (c[2] * x[2] + c[3] * x[3])
    return both[:, n:] * unit


def farthest_first(m, n):
    steps = [(i, j) for i in range(m) for j in range(n) if i or j]
    return sorted(steps, key=lambda s: -min(s[0], m - s[0]) - min(s[1], n - s[1]))


def davidson(
    nr,
    nc,
    l_hbm,
    e_hbm,
    v_hbm,
    tiles_ref,
    one_ref,
    two_ref,
    ray_ref,
    l_ref,
    e_ref,
    v_ref,
    block,
    own_t,
    slabs,
    gathered,
    v_send,
    v_recv,
    weights,
    split_all,
    basis,
    pair_send,
    pair_recv,
    image_send,
    image_recv,
    gram_pair_send,
    gram_pair_recv,
    gram_send,
    gram_recv,
    walk_send,
    walk_recv,
    norm_send,
    norm_recv,
    loads,
    sends,
    recvs,
    ring_sems,
):
    p = lax.axis_index("prow")
    q = lax.axis_index("pcol")
    z = p // 2
    core = p % 2
    nz = nr // 2
    wide = 64 * nc
    walkers = 32 * nc
    params = wide * nr

    def row_of(zz, cc):
        return lax.rem(zz + nz, nz) * 2 + cc

    sibling = z * 2 + 1 - core

    def push(src, dst, send_sem, recv_sem, device):
        pltpu.make_async_remote_copy(
            src_ref=src,
            dst_ref=dst,
            send_sem=send_sem,
            recv_sem=recv_sem,
            device_id=device,
            device_id_type=MESH,
        ).start()

    def sent(ref, sem):
        pltpu.make_async_remote_copy(
            src_ref=ref,
            dst_ref=ref,
            send_sem=sem,
            recv_sem=sem,
            device_id={"prow": sibling},
            device_id_type=MESH,
        ).wait_send()

    def landed(ref, sem):
        pltpu.make_async_remote_copy(
            src_ref=ref,
            dst_ref=ref,
            send_sem=sem,
            recv_sem=sem,
            device_id={"prow": sibling},
            device_id_type=MESH,
        ).wait_recv()

    reads = [
        pltpu.make_async_copy(src, dst, loads.at[i])
        for i, (src, dst) in enumerate(((v_hbm, v_ref), (l_hbm, l_ref), (e_hbm, e_ref)))
    ]
    for read in reads:
        read.start()

    barrier = pltpu.get_barrier_semaphore()

    nx = 4
    ny = nc // nx
    x, y = q % nx, q // nx

    def along_x(i):
        return y * nx + lax.rem(x + i, nx)

    def along_y(i):
        return lax.rem(y + i, ny) * nx + x

    plane = [
        lax.rem(y + j, ny) * nx + lax.rem(x + i, nx)
        for i, j in farthest_first(nx, ny)
    ]
    chips = [row_of(z + i, core) for i, _ in farthest_first(nz, 1)]
    rows = [
        row_of(z + i, lax.rem(core + j, 2)) for i, j in farthest_first(nz, 2)
    ]
    for axis, members in (("pcol", plane), ("prow", rows)):
        for member in members:
            pl.semaphore_signal(
                barrier, inc=1, device_id={axis: member}, device_id_type=MESH
            )

    def to_plane(copy):
        for peer in plane:
            copy(peer)

    reads[0].wait()
    v_own = v_ref[...]
    v_send[...] = jnp.concatenate([v_own[:16], v_own[16:]], axis=1)
    v_recv[pl.ds(q, 1)] = v_send[...][None]
    reads[1].wait()
    reads[2].wait()
    l_own = l_ref[...]
    e_own = e_ref[...]
    for j in range(nc):
        slabs[j] = jnp.concatenate(
            [l_own[:, 64 * j : 64 * j + 64], e_own[:, 64 * j : 64 * j + 64]], axis=1
        )
    own_rows = pl.ds(pl.multiple_of(q * 32, 32), 32)
    gathered[pl.ds(p, 1), own_rows, :] = slabs[pl.ds(q, 1)]
    block[own_rows, :] = l_own
    weights[...] = jnp.concatenate([l_own, e_own], axis=0).T
    with scope("barrier"):
        pl.semaphore_wait(barrier, nc - 1 + nr - 1)
    to_plane(
        lambda peer: push(
            v_send, v_recv.at[q], sends.at[0], recvs.at[0], {"pcol": peer}
        )
    )
    def half_of(member, part):
        return block.at[pl.ds(pl.multiple_of(member * 32 + 16 * part, 16), 16)]

    def block_first():
        for i in range(1, nx):
            ref = half_of(q, 0)
            push(ref, ref, sends.at[2], recvs.at[2], {"pcol": along_x(i)})
        for i in range(1, ny):
            ref = half_of(q, 1)
            push(ref, ref, sends.at[10], recvs.at[10], {"pcol": along_y(i)})

    def block_second():
        landed(block.at[pl.ds(0, 16 * (nx - 1))], recvs.at[2])
        landed(block.at[pl.ds(0, 16 * (ny - 1))], recvs.at[10])

        def forward_y(i, carry):
            for k in range(nx):
                ref = half_of(along_x(k), 0)
                push(ref, ref, sends.at[11], recvs.at[11], {"pcol": along_y(i)})
            return carry

        def forward_x(i, carry):
            for k in range(ny):
                ref = half_of(along_y(k), 1)
                push(ref, ref, sends.at[12], recvs.at[12], {"pcol": along_x(i)})
            return carry

        lax.fori_loop(1, ny, forward_y, 0)
        lax.fori_loop(1, nx, forward_x, 0)

    counts = (nx - 1, ny - 1, nx * (ny - 1), ny * (nx - 1))

    def block_landed():
        for sem, count in zip((11, 12), counts[2:], strict=True):
            landed(block.at[pl.ds(0, 16 * count)], recvs.at[sem])

    def block_sent():
        for sem, count in zip((2, 10, 11, 12), counts, strict=True):
            sent(block.at[pl.ds(0, 16 * count)], sends.at[sem])

    block_first()
    to_plane(
        lambda peer: push(
            slabs.at[peer],
            gathered.at[p, own_rows],
            sends.at[1],
            recvs.at[1],
            {"pcol": peer},
        )
    )

    eye = lax.broadcasted_iota(jnp.int32, (32, 32), 0) == lax.broadcasted_iota(
        jnp.int32, (32, 32), 1
    )
    far = pl.ds(0, nc - 1)

    full = nz // 2 - 1
    half = walkers // 2
    everything, lower, upper = pl.ds(0, walkers), pl.ds(0, half), pl.ds(half, half)

    def part_of(way, step):
        return everything if step < full else (lower, upper)[way]

    def ring_start():
        landed(gathered.at[0, pl.ds(0, 32 * (nc - 1))], recvs.at[1])
        ring_send(0)
        own = gathered.at[p]
        push(
            own,
            own,
            ring_sems.at[2, 0, full + 1],
            ring_sems.at[3, 0, full + 1],
            {"prow": sibling},
        )

    def ring_send(step):
        for way, sign in ((0, 1), (1, -1)):
            ref = gathered.at[row_of(z - sign * step, core), part_of(way, step)]
            push(
                ref,
                ref,
                ring_sems.at[0, way, step],
                ring_sems.at[1, way, step],
                {"prow": row_of(z + sign, core)},
            )

    def ring_landed(step):
        for way, sign in ((0, 1), (1, -1)):
            ref = gathered.at[row_of(z - sign * (step + 1), core), part_of(way, step)]
            landed(ref, ring_sems.at[1, way, step])
            push(
                ref,
                ref,
                ring_sems.at[2, way, step],
                ring_sems.at[3, way, step],
                {"prow": sibling},
            )

    def ring_advance(step):
        if step <= full:
            ring_landed(step)
        if step < full:
            ring_send(step + 1)

    def sibling_landed(step):
        for way, sign in ((0, 1), (1, -1)):
            chunk = row_of(z - sign * (step + 1), 1 - core)
            landed(gathered.at[chunk, part_of(way, step)], ring_sems.at[3, way, step])

    def ring_sent():
        sent(gathered.at[p], ring_sems.at[2, 0, full + 1])
        for step in range(full + 1):
            for way in range(2):
                ref = gathered.at[p, part_of(way, step)]
                sent(ref, ring_sems.at[0, way, step])
                sent(ref, ring_sems.at[2, way, step])

    def multiply(chunk):
        a = gathered[pl.ds(2 * chunk, 1)][0]
        b = gathered[pl.ds(2 * chunk + 1, 1)][0]
        right = jnp.concatenate(
            [a[:, :64], b[:, :64], a[:, 64:], b[:, 64:]], axis=1
        )
        out = jnp.dot(own_t[...], right, preferred_element_type=F32) * (1.0 / walkers)
        columns = pl.ds(pl.multiple_of(chunk * 128, 128), 128)
        tiles_ref[0, :, columns] = out[:, :128]
        tiles_ref[1, :, columns] = out[:, 128:]

    def multiply_own():
        own_t[...] = block[...].T
        landed(gathered.at[sibling], ring_sems.at[3, 0, full + 1])
        multiply(z)
        row = lax.broadcasted_iota(jnp.int32, (64, 128), 0)
        column = lax.broadcasted_iota(jnp.int32, (64, 128), 1)
        mine = pl.ds(pl.multiple_of(q * 64, 64), 64)
        columns = pl.ds(pl.multiple_of(z * 128, 128), 128)
        tiles_ref[0, mine, columns] += jnp.where(
            column == row + core * 64, STABILIZER, 0.0
        )

    def multiply_step(step):
        if step > full:
            return
        sibling_landed(step)

        def body(way, carry):
            multiply(lax.rem(z + (2 * way - 1) * (step + 1) + nz, nz))
            return carry

        lax.fori_loop(0, 2 if step < full else 1, body, 0)

    def both_cores(src, dst, turn, sem):
        push(
            src.at[turn],
            dst.at[turn],
            sends.at[sem + turn],
            recvs.at[sem + turn],
            {"prow": sibling},
        )

    def along_z(src, dst, turn, sem):
        for chip in chips:
            push(
                src.at[turn],
                dst.at[turn, z],
                sends.at[sem + turn],
                recvs.at[sem + turn],
                {"prow": chip},
            )

    def image_start(vec, turn):
        with scope("values"):
            split = pieces(vec)
            out = sum_rows(jnp.dot(split, weights[...], preferred_element_type=F32), 32)
            pair_send[turn] = jnp.concatenate(
                [fold(out[:, :32]), fold(out[:, 32:])], axis=0
            )
        both_cores(pair_send, pair_recv, turn, 4)
        if turn == 0:
            with scope("block_second"):
                block_second()
        else:
            sent(v_recv.at[far], sends.at[0])
        with scope("gram"):
            split_all[...] = split
            out = lax.dot_general(
                split, split_all[...], NT, preferred_element_type=F32
            )
            out = sum_rows(out, 32)
            gram_pair_send[turn] = fold(out[:, :32] + out[:, 32:64] + out[:, 64:])
        both_cores(gram_pair_send, gram_pair_recv, turn, 15)
        with scope("wait_pair"):
            landed(pair_recv.at[turn], recvs.at[4 + turn])
        with scope("pair_sum"):
            mine = pair_send[turn] + pair_recv[turn]
            image_send[turn] = mine
            image_recv[turn, pl.ds(z, 1)] = mine[None]
        along_z(image_send, image_recv, turn, 6)
        landed(gram_pair_recv.at[turn], recvs.at[15 + turn])
        mine = gram_pair_send[turn] + gram_pair_recv[turn]
        gram_send[turn] = mine
        gram_recv[turn, pl.ds(z, 1)] = mine[None]
        along_z(gram_send, gram_recv, turn, 13)

    def walk_start(turn):
        with scope("wait_image"):
            landed(image_recv.at[turn, pl.ds(0, nz - 1)], recvs.at[6 + turn])
        with scope("image_sum"):
            mine = jnp.sum(image_recv[turn], axis=0)
            walk_send[turn] = mine
        walk_recv[turn, pl.ds(q, 1)] = mine[None]
        to_plane(
            lambda peer: push(
                walk_send.at[turn],
                walk_recv.at[turn, q],
                sends.at[8 + turn],
                recvs.at[8 + turn],
                {"pcol": peer},
            )
        )

    def gram_landed(turn):
        landed(gram_recv.at[turn, pl.ds(0, nz - 1)], recvs.at[13 + turn])
        return unfold([jnp.sum(gram_recv[turn], axis=0)])

    def walk_landed(turn):
        with scope("wait_walk"):
            landed(walk_recv.at[turn, far], recvs.at[8 + turn])
        return [
            jnp.concatenate(
                [
                    unfold([walk_recv[turn, k + j, rows] for j in range(4)])
                    for k in range(0, nc, 4)
                ],
                axis=1,
            )
            for rows in (slice(0, 8), slice(8, 16))
        ]

    def residual(vec, l_val, e_val, gram, inverse_diag):
        with scope("products"):
            l_split = pieces(l_val)
            both = jnp.concatenate([l_split, pieces(e_val)], axis=0)
            out = sum_rows(
                lax.dot_general(l_split, both, NT, preferred_element_type=F32), 32
            )
        ray_s = out[:, :32] + out[:, 32:64] + out[:, 64:96]
        ray_h = out[:, 96:128] + out[:, 128:160] + out[:, 160:192]
        with scope("images"):
            image = jnp.dot(both, block[...], preferred_element_type=F32)
            image_s = sum_rows(image[:96], 32) * (1.0 / walkers) + STABILIZER * vec
            image_h = sum_rows(image[96:], 32) * (1.0 / walkers) * inverse_diag
            s = pieces(image_s * inverse_diag)
            right = jnp.concatenate(
                [s[:32], s[32:64], s[:32], s[64:], s[32:64], s[:32]], axis=0
            )
        with scope("eliminate"):
            coeffs = eliminate(
                ray_s * (1.0 / walkers) + STABILIZER * gram,
                ray_h * (1.0 / walkers),
                eye,
            )
        with scope("mix"):
            c = pieces(coeffs)
            left = jnp.concatenate(
                [c[:32], c[:32], c[32:64], c[:32], c[32:64], c[64:]], axis=0
            )
            out = lax.dot_general(left, right, TN, preferred_element_type=F32)
            result = image_h - out
        return result, coeffs

    def own_part(vec):
        for k in range(nc // 2):
            basis[k] = vec[:, 128 * k : 128 * k + 128]
        chunk = basis[pl.ds(q // 2, 1)][0]
        return jnp.where(q % 2 == 0, chunk[:, :64], chunk[:, 64:])

    with scope("wait_v"):
        landed(v_recv.at[far], recvs.at[0])
    top, bottom = [], []
    for k in range(0, nc, 2):
        a, b = v_recv[k], v_recv[k + 1]
        top += [a[:, :64], b[:, :64]]
        bottom += [a[:, 64:], b[:, 64:]]
    vec = jnp.concatenate(
        [jnp.concatenate(top, axis=1), jnp.concatenate(bottom, axis=1)], axis=0
    )
    image_start(vec, 0)
    with scope("ring_start"):
        ring_start()
    walk_start(0)
    with scope("wait_block"):
        block_landed()
    squares = jnp.zeros((8, wide), F32)
    for k in range(0, walkers, 16):
        part = block[k : k + 16].astype(F32)
        part = part * part
        squares = squares + part[:8] + part[8:]
    inverse_diag = 1.0 / (
        jnp.sum(squares, axis=0, keepdims=True) * (1.0 / walkers) + STABILIZER
    )
    gram = gram_landed(0)
    with scope("ring_0"):
        ring_advance(0)
    l_val, e_val = walk_landed(0)
    vec, _ = residual(vec, l_val, e_val, gram, inverse_diag)

    image_start(vec, 1)
    with scope("ring_1"):
        ring_advance(1)
    with scope("tiles_a"):
        multiply_own()
        multiply_step(0)
    walk_start(1)
    with scope("tiles_b"):
        multiply_step(1)
    with scope("ring_2"):
        ring_advance(2)
    gram = gram_landed(1)
    norms = jnp.sum(jnp.where(eye, gram, 0.0), axis=1, keepdims=True)
    scale = 1.0 / jnp.sqrt(norms * (1.0 / params) + EPSILON)
    gram = gram * scale * to_row(scale, eye)
    vec = vec * scale
    one_ref[...] = own_part(vec)
    l_val, e_val = walk_landed(1)
    vec, coeffs = residual(vec, l_val * scale, e_val * scale, gram, inverse_diag)
    norms = to_row(jnp.sum(vec * vec, axis=1, keepdims=True), eye)
    norm_send[...] = jnp.concatenate([norms, jnp.zeros((1, 96), F32)], axis=1)
    norm_recv[pl.ds(p, 1)] = norm_send[...][None]

    for row in rows:
        push(norm_send, norm_recv.at[p], sends.at[3], recvs.at[3], {"prow": row})
    block_sent()
    ray_ref[...] = coeffs
    two = own_part(vec)
    with scope("tiles_c"):
        multiply_step(2)
    with scope("ring_3"):
        ring_advance(3)
    with scope("tiles_d"):
        multiply_step(3)
    ring_sent()
    sent(gathered.at[0, pl.ds(0, 32 * (nc - 1))], sends.at[1])
    for turn in range(2):
        sent(pair_send.at[turn], sends.at[4 + turn])
        sent(gram_pair_send.at[turn], sends.at[15 + turn])
        sent(image_recv.at[turn, pl.ds(0, nz - 1)], sends.at[6 + turn])
        sent(gram_recv.at[turn, pl.ds(0, nz - 1)], sends.at[13 + turn])
        sent(walk_recv.at[turn, far], sends.at[8 + turn])
    with scope("wait_norm"):
        landed(norm_recv.at[pl.ds(0, nr - 1)], recvs.at[3])
    norms = to_column(jnp.sum(norm_recv[...], axis=0)[:, :32], eye)
    two_ref[...] = two * (1.0 / jnp.sqrt(norms * (1.0 / params) + EPSILON))
    sent(norm_recv.at[pl.ds(0, nr - 1)], sends.at[3])


def write(tiles, one, two, ray, corr_ref, ham_ref, one_ref, two_ref, ray_ref, sems):
    rows = tiles.shape[1] // 4
    pairs = []
    for k in range(4):
        part = pl.ds(k * rows, rows)
        pairs.append((tiles.at[0, part], corr_ref.at[0, part]))
        pairs.append((tiles.at[1, part], ham_ref.at[0, part]))
    pairs += [(one, one_ref), (two, two_ref), (ray, ray_ref)]
    writes = [
        pltpu.make_async_copy(src, dst, sems.at[i])
        for i, (src, dst) in enumerate(pairs)
    ]
    for copy in writes:
        copy.start()
    for copy in writes:
        copy.wait()


def local(nr, nc, log_derivs, energy_derivs, start_block):
    wide, walkers, narrow = 64 * nc, 32 * nc, 64 * nr
    nz = nr // 2
    vmem = pl.BlockSpec(memory_space=pltpu.VMEM)
    full = nz // 2 - 1
    hbm = pl.BlockSpec(memory_space=pltpu.HBM)
    small = (
        jax.ShapeDtypeStruct((32, 64), F32),
        jax.ShapeDtypeStruct((32, 64), F32),
        jax.ShapeDtypeStruct((32, 32), F32),
    )
    arguments = (log_derivs, energy_derivs, start_block.T)
    results = pl.pallas_call(
        functools.partial(davidson, nr, nc),
        out_shape=(
            pltpu.VMEM((2, wide, narrow), F32),
            *(pltpu.VMEM(x.shape, F32) for x in small),
        ),
        in_specs=[hbm] * 3,
        out_specs=(vmem,) * 4,
        scratch_shapes=[
            pltpu.VMEM((32, wide), BF16),
            pltpu.VMEM((32, wide), BF16),
            pltpu.VMEM((32, 64), F32),
            pltpu.VMEM((walkers, wide), BF16),
            pltpu.VMEM((wide, walkers), BF16),
            pltpu.VMEM((nc, 32, 128), BF16),
            pltpu.VMEM((nr, walkers, 128), BF16),
            pltpu.VMEM((16, 128), F32),
            pltpu.VMEM((nc, 16, 128), F32),
            pltpu.VMEM((wide, 64), BF16),
            pltpu.VMEM((96, wide), BF16),
            pltpu.VMEM((nc // 2, 32, 128), F32),
            pltpu.VMEM((2, 16, 128), F32),
            pltpu.VMEM((2, 16, 128), F32),
            pltpu.VMEM((2, 16, 128), F32),
            pltpu.VMEM((2, nz, 16, 128), F32),
            pltpu.VMEM((2, 8, 128), F32),
            pltpu.VMEM((2, 8, 128), F32),
            pltpu.VMEM((2, 8, 128), F32),
            pltpu.VMEM((2, nz, 8, 128), F32),
            pltpu.VMEM((2, 16, 128), F32),
            pltpu.VMEM((2, nc, 16, 128), F32),
            pltpu.VMEM((1, 128), F32),
            pltpu.VMEM((nr, 1, 128), F32),
            pltpu.SemaphoreType.DMA((3,)),
            pltpu.SemaphoreType.DMA((17,)),
            pltpu.SemaphoreType.DMA((17,)),
            pltpu.SemaphoreType.DMA((4, 2, full + 2)),
        ],
        compiler_params=pltpu.CompilerParams(
            collective_id=0, has_side_effects=True, vmem_limit_bytes=24 * 1024 * 1024
        ),
        name="davidson",
    )(*(pltpu.with_memory_space_constraint(x, pltpu.HBM) for x in arguments))

    corr, ham, one, two, ray = pl.pallas_call(
        write,
        out_shape=(
            jax.ShapeDtypeStruct((1, wide, narrow), F32),
            jax.ShapeDtypeStruct((1, wide, narrow), F32),
            *small,
        ),
        in_specs=[vmem] * 4,
        out_specs=(hbm,) * 5,
        scratch_shapes=[pltpu.SemaphoreType.DMA((11,))],
        compiler_params=pltpu.CompilerParams(vmem_limit_bytes=24 * 1024 * 1024),
        name="tiles",
    )(*(pltpu.with_memory_space_constraint(x, pltpu.VMEM) for x in results))
    return one.T, two.T, ray, corr, ham


def solution(mesh):
    return jax.shard_map(
        functools.partial(local, mesh.shape["prow"], mesh.shape["pcol"]),
        mesh=mesh,
        in_specs=(P("pcol", "prow"), P("pcol", "prow"), P(("prow", "pcol"), None)),
        out_specs=(
            P(("prow", "pcol"), None),
            P(("prow", "pcol"), None),
            P(),
            P("pcol", "prow", None),
            P("pcol", "prow", None),
        ),
        check_vma=False,
    )
```

```python
import contextlib
import functools

import jax
import jax.numpy as jnp
from jax import lax
from jax.experimental import pallas as pl
from jax.experimental.pallas import tpu as pltpu
from jax.sharding import PartitionSpec as P

STABILIZER = 0.5
EPSILON = 1e-6
F32 = jnp.float32
BF16 = jnp.bfloat16
HIGHEST = lax.Precision.HIGHEST
MESH = pl.DeviceIdType.MESH
NT = (((1,), (1,)), ((), ()))
TN = (((0,), (0,)), ((), ()))


def scope(name):
    return contextlib.nullcontext()


def pieces(x):
    high = x.astype(BF16)
    rest = x - high.astype(F32)
    middle = rest.astype(BF16)
    low = (rest - middle.astype(F32)).astype(BF16)
    return jnp.concatenate([high, middle, low], axis=0)


def sum_rows(x, n):
    return x[:n] + x[n : 2 * n] + x[2 * n : 3 * n]


def to_row(column, eye):
    return jnp.sum(jnp.where(eye, column, 0.0), axis=0, keepdims=True)


def to_column(row, eye):
    return jnp.sum(jnp.where(eye, row, 0.0), axis=1, keepdims=True)


def fold(x):
    return jnp.concatenate([x[8 * g : 8 * g + 8] for g in range(4)], axis=1)


def unfold(folded):
    return jnp.concatenate(
        [
            jnp.concatenate([x[:, 32 * g : 32 * g + 32] for x in folded], axis=1)
            for g in range(4)
        ],
        axis=0,
    )


def inverse_of_two(a, b, d):
    scale = 1.0 / (a * d - b * b)
    return d * scale, -b * scale, a * scale


def solver_of_four(columns, k):
    g = [[columns[j][k + i : k + i + 1] for j in range(4)] for i in range(4)]
    p0, p1, p2 = inverse_of_two(g[0][0], g[1][0], g[1][1])
    t02, t12 = p0 * g[2][0] + p1 * g[2][1], p1 * g[2][0] + p2 * g[2][1]
    t03, t13 = p0 * g[3][0] + p1 * g[3][1], p1 * g[3][0] + p2 * g[3][1]
    w0, w1, w2 = inverse_of_two(
        g[2][2] - g[2][0] * t02 - g[2][1] * t12,
        g[3][2] - g[3][0] * t02 - g[3][1] * t12,
        g[3][3] - g[3][0] * t03 - g[3][1] * t13,
    )

    def solve(array):
        r = [array[k + i : k + i + 1] for i in range(4)]
        u0, u1 = p0 * r[0] + p1 * r[1], p1 * r[0] + p2 * r[1]
        v2 = r[2] - t02 * r[0] - t12 * r[1]
        v3 = r[3] - t03 * r[0] - t13 * r[1]
        x2, x3 = w0 * v2 + w1 * v3, w1 * v2 + w2 * v3
        return u0 - t02 * x2 - t03 * x3, u1 - t12 * x2 - t13 * x3, x2, x3

    return solve


def eliminate(matrix, right, eye):
    n = matrix.shape[0]
    diagonal = jnp.where(eye, matrix, 0.0)
    unit = lax.rsqrt(jnp.sum(diagonal, axis=1, keepdims=True))
    unit_row = lax.rsqrt(jnp.sum(diagonal, axis=0, keepdims=True))
    both = jnp.concatenate([matrix * unit * unit_row, right * unit], axis=1)
    rows = lax.broadcasted_iota(jnp.int32, both.shape, 0)

    def spread(at):
        return [
            jnp.broadcast_to(both[:, at + j : at + j + 1], both.shape)
            for j in range(4 if at < n else 0)
        ]

    now, later = spread(0), spread(4)
    for k in range(0, n, 4):
        solve = solver_of_four(now, k)
        pivots = (rows >= k) & (rows < k + 4)
        c = [
            jnp.where(rows == k + j, -1.0, jnp.where(pivots, 0.0, now[j]))
            for j in range(4)
        ]

        def step(array):
            x = solve(array)
            rest = jnp.where(pivots, 0.0, array)
            return (rest - c[0] * x[0] - c[1] * x[1]) - (c[2] * x[2] + c[3] * x[3])

        now = [step(array) for array in later]
        both = step(both)
        later = spread(k + 8)
    return both[:, n:] * unit


def farthest_first(m, n):
    steps = [(i, j) for i in range(m) for j in range(n) if i or j]
    return sorted(steps, key=lambda s: -min(s[0], m - s[0]) - min(s[1], n - s[1]))


def davidson(
    nr,
    nc,
    l_hbm,
    e_hbm,
    v_hbm,
    tiles_ref,
    one_ref,
    two_ref,
    ray_ref,
    norms_ref,
    l_ref,
    e_ref,
    v_ref,
    block,
    own_t,
    slabs,
    gathered,
    v_send,
    v_recv,
    weights,
    split_all,
    basis,
    pair_send,
    pair_recv,
    image_send,
    image_recv,
    gram_pair_send,
    gram_pair_recv,
    gram_send,
    gram_recv,
    walk_send,
    walk_recv,
    norm_send,
    norm_recv,
    loads,
    sends,
    recvs,
    ring_sems,
):
    p = lax.axis_index("prow")
    q = lax.axis_index("pcol")
    z = p // 2
    core = p % 2
    nz = nr // 2
    wide = 64 * nc
    walkers = 32 * nc
    params = wide * nr

    def row_of(zz, cc):
        return lax.rem(zz + nz, nz) * 2 + cc

    sibling = z * 2 + 1 - core

    def push(src, dst, send_sem, recv_sem, device):
        pltpu.make_async_remote_copy(
            src_ref=src,
            dst_ref=dst,
            send_sem=send_sem,
            recv_sem=recv_sem,
            device_id=device,
            device_id_type=MESH,
        ).start()

    def sent(ref, sem):
        pltpu.make_async_remote_copy(
            src_ref=ref,
            dst_ref=ref,
            send_sem=sem,
            recv_sem=sem,
            device_id={"prow": sibling},
            device_id_type=MESH,
        ).wait_send()

    def landed(ref, sem):
        pltpu.make_async_remote_copy(
            src_ref=ref,
            dst_ref=ref,
            send_sem=sem,
            recv_sem=sem,
            device_id={"prow": sibling},
            device_id_type=MESH,
        ).wait_recv()

    barrier = pltpu.get_barrier_semaphore()

    nx = 4
    ny = nc // nx
    x, y = q % nx, q // nx

    def along_x(i):
        return y * nx + lax.rem(x + i, nx)

    def along_y(i):
        return lax.rem(y + i, ny) * nx + x

    plane = [
        lax.rem(y + j, ny) * nx + lax.rem(x + i, nx)
        for i, j in farthest_first(nx, ny)
    ]
    chips = [row_of(z + i, core) for i, _ in farthest_first(nz, 1)]
    rows = [
        row_of(z + i, lax.rem(core + j, 2)) for i, j in farthest_first(nz, 2)
    ]
    far_rows = len(rows) // 3
    for axis, members in (
        ("pcol", plane[: nc // 3]),
        ("prow", rows[:far_rows]),
        ("pcol", plane[nc // 3 :]),
        ("prow", rows[far_rows:]),
    ):
        for member in members:
            pl.semaphore_signal(
                barrier, inc=1, device_id={axis: member}, device_id_type=MESH
            )
    reads = [
        pltpu.make_async_copy(src, dst, loads.at[i])
        for i, (src, dst) in enumerate(((v_hbm, v_ref), (l_hbm, l_ref), (e_hbm, e_ref)))
    ]
    for read in reads:
        read.start()


    def to_plane(copy):
        for peer in plane:
            copy(peer)

    reads[0].wait()
    v_own = v_ref[...]
    v_send[...] = jnp.concatenate([v_own[:16], v_own[16:]], axis=1)
    v_recv[pl.ds(q, 1)] = v_send[...][None]
    reads[1].wait()
    reads[2].wait()
    l_own = l_ref[...]
    e_own = e_ref[...]
    for j in range(nc):
        slabs[j] = jnp.concatenate(
            [l_own[:, 64 * j : 64 * j + 64], e_own[:, 64 * j : 64 * j + 64]], axis=1
        )
    own_rows = pl.ds(pl.multiple_of(q * 32, 32), 32)
    gathered[pl.ds(p, 1), own_rows, :] = slabs[pl.ds(q, 1)]
    block[own_rows, :] = l_own
    weights[...] = jnp.concatenate([l_own, e_own], axis=0).T
    with scope("barrier"):
        pl.semaphore_wait(barrier, nc - 1 + nr - 1)
    to_plane(
        lambda peer: push(
            v_send, v_recv.at[q], sends.at[0], recvs.at[0], {"pcol": peer}
        )
    )
    def half_of(member, part):
        return block.at[pl.ds(pl.multiple_of(member * 32 + 16 * part, 16), 16)]

    def block_first():
        for i in range(1, nx):
            ref = half_of(q, 0)
            push(ref, ref, sends.at[2], recvs.at[2], {"pcol": along_x(i)})
        for i in range(1, ny):
            ref = half_of(q, 1)
            push(ref, ref, sends.at[10], recvs.at[10], {"pcol": along_y(i)})

    def block_second():
        landed(block.at[pl.ds(0, 16 * (nx - 1))], recvs.at[2])
        landed(block.at[pl.ds(0, 16 * (ny - 1))], recvs.at[10])

        def forward_y(i, carry):
            for k in range(nx):
                ref = half_of(along_x(k), 0)
                push(ref, ref, sends.at[11], recvs.at[11], {"pcol": along_y(i)})
            return carry

        def forward_x(i, carry):
            for k in range(ny):
                ref = half_of(along_y(k), 1)
                push(ref, ref, sends.at[12], recvs.at[12], {"pcol": along_x(i)})
            return carry

        lax.fori_loop(1, ny, forward_y, 0)
        lax.fori_loop(1, nx, forward_x, 0)

    counts = (nx - 1, ny - 1, nx * (ny - 1), ny * (nx - 1))

    def block_landed():
        for sem, count in zip((11, 12), counts[2:], strict=True):
            landed(block.at[pl.ds(0, 16 * count)], recvs.at[sem])

    def block_sent():
        for sem, count in zip((2, 10, 11, 12), counts, strict=True):
            sent(block.at[pl.ds(0, 16 * count)], sends.at[sem])

    block_first()
    to_plane(
        lambda peer: push(
            slabs.at[peer],
            gathered.at[p, own_rows],
            sends.at[1],
            recvs.at[1],
            {"pcol": peer},
        )
    )

    eye = lax.broadcasted_iota(jnp.int32, (32, 32), 0) == lax.broadcasted_iota(
        jnp.int32, (32, 32), 1
    )
    far = pl.ds(0, nc - 1)

    full = nz // 2 - 1
    half = walkers // 2
    everything, lower, upper = pl.ds(0, walkers), pl.ds(0, half), pl.ds(half, half)

    def part_of(way, step):
        return everything if step < full else (lower, upper)[way]

    def ring_start():
        landed(gathered.at[0, pl.ds(0, 32 * (nc - 1))], recvs.at[1])
        ring_send(0)
        own = gathered.at[p]
        push(
            own,
            own,
            ring_sems.at[2, 0, full + 1],
            ring_sems.at[3, 0, full + 1],
            {"prow": sibling},
        )

    def ring_send(step):
        for way, sign in ((0, 1), (1, -1)):
            ref = gathered.at[row_of(z - sign * step, core), part_of(way, step)]
            push(
                ref,
                ref,
                ring_sems.at[0, way, step],
                ring_sems.at[1, way, step],
                {"prow": row_of(z + sign, core)},
            )

    def ring_landed(step):
        for way, sign in ((0, 1), (1, -1)):
            ref = gathered.at[row_of(z - sign * (step + 1), core), part_of(way, step)]
            landed(ref, ring_sems.at[1, way, step])
            push(
                ref,
                ref,
                ring_sems.at[2, way, step],
                ring_sems.at[3, way, step],
                {"prow": sibling},
            )

    def ring_advance(step):
        if step <= full:
            ring_landed(step)
        if step < full:
            ring_send(step + 1)

    def sibling_landed(step):
        for way, sign in ((0, 1), (1, -1)):
            chunk = row_of(z - sign * (step + 1), 1 - core)
            landed(gathered.at[chunk, part_of(way, step)], ring_sems.at[3, way, step])

    def ring_sent():
        sent(gathered.at[p], ring_sems.at[2, 0, full + 1])
        for step in range(full + 1):
            for way in range(2):
                ref = gathered.at[p, part_of(way, step)]
                sent(ref, ring_sems.at[0, way, step])
                sent(ref, ring_sems.at[2, way, step])

    def multiply(chunk):
        a = gathered[pl.ds(2 * chunk, 1)][0]
        b = gathered[pl.ds(2 * chunk + 1, 1)][0]
        right = jnp.concatenate(
            [a[:, :64], b[:, :64], a[:, 64:], b[:, 64:]], axis=1
        )
        out = jnp.dot(own_t[...], right, preferred_element_type=F32) * (1.0 / walkers)
        columns = pl.ds(pl.multiple_of(chunk * 128, 128), 128)
        tiles_ref[0, :, columns] = out[:, :128]
        tiles_ref[1, :, columns] = out[:, 128:]

    def multiply_own():
        own_t[...] = block[...].T
        landed(gathered.at[sibling], ring_sems.at[3, 0, full + 1])
        multiply(z)
        row = lax.broadcasted_iota(jnp.int32, (64, 128), 0)
        column = lax.broadcasted_iota(jnp.int32, (64, 128), 1)
        mine = pl.ds(pl.multiple_of(q * 64, 64), 64)
        columns = pl.ds(pl.multiple_of(z * 128, 128), 128)
        tiles_ref[0, mine, columns] += jnp.where(
            column == row + core * 64, STABILIZER, 0.0
        )

    def multiply_step(step):
        if step > full:
            return
        sibling_landed(step)

        def body(way, carry):
            multiply(lax.rem(z + (2 * way - 1) * (step + 1) + nz, nz))
            return carry

        lax.fori_loop(0, 2 if step < full else 1, body, 0)

    def both_cores(src, dst, turn, sem):
        push(
            src.at[turn],
            dst.at[turn],
            sends.at[sem + turn],
            recvs.at[sem + turn],
            {"prow": sibling},
        )

    def along_z(src, dst, turn, sem):
        for chip in chips:
            push(
                src.at[turn],
                dst.at[turn, z],
                sends.at[sem + turn],
                recvs.at[sem + turn],
                {"prow": chip},
            )

    def image_start(vec, turn):
        with scope("values"):
            split = pieces(vec)
            out = sum_rows(jnp.dot(split, weights[...], preferred_element_type=F32), 32)
            pair_send[turn] = jnp.concatenate(
                [fold(out[:, :32]), fold(out[:, 32:])], axis=0
            )
        both_cores(pair_send, pair_recv, turn, 4)
        if turn == 0:
            with scope("block_second"):
                block_second()
        else:
            sent(v_recv.at[far], sends.at[0])
        with scope("gram"):
            split_all[...] = split
            out = lax.dot_general(
                split, split_all[...], NT, preferred_element_type=F32
            )
            out = sum_rows(out, 32)
            gram_pair_send[turn] = fold(out[:, :32] + out[:, 32:64] + out[:, 64:])
        both_cores(gram_pair_send, gram_pair_recv, turn, 15)
        with scope("wait_pair"):
            landed(pair_recv.at[turn], recvs.at[4 + turn])
        with scope("pair_sum"):
            mine = pair_send[turn] + pair_recv[turn]
            image_send[turn] = mine
            image_recv[turn, pl.ds(z, 1)] = mine[None]
        along_z(image_send, image_recv, turn, 6)
        landed(gram_pair_recv.at[turn], recvs.at[15 + turn])
        mine = gram_pair_send[turn] + gram_pair_recv[turn]
        gram_send[turn] = mine
        gram_recv[turn, pl.ds(z, 1)] = mine[None]
        along_z(gram_send, gram_recv, turn, 13)

    def walk_start(turn):
        with scope("wait_image"):
            landed(image_recv.at[turn, pl.ds(0, nz - 1)], recvs.at[6 + turn])
        with scope("image_sum"):
            mine = jnp.sum(image_recv[turn], axis=0)
            walk_send[turn] = mine
        walk_recv[turn, pl.ds(q, 1)] = mine[None]
        to_plane(
            lambda peer: push(
                walk_send.at[turn],
                walk_recv.at[turn, q],
                sends.at[8 + turn],
                recvs.at[8 + turn],
                {"pcol": peer},
            )
        )

    def gram_landed(turn):
        landed(gram_recv.at[turn, pl.ds(0, nz - 1)], recvs.at[13 + turn])
        return unfold([jnp.sum(gram_recv[turn], axis=0)])

    def walk_landed(turn):
        with scope("wait_walk"):
            landed(walk_recv.at[turn, far], recvs.at[8 + turn])
        return [
            jnp.concatenate(
                [
                    unfold([walk_recv[turn, k + j, rows] for j in range(4)])
                    for k in range(0, nc, 4)
                ],
                axis=1,
            )
            for rows in (slice(0, 8), slice(8, 16))
        ]

    def residual(vec, l_val, e_val, gram, inverse_diag):
        with scope("products"):
            l_split = pieces(l_val)
            both = jnp.concatenate([l_split, pieces(e_val)], axis=0)
            out = sum_rows(
                lax.dot_general(l_split, both, NT, preferred_element_type=F32), 32
            )
        ray_s = out[:, :32] + out[:, 32:64] + out[:, 64:96]
        ray_h = out[:, 96:128] + out[:, 128:160] + out[:, 160:192]
        with scope("images"):
            image = jnp.dot(both, block[...], preferred_element_type=F32)
            image_s = sum_rows(image[:96], 32) * (1.0 / walkers) + STABILIZER * vec
            image_h = sum_rows(image[96:], 32) * (1.0 / walkers) * inverse_diag
            s = pieces(image_s * inverse_diag)
            right = jnp.concatenate(
                [s[:32], s[32:64], s[:32], s[64:], s[32:64], s[:32]], axis=0
            )
        with scope("eliminate"):
            coeffs = eliminate(
                ray_s * (1.0 / walkers) + STABILIZER * gram,
                ray_h * (1.0 / walkers),
                eye,
            )
        with scope("mix"):
            c = pieces(coeffs)
            left = jnp.concatenate(
                [c[:32], c[:32], c[32:64], c[:32], c[32:64], c[64:]], axis=0
            )
            out = lax.dot_general(left, right, TN, preferred_element_type=F32)
            result = image_h - out
        return result, coeffs

    def own_part(vec):
        for k in range(nc // 2):
            basis[k] = vec[:, 128 * k : 128 * k + 128]
        chunk = basis[pl.ds(q // 2, 1)][0]
        return jnp.where(q % 2 == 0, chunk[:, :64], chunk[:, 64:])

    with scope("wait_v"):
        landed(v_recv.at[far], recvs.at[0])
    top, bottom = [], []
    for k in range(0, nc, 2):
        a, b = v_recv[k], v_recv[k + 1]
        top += [a[:, :64], b[:, :64]]
        bottom += [a[:, 64:], b[:, 64:]]
    vec = jnp.concatenate(
        [jnp.concatenate(top, axis=1), jnp.concatenate(bottom, axis=1)], axis=0
    )
    image_start(vec, 0)
    with scope("ring_start"):
        ring_start()
    walk_start(0)
    with scope("wait_block"):
        block_landed()
    squares = jnp.zeros((8, wide), F32)
    for k in range(0, walkers, 16):
        part = block[k : k + 16].astype(F32)
        part = part * part
        squares = squares + part[:8] + part[8:]
    inverse_diag = 1.0 / (
        jnp.sum(squares, axis=0, keepdims=True) * (1.0 / walkers) + STABILIZER
    )
    gram = gram_landed(0)
    with scope("ring_0"):
        ring_advance(0)
    l_val, e_val = walk_landed(0)
    vec, _ = residual(vec, l_val, e_val, gram, inverse_diag)

    image_start(vec, 1)
    with scope("ring_1"):
        ring_advance(1)
    with scope("tiles_a"):
        multiply_own()
        multiply_step(0)
    walk_start(1)
    with scope("tiles_b"):
        multiply_step(1)
    with scope("ring_2"):
        ring_advance(2)
    gram = gram_landed(1)
    norms = jnp.sum(jnp.where(eye, gram, 0.0), axis=1, keepdims=True)
    scale = 1.0 / jnp.sqrt(norms * (1.0 / params) + EPSILON)
    gram = gram * scale * to_row(scale, eye)
    vec = vec * scale
    one_ref[...] = own_part(vec)
    l_val, e_val = walk_landed(1)
    vec, coeffs = residual(vec, l_val * scale, e_val * scale, gram, inverse_diag)
    norms = to_row(jnp.sum(vec * vec, axis=1, keepdims=True), eye)
    norm_send[...] = jnp.concatenate([norms, jnp.zeros((1, 96), F32)], axis=1)
    norm_recv[pl.ds(p, 1)] = norm_send[...][None]

    for row in rows:
        push(norm_send, norm_recv.at[p], sends.at[3], recvs.at[3], {"prow": row})
    block_sent()
    ray_ref[...] = coeffs
    two_ref[...] = own_part(vec)
    with scope("tiles_c"):
        multiply_step(2)
    with scope("ring_3"):
        ring_advance(3)
    with scope("tiles_d"):
        multiply_step(3)
    ring_sent()
    sent(gathered.at[0, pl.ds(0, 32 * (nc - 1))], sends.at[1])
    for turn in range(2):
        sent(pair_send.at[turn], sends.at[4 + turn])
        sent(gram_pair_send.at[turn], sends.at[15 + turn])
        sent(image_recv.at[turn, pl.ds(0, nz - 1)], sends.at[6 + turn])
        sent(gram_recv.at[turn, pl.ds(0, nz - 1)], sends.at[13 + turn])
        sent(walk_recv.at[turn, far], sends.at[8 + turn])
    with scope("wait_norm"):
        landed(norm_recv.at[pl.ds(0, nr - 1)], recvs.at[3])
    norms_ref[...] = jnp.sum(norm_recv[...], axis=0)
    sent(norm_recv.at[pl.ds(0, nr - 1)], sends.at[3])


def write(
    params,
    tiles,
    one,
    two,
    ray,
    norms,
    corr_ref,
    ham_ref,
    one_ref,
    two_ref,
    ray_ref,
    scaled,
    sems,
):
    rows = tiles.shape[1] // 4
    pairs = []
    for k in range(4):
        part = pl.ds(k * rows, rows)
        pairs.append((tiles.at[0, part], corr_ref.at[0, part]))
        pairs.append((tiles.at[1, part], ham_ref.at[0, part]))
    pairs += [(one, one_ref), (ray, ray_ref), (scaled, two_ref)]
    writes = [
        pltpu.make_async_copy(src, dst, sems.at[i])
        for i, (src, dst) in enumerate(pairs)
    ]
    for copy in writes[:-1]:
        copy.start()
    eye = lax.broadcasted_iota(jnp.int32, (32, 32), 0) == lax.broadcasted_iota(
        jnp.int32, (32, 32), 1
    )
    squares = to_column(norms[:, :32], eye)
    scaled[...] = two[...] * (1.0 / jnp.sqrt(squares * (1.0 / params) + EPSILON))
    writes[-1].start()
    for copy in writes:
        copy.wait()


def local(nr, nc, log_derivs, energy_derivs, start_block):
    wide, walkers, narrow = 64 * nc, 32 * nc, 64 * nr
    nz = nr // 2
    vmem = pl.BlockSpec(memory_space=pltpu.VMEM)
    full = nz // 2 - 1
    hbm = pl.BlockSpec(memory_space=pltpu.HBM)
    small = (
        jax.ShapeDtypeStruct((32, 64), F32),
        jax.ShapeDtypeStruct((32, 64), F32),
        jax.ShapeDtypeStruct((32, 32), F32),
    )
    arguments = (log_derivs, energy_derivs, start_block.T)
    results = pl.pallas_call(
        functools.partial(davidson, nr, nc),
        out_shape=(
            pltpu.VMEM((2, wide, narrow), F32),
            *(pltpu.VMEM(x.shape, F32) for x in small),
            pltpu.VMEM((1, 128), F32),
        ),
        in_specs=[hbm] * 3,
        out_specs=(vmem,) * 5,
        scratch_shapes=[
            pltpu.VMEM((32, wide), BF16),
            pltpu.VMEM((32, wide), BF16),
            pltpu.VMEM((32, 64), F32),
            pltpu.VMEM((walkers, wide), BF16),
            pltpu.VMEM((wide, walkers), BF16),
            pltpu.VMEM((nc, 32, 128), BF16),
            pltpu.VMEM((nr, walkers, 128), BF16),
            pltpu.VMEM((16, 128), F32),
            pltpu.VMEM((nc, 16, 128), F32),
            pltpu.VMEM((wide, 64), BF16),
            pltpu.VMEM((96, wide), BF16),
            pltpu.VMEM((nc // 2, 32, 128), F32),
            pltpu.VMEM((2, 16, 128), F32),
            pltpu.VMEM((2, 16, 128), F32),
            pltpu.VMEM((2, 16, 128), F32),
            pltpu.VMEM((2, nz, 16, 128), F32),
            pltpu.VMEM((2, 8, 128), F32),
            pltpu.VMEM((2, 8, 128), F32),
            pltpu.VMEM((2, 8, 128), F32),
            pltpu.VMEM((2, nz, 8, 128), F32),
            pltpu.VMEM((2, 16, 128), F32),
            pltpu.VMEM((2, nc, 16, 128), F32),
            pltpu.VMEM((1, 128), F32),
            pltpu.VMEM((nr, 1, 128), F32),
            pltpu.SemaphoreType.DMA((3,)),
            pltpu.SemaphoreType.DMA((17,)),
            pltpu.SemaphoreType.DMA((17,)),
            pltpu.SemaphoreType.DMA((4, 2, full + 2)),
        ],
        compiler_params=pltpu.CompilerParams(
            collective_id=0, has_side_effects=True, vmem_limit_bytes=24 * 1024 * 1024
        ),
        name="davidson",
    )(*(pltpu.with_memory_space_constraint(x, pltpu.HBM) for x in arguments))

    corr, ham, one, two, ray = pl.pallas_call(
        functools.partial(write, 64 * nc * nr),
        out_shape=(
            jax.ShapeDtypeStruct((1, wide, narrow), F32),
            jax.ShapeDtypeStruct((1, wide, narrow), F32),
            *small,
        ),
        in_specs=[vmem] * 5,
        out_specs=(hbm,) * 5,
        scratch_shapes=[pltpu.VMEM((32, 64), F32), pltpu.SemaphoreType.DMA((11,))],
        compiler_params=pltpu.CompilerParams(vmem_limit_bytes=24 * 1024 * 1024),
        name="tiles",
    )(*(pltpu.with_memory_space_constraint(x, pltpu.VMEM) for x in results))
    return one.T, two.T, ray, corr, ham


def solution(mesh):
    return jax.shard_map(
        functools.partial(local, mesh.shape["prow"], mesh.shape["pcol"]),
        mesh=mesh,
        in_specs=(P("pcol", "prow"), P("pcol", "prow"), P(("prow", "pcol"), None)),
        out_specs=(
            P(("prow", "pcol"), None),
            P(("prow", "pcol"), None),
            P(),
            P("pcol", "prow", None),
            P("pcol", "prow", None),
        ),
        check_vma=False,
    )
```

```python
import contextlib
import functools

import jax
import jax.numpy as jnp
from jax import lax
from jax.experimental import pallas as pl
from jax.experimental.pallas import tpu as pltpu
from jax.sharding import PartitionSpec as P

STABILIZER = 0.5
EPSILON = 1e-6
F32 = jnp.float32
BF16 = jnp.bfloat16
HIGHEST = lax.Precision.HIGHEST
MESH = pl.DeviceIdType.MESH
NT = (((1,), (1,)), ((), ()))
TN = (((0,), (0,)), ((), ()))


def scope(name):
    return contextlib.nullcontext()


def pieces(x):
    high = x.astype(BF16)
    rest = x - high.astype(F32)
    middle = rest.astype(BF16)
    low = (rest - middle.astype(F32)).astype(BF16)
    return jnp.concatenate([high, middle, low], axis=0)


def sum_rows(x, n):
    return x[:n] + x[n : 2 * n] + x[2 * n : 3 * n]


def to_row(column, eye):
    return jnp.sum(jnp.where(eye, column, 0.0), axis=0, keepdims=True)


def to_column(row, eye):
    return jnp.sum(jnp.where(eye, row, 0.0), axis=1, keepdims=True)


def fold(x):
    return jnp.concatenate([x[8 * g : 8 * g + 8] for g in range(4)], axis=1)


def unfold(folded):
    return jnp.concatenate(
        [
            jnp.concatenate([x[:, 32 * g : 32 * g + 32] for x in folded], axis=1)
            for g in range(4)
        ],
        axis=0,
    )


def inverse_of_two(a, b, d):
    scale = 1.0 / (a * d - b * b)
    return d * scale, -b * scale, a * scale


def solver_of_four(columns, k):
    g = [[columns[j][k + i : k + i + 1] for j in range(4)] for i in range(4)]
    p0, p1, p2 = inverse_of_two(g[0][0], g[1][0], g[1][1])
    t02, t12 = p0 * g[2][0] + p1 * g[2][1], p1 * g[2][0] + p2 * g[2][1]
    t03, t13 = p0 * g[3][0] + p1 * g[3][1], p1 * g[3][0] + p2 * g[3][1]
    w0, w1, w2 = inverse_of_two(
        g[2][2] - g[2][0] * t02 - g[2][1] * t12,
        g[3][2] - g[3][0] * t02 - g[3][1] * t12,
        g[3][3] - g[3][0] * t03 - g[3][1] * t13,
    )

    def solve(array):
        r = [array[k + i : k + i + 1] for i in range(4)]
        u0, u1 = p0 * r[0] + p1 * r[1], p1 * r[0] + p2 * r[1]
        v2 = r[2] - t02 * r[0] - t12 * r[1]
        v3 = r[3] - t03 * r[0] - t13 * r[1]
        x2, x3 = w0 * v2 + w1 * v3, w1 * v2 + w2 * v3
        return u0 - t02 * x2 - t03 * x3, u1 - t12 * x2 - t13 * x3, x2, x3

    return solve


def eliminate(matrix, right, eye):
    n = matrix.shape[0]
    diagonal = jnp.where(eye, matrix, 0.0)
    unit = lax.rsqrt(jnp.sum(diagonal, axis=1, keepdims=True))
    unit_row = lax.rsqrt(jnp.sum(diagonal, axis=0, keepdims=True))
    both = jnp.concatenate([matrix * unit * unit_row, right * unit], axis=1)
    rows = lax.broadcasted_iota(jnp.int32, both.shape, 0)

    def spread(at):
        return [
            jnp.broadcast_to(both[:, at + j : at + j + 1], both.shape)
            for j in range(4 if at < n else 0)
        ]

    now, later = spread(0), spread(4)
    for k in range(0, n, 4):
        solve = solver_of_four(now, k)
        pivots = (rows >= k) & (rows < k + 4)
        c = [
            jnp.where(rows == k + j, -1.0, jnp.where(pivots, 0.0, now[j]))
            for j in range(4)
        ]

        def step(array):
            x = solve(array)
            rest = jnp.where(pivots, 0.0, array)
            return (rest - c[0] * x[0] - c[1] * x[1]) - (c[2] * x[2] + c[3] * x[3])

        now = [step(array) for array in later]
        both = step(both)
        later = spread(k + 8)
    return both[:, n:] * unit


def farthest_first(m, n):
    steps = [(i, j) for i in range(m) for j in range(n) if i or j]
    return sorted(steps, key=lambda s: -min(s[0], m - s[0]) - min(s[1], n - s[1]))


def davidson(
    nr,
    nc,
    l_hbm,
    e_hbm,
    v_hbm,
    tiles_ref,
    one_ref,
    two_ref,
    ray_ref,
    norms_ref,
    l_ref,
    e_ref,
    v_ref,
    block,
    own_t,
    slabs,
    gathered,
    v_send,
    v_recv,
    weights,
    split_all,
    basis,
    pair_send,
    pair_recv,
    image_send,
    image_recv,
    gram_pair_send,
    gram_pair_recv,
    gram_send,
    gram_recv,
    walk_send,
    walk_recv,
    norm_send,
    norm_recv,
    loads,
    sends,
    recvs,
    ring_sems,
):
    p = lax.axis_index("prow")
    q = lax.axis_index("pcol")
    z = p // 2
    core = p % 2
    nz = nr // 2
    wide = 64 * nc
    walkers = 32 * nc
    params = wide * nr

    def row_of(zz, cc):
        return lax.rem(zz + nz, nz) * 2 + cc

    sibling = z * 2 + 1 - core

    def push(src, dst, send_sem, recv_sem, device):
        pltpu.make_async_remote_copy(
            src_ref=src,
            dst_ref=dst,
            send_sem=send_sem,
            recv_sem=recv_sem,
            device_id=device,
            device_id_type=MESH,
        ).start()

    def sent(ref, sem):
        pltpu.make_async_remote_copy(
            src_ref=ref,
            dst_ref=ref,
            send_sem=sem,
            recv_sem=sem,
            device_id={"prow": sibling},
            device_id_type=MESH,
        ).wait_send()

    def landed(ref, sem):
        pltpu.make_async_remote_copy(
            src_ref=ref,
            dst_ref=ref,
            send_sem=sem,
            recv_sem=sem,
            device_id={"prow": sibling},
            device_id_type=MESH,
        ).wait_recv()

    barrier = pltpu.get_barrier_semaphore()

    nx = 4
    ny = nc // nx
    x, y = q % nx, q // nx

    def along_x(i):
        return y * nx + lax.rem(x + i, nx)

    def along_y(i):
        return lax.rem(y + i, ny) * nx + x

    plane = [
        lax.rem(y + j, ny) * nx + lax.rem(x + i, nx)
        for i, j in farthest_first(nx, ny)
    ]
    chips = [row_of(z + i, core) for i, _ in farthest_first(nz, 1)]
    rows = [
        row_of(z + i, lax.rem(core + j, 2)) for i, j in farthest_first(nz, 2)
    ]
    far_rows = len(rows) // 3
    for axis, members in (
        ("pcol", plane[: nc // 3]),
        ("prow", rows[:far_rows]),
        ("pcol", plane[nc // 3 :]),
        ("prow", rows[far_rows:]),
    ):
        for member in members:
            pl.semaphore_signal(
                barrier, inc=1, device_id={axis: member}, device_id_type=MESH
            )
    reads = [
        pltpu.make_async_copy(src, dst, loads.at[i])
        for i, (src, dst) in enumerate(((v_hbm, v_ref), (l_hbm, l_ref), (e_hbm, e_ref)))
    ]
    for read in reads:
        read.start()


    def to_plane(copy):
        for peer in plane:
            copy(peer)

    reads[0].wait()
    v_own = v_ref[...]
    v_send[...] = jnp.concatenate([v_own[:16], v_own[16:]], axis=1)
    v_recv[pl.ds(q, 1)] = v_send[...][None]
    reads[1].wait()
    reads[2].wait()
    l_own = l_ref[...]
    e_own = e_ref[...]
    for j in range(nc):
        slabs[j] = jnp.concatenate(
            [l_own[:, 64 * j : 64 * j + 64], e_own[:, 64 * j : 64 * j + 64]], axis=1
        )
    own_rows = pl.ds(pl.multiple_of(q * 32, 32), 32)
    gathered[pl.ds(p, 1), own_rows, :] = slabs[pl.ds(q, 1)]
    block[own_rows, :] = l_own
    weights[...] = jnp.concatenate([l_own, e_own], axis=0).T
    with scope("barrier"):
        pl.semaphore_wait(barrier, nc - 1 + nr - 1)
    to_plane(
        lambda peer: push(
            v_send, v_recv.at[q], sends.at[0], recvs.at[0], {"pcol": peer}
        )
    )
    def half_of(member, part):
        return block.at[pl.ds(pl.multiple_of(member * 32 + 16 * part, 16), 16)]

    def block_first():
        for i in range(1, nx):
            ref = half_of(q, 0)
            push(ref, ref, sends.at[2], recvs.at[2], {"pcol": along_x(i)})
        for i in range(1, ny):
            ref = half_of(q, 1)
            push(ref, ref, sends.at[10], recvs.at[10], {"pcol": along_y(i)})

    def block_second():
        landed(block.at[pl.ds(0, 16 * (nx - 1))], recvs.at[2])
        landed(block.at[pl.ds(0, 16 * (ny - 1))], recvs.at[10])

        def forward_y(i, carry):
            for k in range(nx):
                ref = half_of(along_x(k), 0)
                push(ref, ref, sends.at[11], recvs.at[11], {"pcol": along_y(i)})
            return carry

        def forward_x(i, carry):
            for k in range(ny):
                ref = half_of(along_y(k), 1)
                push(ref, ref, sends.at[12], recvs.at[12], {"pcol": along_x(i)})
            return carry

        lax.fori_loop(1, ny, forward_y, 0)
        lax.fori_loop(1, nx, forward_x, 0)

    counts = (nx - 1, ny - 1, nx * (ny - 1), ny * (nx - 1))

    def block_landed():
        for sem, count in zip((11, 12), counts[2:], strict=True):
            landed(block.at[pl.ds(0, 16 * count)], recvs.at[sem])

    def block_sent():
        for sem, count in zip((2, 10, 11, 12), counts, strict=True):
            sent(block.at[pl.ds(0, 16 * count)], sends.at[sem])

    block_first()
    to_plane(
        lambda peer: push(
            slabs.at[peer],
            gathered.at[p, own_rows],
            sends.at[1],
            recvs.at[1],
            {"pcol": peer},
        )
    )

    eye = lax.broadcasted_iota(jnp.int32, (32, 32), 0) == lax.broadcasted_iota(
        jnp.int32, (32, 32), 1
    )
    far = pl.ds(0, nc - 1)

    full = nz // 2 - 1
    half = walkers // 2
    everything, lower, upper = pl.ds(0, walkers), pl.ds(0, half), pl.ds(half, half)

    def part_of(way, step):
        return everything if step < full else (lower, upper)[way]

    def ring_start():
        landed(gathered.at[0, pl.ds(0, 32 * (nc - 1))], recvs.at[1])
        ring_send(0)
        own = gathered.at[p]
        push(
            own,
            own,
            ring_sems.at[2, 0, full + 1],
            ring_sems.at[3, 0, full + 1],
            {"prow": sibling},
        )

    def ring_send(step):
        for way, sign in ((0, 1), (1, -1)):
            ref = gathered.at[row_of(z - sign * step, core), part_of(way, step)]
            push(
                ref,
                ref,
                ring_sems.at[0, way, step],
                ring_sems.at[1, way, step],
                {"prow": row_of(z + sign, core)},
            )

    def ring_landed(step):
        for way, sign in ((0, 1), (1, -1)):
            ref = gathered.at[row_of(z - sign * (step + 1), core), part_of(way, step)]
            landed(ref, ring_sems.at[1, way, step])
            push(
                ref,
                ref,
                ring_sems.at[2, way, step],
                ring_sems.at[3, way, step],
                {"prow": sibling},
            )

    def ring_advance(step):
        if step <= full:
            ring_landed(step)
        if step < full:
            ring_send(step + 1)

    def sibling_landed(step):
        for way, sign in ((0, 1), (1, -1)):
            chunk = row_of(z - sign * (step + 1), 1 - core)
            landed(gathered.at[chunk, part_of(way, step)], ring_sems.at[3, way, step])

    def ring_sent():
        sent(gathered.at[p], ring_sems.at[2, 0, full + 1])
        for step in range(full + 1):
            for way in range(2):
                ref = gathered.at[p, part_of(way, step)]
                sent(ref, ring_sems.at[0, way, step])
                sent(ref, ring_sems.at[2, way, step])

    def multiply(chunk):
        a = gathered[pl.ds(2 * chunk, 1)][0]
        b = gathered[pl.ds(2 * chunk + 1, 1)][0]
        right = jnp.concatenate(
            [a[:, :64], b[:, :64], a[:, 64:], b[:, 64:]], axis=1
        )
        out = jnp.dot(own_t[...], right, preferred_element_type=F32) * (1.0 / walkers)
        columns = pl.ds(pl.multiple_of(chunk * 128, 128), 128)
        tiles_ref[0, :, columns] = out[:, :128]
        tiles_ref[1, :, columns] = out[:, 128:]

    def multiply_own():
        own_t[...] = block[...].T
        landed(gathered.at[sibling], ring_sems.at[3, 0, full + 1])
        multiply(z)
        row = lax.broadcasted_iota(jnp.int32, (64, 128), 0)
        column = lax.broadcasted_iota(jnp.int32, (64, 128), 1)
        mine = pl.ds(pl.multiple_of(q * 64, 64), 64)
        columns = pl.ds(pl.multiple_of(z * 128, 128), 128)
        tiles_ref[0, mine, columns] += jnp.where(
            column == row + core * 64, STABILIZER, 0.0
        )

    def multiply_step(step):
        if step > full:
            return
        sibling_landed(step)

        def body(way, carry):
            multiply(lax.rem(z + (2 * way - 1) * (step + 1) + nz, nz))
            return carry

        lax.fori_loop(0, 2 if step < full else 1, body, 0)

    def both_cores(src, dst, turn, sem):
        push(
            src.at[turn],
            dst.at[turn],
            sends.at[sem + turn],
            recvs.at[sem + turn],
            {"prow": sibling},
        )

    def along_z(src, dst, turn, sem):
        for chip in chips:
            push(
                src.at[turn],
                dst.at[turn, z],
                sends.at[sem + turn],
                recvs.at[sem + turn],
                {"prow": chip},
            )

    def image_start(vec, turn):
        with scope("values"):
            split = pieces(vec)
            out = sum_rows(jnp.dot(split, weights[...], preferred_element_type=F32), 32)
            pair_send[turn] = jnp.concatenate(
                [fold(out[:, :32]), fold(out[:, 32:])], axis=0
            )
        both_cores(pair_send, pair_recv, turn, 4)
        if turn == 0:
            with scope("block_second"):
                block_second()
        with scope("wait_pair"):
            landed(pair_recv.at[turn], recvs.at[4 + turn])
        with scope("pair_sum"):
            mine = pair_send[turn] + pair_recv[turn]
            image_send[turn] = mine
            image_recv[turn, pl.ds(z, 1)] = mine[None]
        along_z(image_send, image_recv, turn, 6)
        if turn == 1:
            sent(v_recv.at[far], sends.at[0])
        with scope("gram"):
            split_all[...] = split
            out = lax.dot_general(
                split, split_all[...], NT, preferred_element_type=F32
            )
            out = sum_rows(out, 32)
            gram_pair_send[turn] = fold(out[:, :32] + out[:, 32:64] + out[:, 64:])
        both_cores(gram_pair_send, gram_pair_recv, turn, 15)

    def gram_start(turn):
        landed(gram_pair_recv.at[turn], recvs.at[15 + turn])
        mine = gram_pair_send[turn] + gram_pair_recv[turn]
        gram_send[turn] = mine
        gram_recv[turn, pl.ds(z, 1)] = mine[None]
        along_z(gram_send, gram_recv, turn, 13)

    def walk_start(turn):
        with scope("wait_image"):
            landed(image_recv.at[turn, pl.ds(0, nz - 1)], recvs.at[6 + turn])
        with scope("image_sum"):
            mine = jnp.sum(image_recv[turn], axis=0)
            walk_send[turn] = mine
        walk_recv[turn, pl.ds(q, 1)] = mine[None]
        to_plane(
            lambda peer: push(
                walk_send.at[turn],
                walk_recv.at[turn, q],
                sends.at[8 + turn],
                recvs.at[8 + turn],
                {"pcol": peer},
            )
        )

    def gram_landed(turn):
        landed(gram_recv.at[turn, pl.ds(0, nz - 1)], recvs.at[13 + turn])
        return unfold([jnp.sum(gram_recv[turn], axis=0)])

    def walk_landed(turn):
        with scope("wait_walk"):
            landed(walk_recv.at[turn, far], recvs.at[8 + turn])
        return [
            jnp.concatenate(
                [
                    unfold([walk_recv[turn, k + j, rows] for j in range(4)])
                    for k in range(0, nc, 4)
                ],
                axis=1,
            )
            for rows in (slice(0, 8), slice(8, 16))
        ]

    def residual(vec, l_val, e_val, gram, inverse_diag):
        with scope("products"):
            l_split = pieces(l_val)
            both = jnp.concatenate([l_split, pieces(e_val)], axis=0)
            out = sum_rows(
                lax.dot_general(l_split, both, NT, preferred_element_type=F32), 32
            )
        ray_s = out[:, :32] + out[:, 32:64] + out[:, 64:96]
        ray_h = out[:, 96:128] + out[:, 128:160] + out[:, 160:192]
        with scope("images"):
            image = jnp.dot(both, block[...], preferred_element_type=F32)
            image_s = sum_rows(image[:96], 32) * (1.0 / walkers) + STABILIZER * vec
            image_h = sum_rows(image[96:], 32) * (1.0 / walkers) * inverse_diag
            s = pieces(image_s * inverse_diag)
            right = jnp.concatenate(
                [s[:32], s[32:64], s[:32], s[64:], s[32:64], s[:32]], axis=0
            )
        with scope("eliminate"):
            coeffs = eliminate(
                ray_s * (1.0 / walkers) + STABILIZER * gram,
                ray_h * (1.0 / walkers),
                eye,
            )
        with scope("mix"):
            c = pieces(coeffs)
            left = jnp.concatenate(
                [c[:32], c[:32], c[32:64], c[:32], c[32:64], c[64:]], axis=0
            )
            out = lax.dot_general(left, right, TN, preferred_element_type=F32)
            result = image_h - out
        return result, coeffs

    def own_part(vec):
        for k in range(nc // 2):
            basis[k] = vec[:, 128 * k : 128 * k + 128]
        chunk = basis[pl.ds(q // 2, 1)][0]
        return jnp.where(q % 2 == 0, chunk[:, :64], chunk[:, 64:])

    with scope("wait_v"):
        landed(v_recv.at[far], recvs.at[0])
    top, bottom = [], []
    for k in range(0, nc, 2):
        a, b = v_recv[k], v_recv[k + 1]
        top += [a[:, :64], b[:, :64]]
        bottom += [a[:, 64:], b[:, 64:]]
    vec = jnp.concatenate(
        [jnp.concatenate(top, axis=1), jnp.concatenate(bottom, axis=1)], axis=0
    )
    image_start(vec, 0)
    with scope("ring_start"):
        ring_start()
    gram_start(0)
    walk_start(0)
    with scope("wait_block"):
        block_landed()
    squares = jnp.zeros((8, wide), F32)
    for k in range(0, walkers, 16):
        part = block[k : k + 16].astype(F32)
        part = part * part
        squares = squares + part[:8] + part[8:]
    inverse_diag = 1.0 / (
        jnp.sum(squares, axis=0, keepdims=True) * (1.0 / walkers) + STABILIZER
    )
    gram = gram_landed(0)
    with scope("ring_0"):
        ring_advance(0)
    l_val, e_val = walk_landed(0)
    vec, _ = residual(vec, l_val, e_val, gram, inverse_diag)

    image_start(vec, 1)
    with scope("ring_1"):
        ring_advance(1)
    gram_start(1)
    with scope("tiles_a"):
        multiply_own()
    walk_start(1)
    with scope("tiles_b"):
        multiply_step(0)
    with scope("ring_2"):
        ring_advance(2)
    gram = gram_landed(1)
    norms = jnp.sum(jnp.where(eye, gram, 0.0), axis=1, keepdims=True)
    scale = 1.0 / jnp.sqrt(norms * (1.0 / params) + EPSILON)
    gram = gram * scale * to_row(scale, eye)
    vec = vec * scale
    one_ref[...] = own_part(vec)
    l_val, e_val = walk_landed(1)
    vec, coeffs = residual(vec, l_val * scale, e_val * scale, gram, inverse_diag)
    norms = to_row(jnp.sum(vec * vec, axis=1, keepdims=True), eye)
    norm_send[...] = jnp.concatenate([norms, jnp.zeros((1, 96), F32)], axis=1)
    norm_recv[pl.ds(p, 1)] = norm_send[...][None]

    for row in rows:
        push(norm_send, norm_recv.at[p], sends.at[3], recvs.at[3], {"prow": row})
    block_sent()
    ray_ref[...] = coeffs
    two_ref[...] = own_part(vec)
    with scope("tiles_c"):
        multiply_step(1)
        multiply_step(2)
    with scope("ring_3"):
        ring_advance(3)
    with scope("tiles_d"):
        multiply_step(3)
    ring_sent()
    sent(gathered.at[0, pl.ds(0, 32 * (nc - 1))], sends.at[1])
    for turn in range(2):
        sent(pair_send.at[turn], sends.at[4 + turn])
        sent(gram_pair_send.at[turn], sends.at[15 + turn])
        sent(image_recv.at[turn, pl.ds(0, nz - 1)], sends.at[6 + turn])
        sent(gram_recv.at[turn, pl.ds(0, nz - 1)], sends.at[13 + turn])
        sent(walk_recv.at[turn, far], sends.at[8 + turn])
    with scope("wait_norm"):
        landed(norm_recv.at[pl.ds(0, nr - 1)], recvs.at[3])
    norms_ref[...] = jnp.sum(norm_recv[...], axis=0)
    sent(norm_recv.at[pl.ds(0, nr - 1)], sends.at[3])


def write(
    params,
    tiles,
    one,
    two,
    ray,
    norms,
    corr_ref,
    ham_ref,
    one_ref,
    two_ref,
    ray_ref,
    scaled,
    sems,
):
    rows = tiles.shape[1] // 4
    pairs = []
    for k in range(4):
        part = pl.ds(k * rows, rows)
        pairs.append((tiles.at[0, part], corr_ref.at[0, part]))
        pairs.append((tiles.at[1, part], ham_ref.at[0, part]))
    pairs += [(one, one_ref), (ray, ray_ref), (scaled, two_ref)]
    writes = [
        pltpu.make_async_copy(src, dst, sems.at[i])
        for i, (src, dst) in enumerate(pairs)
    ]
    for copy in writes[:-1]:
        copy.start()
    eye = lax.broadcasted_iota(jnp.int32, (32, 32), 0) == lax.broadcasted_iota(
        jnp.int32, (32, 32), 1
    )
    squares = to_column(norms[:, :32], eye)
    scaled[...] = two[...] * (1.0 / jnp.sqrt(squares * (1.0 / params) + EPSILON))
    writes[-1].start()
    for copy in writes:
        copy.wait()


def local(nr, nc, log_derivs, energy_derivs, start_block):
    wide, walkers, narrow = 64 * nc, 32 * nc, 64 * nr
    nz = nr // 2
    vmem = pl.BlockSpec(memory_space=pltpu.VMEM)
    full = nz // 2 - 1
    hbm = pl.BlockSpec(memory_space=pltpu.HBM)
    small = (
        jax.ShapeDtypeStruct((32, 64), F32),
        jax.ShapeDtypeStruct((32, 64), F32),
        jax.ShapeDtypeStruct((32, 32), F32),
    )
    arguments = (log_derivs, energy_derivs, start_block.T)
    results = pl.pallas_call(
        functools.partial(davidson, nr, nc),
        out_shape=(
            pltpu.VMEM((2, wide, narrow), F32),
            *(pltpu.VMEM(x.shape, F32) for x in small),
            pltpu.VMEM((1, 128), F32),
        ),
        in_specs=[hbm] * 3,
        out_specs=(vmem,) * 5,
        scratch_shapes=[
            pltpu.VMEM((32, wide), BF16),
            pltpu.VMEM((32, wide), BF16),
            pltpu.VMEM((32, 64), F32),
            pltpu.VMEM((walkers, wide), BF16),
            pltpu.VMEM((wide, walkers), BF16),
            pltpu.VMEM((nc, 32, 128), BF16),
            pltpu.VMEM((nr, walkers, 128), BF16),
            pltpu.VMEM((16, 128), F32),
            pltpu.VMEM((nc, 16, 128), F32),
            pltpu.VMEM((wide, 64), BF16),
            pltpu.VMEM((96, wide), BF16),
            pltpu.VMEM((nc // 2, 32, 128), F32),
            pltpu.VMEM((2, 16, 128), F32),
            pltpu.VMEM((2, 16, 128), F32),
            pltpu.VMEM((2, 16, 128), F32),
            pltpu.VMEM((2, nz, 16, 128), F32),
            pltpu.VMEM((2, 8, 128), F32),
            pltpu.VMEM((2, 8, 128), F32),
            pltpu.VMEM((2, 8, 128), F32),
            pltpu.VMEM((2, nz, 8, 128), F32),
            pltpu.VMEM((2, 16, 128), F32),
            pltpu.VMEM((2, nc, 16, 128), F32),
            pltpu.VMEM((1, 128), F32),
            pltpu.VMEM((nr, 1, 128), F32),
            pltpu.SemaphoreType.DMA((3,)),
            pltpu.SemaphoreType.DMA((17,)),
            pltpu.SemaphoreType.DMA((17,)),
            pltpu.SemaphoreType.DMA((4, 2, full + 2)),
        ],
        compiler_params=pltpu.CompilerParams(
            collective_id=0, has_side_effects=True, vmem_limit_bytes=24 * 1024 * 1024
        ),
        name="davidson",
    )(*(pltpu.with_memory_space_constraint(x, pltpu.HBM) for x in arguments))

    corr, ham, one, two, ray = pl.pallas_call(
        functools.partial(write, 64 * nc * nr),
        out_shape=(
            jax.ShapeDtypeStruct((1, wide, narrow), F32),
            jax.ShapeDtypeStruct((1, wide, narrow), F32),
            *small,
        ),
        in_specs=[vmem] * 5,
        out_specs=(hbm,) * 5,
        scratch_shapes=[pltpu.VMEM((32, 64), F32), pltpu.SemaphoreType.DMA((11,))],
        compiler_params=pltpu.CompilerParams(vmem_limit_bytes=24 * 1024 * 1024),
        name="tiles",
    )(*(pltpu.with_memory_space_constraint(x, pltpu.VMEM) for x in results))
    return one.T, two.T, ray, corr, ham


def solution(mesh):
    return jax.shard_map(
        functools.partial(local, mesh.shape["prow"], mesh.shape["pcol"]),
        mesh=mesh,
        in_specs=(P("pcol", "prow"), P("pcol", "prow"), P(("prow", "pcol"), None)),
        out_specs=(
            P(("prow", "pcol"), None),
            P(("prow", "pcol"), None),
            P(),
            P("pcol", "prow", None),
            P("pcol", "prow", None),
        ),
        check_vma=False,
    )
```

```python
import contextlib
import functools

import jax
import jax.numpy as jnp
from jax import lax
from jax.experimental import pallas as pl
from jax.experimental.pallas import tpu as pltpu
from jax.sharding import PartitionSpec as P

STABILIZER = 0.5
EPSILON = 1e-6
ENLARGED = 2.0**30
F32 = jnp.float32
BF16 = jnp.bfloat16
HIGHEST = lax.Precision.HIGHEST
MESH = pl.DeviceIdType.MESH
NT = (((1,), (1,)), ((), ()))
TN = (((0,), (0,)), ((), ()))


def scope(name):
    return contextlib.nullcontext()


def pieces(x):
    high = x.astype(BF16)
    rest = x - high.astype(F32)
    middle = rest.astype(BF16)
    low = (rest - middle.astype(F32)).astype(BF16)
    return jnp.concatenate([high, middle, low], axis=0)


def sum_rows(x, n):
    return x[:n] + x[n : 2 * n] + x[2 * n : 3 * n]


def to_row(column, eye):
    return jnp.sum(jnp.where(eye, column, 0.0), axis=0, keepdims=True)


def to_column(row, eye):
    return jnp.sum(jnp.where(eye, row, 0.0), axis=1, keepdims=True)


def fold(x):
    return jnp.concatenate([x[8 * g : 8 * g + 8] for g in range(4)], axis=1)


def unfold(folded):
    return jnp.concatenate(
        [
            jnp.concatenate([x[:, 32 * g : 32 * g + 32] for x in folded], axis=1)
            for g in range(4)
        ],
        axis=0,
    )


def inverse_of_two(a, b, d):
    scale = 1.0 / (a * d - b * b)
    return d * scale, -b * scale, a * scale


def solver_of_four(columns, k):
    g = [[columns[j][k + i : k + i + 1] for j in range(4)] for i in range(4)]
    p0, p1, p2 = inverse_of_two(g[0][0], g[1][0], g[1][1])
    t02, t12 = p0 * g[2][0] + p1 * g[2][1], p1 * g[2][0] + p2 * g[2][1]
    t03, t13 = p0 * g[3][0] + p1 * g[3][1], p1 * g[3][0] + p2 * g[3][1]
    w0, w1, w2 = inverse_of_two(
        g[2][2] - g[2][0] * t02 - g[2][1] * t12,
        g[3][2] - g[3][0] * t02 - g[3][1] * t12,
        g[3][3] - g[3][0] * t03 - g[3][1] * t13,
    )

    def solve(array):
        r = [array[k + i : k + i + 1] for i in range(4)]
        u0, u1 = p0 * r[0] + p1 * r[1], p1 * r[0] + p2 * r[1]
        v2 = r[2] - t02 * r[0] - t12 * r[1]
        v3 = r[3] - t03 * r[0] - t13 * r[1]
        x2, x3 = w0 * v2 + w1 * v3, w1 * v2 + w2 * v3
        return u0 - t02 * x2 - t03 * x3, u1 - t12 * x2 - t13 * x3, x2, x3

    return solve


def eliminate(matrix, right, eye):
    n = matrix.shape[0]
    diagonal = jnp.where(eye, matrix, 0.0)
    unit = lax.rsqrt(jnp.sum(diagonal, axis=1, keepdims=True))
    unit_row = lax.rsqrt(jnp.sum(diagonal, axis=0, keepdims=True))
    both = jnp.concatenate([matrix * unit * unit_row, right * unit], axis=1)
    rows = lax.broadcasted_iota(jnp.int32, both.shape, 0)

    def spread(at):
        return [
            jnp.broadcast_to(both[:, at + j : at + j + 1], both.shape)
            for j in range(4 if at < n else 0)
        ]

    now, later = spread(0), spread(4)
    for k in range(0, n, 4):
        solve = solver_of_four(now, k)
        pivots = (rows >= k) & (rows < k + 4)
        c = [
            jnp.where(rows == k + j, -1.0, jnp.where(pivots, 0.0, now[j]))
            for j in range(4)
        ]

        def step(array):
            x = solve(array)
            rest = jnp.where(pivots, 0.0, array)
            return (rest - c[0] * x[0] - c[1] * x[1]) - (c[2] * x[2] + c[3] * x[3])

        now = [step(array) for array in later]
        both = step(both)
        later = spread(k + 8)
    return both[:, n:] * unit


def farthest_first(m, n):
    steps = [(i, j) for i in range(m) for j in range(n) if i or j]
    return sorted(steps, key=lambda s: -min(s[0], m - s[0]) - min(s[1], n - s[1]))


def davidson(
    nr,
    nc,
    l_hbm,
    e_hbm,
    v_hbm,
    tiles_ref,
    one_ref,
    two_ref,
    ray_ref,
    norms_ref,
    l_ref,
    e_ref,
    v_ref,
    block,
    own_t,
    slabs,
    gathered,
    v_send,
    v_recv,
    weights,
    split_all,
    basis,
    pair_send,
    pair_recv,
    image_send,
    image_recv,
    gram_pair_send,
    gram_pair_recv,
    gram_send,
    gram_recv,
    walk_send,
    walk_recv,
    norm_send,
    norm_recv,
    loads,
    sends,
    recvs,
    ring_sems,
):
    p = lax.axis_index("prow")
    q = lax.axis_index("pcol")
    z = p // 2
    core = p % 2
    nz = nr // 2
    wide = 64 * nc
    walkers = 32 * nc
    params = wide * nr

    def row_of(zz, cc):
        return lax.rem(zz + nz, nz) * 2 + cc

    sibling = z * 2 + 1 - core

    def push(src, dst, send_sem, recv_sem, device):
        pltpu.make_async_remote_copy(
            src_ref=src,
            dst_ref=dst,
            send_sem=send_sem,
            recv_sem=recv_sem,
            device_id=device,
            device_id_type=MESH,
        ).start()

    def sent(ref, sem):
        pltpu.make_async_remote_copy(
            src_ref=ref,
            dst_ref=ref,
            send_sem=sem,
            recv_sem=sem,
            device_id={"prow": sibling},
            device_id_type=MESH,
        ).wait_send()

    def landed(ref, sem):
        pltpu.make_async_remote_copy(
            src_ref=ref,
            dst_ref=ref,
            send_sem=sem,
            recv_sem=sem,
            device_id={"prow": sibling},
            device_id_type=MESH,
        ).wait_recv()

    barrier = pltpu.get_barrier_semaphore()

    nx = 4
    ny = nc // nx
    x, y = q % nx, q // nx

    def along_x(i):
        return y * nx + lax.rem(x + i, nx)

    def along_y(i):
        return lax.rem(y + i, ny) * nx + x

    plane = [
        lax.rem(y + j, ny) * nx + lax.rem(x + i, nx)
        for i, j in farthest_first(nx, ny)
    ]
    chips = [row_of(z + i, core) for i, _ in farthest_first(nz, 1)]
    rows = [
        row_of(z + i, lax.rem(core + j, 2)) for i, j in farthest_first(nz, 2)
    ]
    far_rows = len(rows) // 3
    for axis, members in (
        ("pcol", plane[: nc // 3]),
        ("prow", rows[:far_rows]),
        ("pcol", plane[nc // 3 :]),
        ("prow", rows[far_rows:]),
    ):
        for member in members:
            pl.semaphore_signal(
                barrier, inc=1, device_id={axis: member}, device_id_type=MESH
            )
    reads = [
        pltpu.make_async_copy(src, dst, loads.at[i])
        for i, (src, dst) in enumerate(((v_hbm, v_ref), (l_hbm, l_ref), (e_hbm, e_ref)))
    ]
    for read in reads:
        read.start()


    def to_plane(copy):
        for peer in plane:
            copy(peer)

    reads[0].wait()
    v_own = v_ref[...]
    v_send[...] = jnp.concatenate([v_own[:16], v_own[16:]], axis=1)
    v_recv[pl.ds(q, 1)] = v_send[...][None]
    reads[1].wait()
    reads[2].wait()
    l_own = l_ref[...]
    e_own = e_ref[...]
    for j in range(nc):
        slabs[j] = jnp.concatenate(
            [l_own[:, 64 * j : 64 * j + 64], e_own[:, 64 * j : 64 * j + 64]], axis=1
        )
    own_rows = pl.ds(pl.multiple_of(q * 32, 32), 32)
    gathered[pl.ds(p, 1), own_rows, :] = slabs[pl.ds(q, 1)]
    block[own_rows, :] = l_own
    weights[...] = jnp.concatenate([l_own, e_own], axis=0).T
    with scope("barrier"):
        pl.semaphore_wait(barrier, nc - 1 + nr - 1)
    to_plane(
        lambda peer: push(
            v_send, v_recv.at[q], sends.at[0], recvs.at[0], {"pcol": peer}
        )
    )
    def half_of(member, part):
        return block.at[pl.ds(pl.multiple_of(member * 32 + 16 * part, 16), 16)]

    def block_first():
        for i in range(1, nx):
            ref = half_of(q, 0)
            push(ref, ref, sends.at[2], recvs.at[2], {"pcol": along_x(i)})
        for i in range(1, ny):
            ref = half_of(q, 1)
            push(ref, ref, sends.at[10], recvs.at[10], {"pcol": along_y(i)})

    def block_second():
        landed(block.at[pl.ds(0, 16 * (nx - 1))], recvs.at[2])
        landed(block.at[pl.ds(0, 16 * (ny - 1))], recvs.at[10])

        def forward_y(i, carry):
            for k in range(nx):
                ref = half_of(along_x(k), 0)
                push(ref, ref, sends.at[11], recvs.at[11], {"pcol": along_y(i)})
            return carry

        def forward_x(i, carry):
            for k in range(ny):
                ref = half_of(along_y(k), 1)
                push(ref, ref, sends.at[12], recvs.at[12], {"pcol": along_x(i)})
            return carry

        lax.fori_loop(1, ny, forward_y, 0)
        lax.fori_loop(1, nx, forward_x, 0)

    counts = (nx - 1, ny - 1, nx * (ny - 1), ny * (nx - 1))

    def block_landed():
        for sem, count in zip((11, 12), counts[2:], strict=True):
            landed(block.at[pl.ds(0, 16 * count)], recvs.at[sem])

    def block_sent():
        for sem, count in zip((2, 10, 11, 12), counts, strict=True):
            sent(block.at[pl.ds(0, 16 * count)], sends.at[sem])

    block_first()
    to_plane(
        lambda peer: push(
            slabs.at[peer],
            gathered.at[p, own_rows],
            sends.at[1],
            recvs.at[1],
            {"pcol": peer},
        )
    )

    eye = lax.broadcasted_iota(jnp.int32, (32, 32), 0) == lax.broadcasted_iota(
        jnp.int32, (32, 32), 1
    )
    far = pl.ds(0, nc - 1)

    full = nz // 2 - 1
    half = walkers // 2
    everything, lower, upper = pl.ds(0, walkers), pl.ds(0, half), pl.ds(half, half)

    def part_of(way, step):
        return everything if step < full else (lower, upper)[way]

    def ring_start():
        landed(gathered.at[0, pl.ds(0, 32 * (nc - 1))], recvs.at[1])
        ring_send(0)
        own = gathered.at[p]
        push(
            own,
            own,
            ring_sems.at[2, 0, full + 1],
            ring_sems.at[3, 0, full + 1],
            {"prow": sibling},
        )

    def ring_send(step):
        for way, sign in ((0, 1), (1, -1)):
            ref = gathered.at[row_of(z - sign * step, core), part_of(way, step)]
            push(
                ref,
                ref,
                ring_sems.at[0, way, step],
                ring_sems.at[1, way, step],
                {"prow": row_of(z + sign, core)},
            )

    def ring_landed(step):
        for way, sign in ((0, 1), (1, -1)):
            ref = gathered.at[row_of(z - sign * (step + 1), core), part_of(way, step)]
            landed(ref, ring_sems.at[1, way, step])
            push(
                ref,
                ref,
                ring_sems.at[2, way, step],
                ring_sems.at[3, way, step],
                {"prow": sibling},
            )

    def ring_advance(step):
        if step <= full:
            ring_landed(step)
        if step < full:
            ring_send(step + 1)

    def sibling_landed(step):
        for way, sign in ((0, 1), (1, -1)):
            chunk = row_of(z - sign * (step + 1), 1 - core)
            landed(gathered.at[chunk, part_of(way, step)], ring_sems.at[3, way, step])

    def ring_sent():
        sent(gathered.at[p], ring_sems.at[2, 0, full + 1])
        for step in range(full + 1):
            for way in range(2):
                ref = gathered.at[p, part_of(way, step)]
                sent(ref, ring_sems.at[0, way, step])
                sent(ref, ring_sems.at[2, way, step])

    def multiply(chunk):
        a = gathered[pl.ds(2 * chunk, 1)][0]
        b = gathered[pl.ds(2 * chunk + 1, 1)][0]
        right = jnp.concatenate(
            [a[:, :64], b[:, :64], a[:, 64:], b[:, 64:]], axis=1
        )
        out = jnp.dot(own_t[...], right, preferred_element_type=F32) * (1.0 / walkers)
        columns = pl.ds(pl.multiple_of(chunk * 128, 128), 128)
        tiles_ref[0, :, columns] = out[:, :128]
        tiles_ref[1, :, columns] = out[:, 128:]

    def multiply_own():
        own_t[...] = block[...].T
        landed(gathered.at[sibling], ring_sems.at[3, 0, full + 1])
        multiply(z)
        row = lax.broadcasted_iota(jnp.int32, (64, 128), 0)
        column = lax.broadcasted_iota(jnp.int32, (64, 128), 1)
        mine = pl.ds(pl.multiple_of(q * 64, 64), 64)
        columns = pl.ds(pl.multiple_of(z * 128, 128), 128)
        tiles_ref[0, mine, columns] += jnp.where(
            column == row + core * 64, STABILIZER, 0.0
        )

    def multiply_step(step):
        if step > full:
            return
        sibling_landed(step)

        def body(way, carry):
            multiply(lax.rem(z + (2 * way - 1) * (step + 1) + nz, nz))
            return carry

        lax.fori_loop(0, 2 if step < full else 1, body, 0)

    def both_cores(src, dst, turn, sem):
        push(
            src.at[turn],
            dst.at[turn],
            sends.at[sem + turn],
            recvs.at[sem + turn],
            {"prow": sibling},
        )

    def along_z(src, dst, turn, sem):
        for chip in chips:
            push(
                src.at[turn],
                dst.at[turn, z],
                sends.at[sem + turn],
                recvs.at[sem + turn],
                {"prow": chip},
            )

    def image_start(vec, turn):
        with scope("values"):
            split = pieces(vec)
            out = sum_rows(jnp.dot(split, weights[...], preferred_element_type=F32), 32)
            pair_send[turn] = jnp.concatenate(
                [fold(out[:, :32]), fold(out[:, 32:])], axis=0
            )
        both_cores(pair_send, pair_recv, turn, 4)
        if turn == 0:
            with scope("block_second"):
                block_second()
        with scope("wait_pair"):
            landed(pair_recv.at[turn], recvs.at[4 + turn])
        with scope("pair_sum"):
            mine = pair_send[turn] + pair_recv[turn]
            image_send[turn] = mine
            image_recv[turn, pl.ds(z, 1)] = mine[None]
        along_z(image_send, image_recv, turn, 6)
        if turn == 1:
            sent(v_recv.at[far], sends.at[0])
        with scope("gram"):
            split_all[...] = split
            out = lax.dot_general(
                split, split_all[...], NT, preferred_element_type=F32
            )
            out = sum_rows(out, 32)
            gram_pair_send[turn] = fold(out[:, :32] + out[:, 32:64] + out[:, 64:])
        both_cores(gram_pair_send, gram_pair_recv, turn, 15)

    def gram_start(turn):
        landed(gram_pair_recv.at[turn], recvs.at[15 + turn])
        mine = gram_pair_send[turn] + gram_pair_recv[turn]
        gram_send[turn] = mine
        gram_recv[turn, pl.ds(z, 1)] = mine[None]
        along_z(gram_send, gram_recv, turn, 13)

    def walk_start(turn):
        with scope("wait_image"):
            landed(image_recv.at[turn, pl.ds(0, nz - 1)], recvs.at[6 + turn])
        with scope("image_sum"):
            mine = jnp.sum(image_recv[turn], axis=0)
            walk_send[turn] = mine
        walk_recv[turn, pl.ds(q, 1)] = mine[None]
        to_plane(
            lambda peer: push(
                walk_send.at[turn],
                walk_recv.at[turn, q],
                sends.at[8 + turn],
                recvs.at[8 + turn],
                {"pcol": peer},
            )
        )

    def gram_landed(turn):
        landed(gram_recv.at[turn, pl.ds(0, nz - 1)], recvs.at[13 + turn])
        return unfold([jnp.sum(gram_recv[turn], axis=0)])

    def walk_landed(turn):
        with scope("wait_walk"):
            landed(walk_recv.at[turn, far], recvs.at[8 + turn])
        return [
            jnp.concatenate(
                [
                    unfold([walk_recv[turn, k + j, rows] for j in range(4)])
                    for k in range(0, nc, 4)
                ],
                axis=1,
            )
            for rows in (slice(0, 8), slice(8, 16))
        ]

    def residual(vec, l_val, e_val, gram, inverse_diag):
        with scope("products"):
            l_split = pieces(l_val)
            both = jnp.concatenate([l_split, pieces(e_val)], axis=0)
            out = sum_rows(
                lax.dot_general(l_split, both, NT, preferred_element_type=F32), 32
            )
        ray_s = out[:, :32] + out[:, 32:64] + out[:, 64:96]
        ray_h = out[:, 96:128] + out[:, 128:160] + out[:, 160:192]
        with scope("images"):
            image = jnp.dot(both, block[...], preferred_element_type=F32)
            image_s = sum_rows(image[:96], 32) * (1.0 / walkers) + STABILIZER * vec
            image_h = sum_rows(image[96:], 32) * (1.0 / walkers) * inverse_diag
            s = pieces(image_s * inverse_diag)
            right = jnp.concatenate(
                [s[:32], s[32:64], s[:32], s[64:], s[32:64], s[:32]], axis=0
            )
        with scope("eliminate"):
            coeffs = eliminate(
                ray_s * (1.0 / walkers) + STABILIZER * gram,
                ray_h * (1.0 / walkers),
                eye,
            )
        with scope("mix"):
            c = pieces(coeffs)
            left = jnp.concatenate(
                [c[:32], c[:32], c[32:64], c[:32], c[32:64], c[64:]], axis=0
            )
            out = lax.dot_general(left, right, TN, preferred_element_type=F32)
            result = image_h - out
        return result, coeffs

    def own_part(vec):
        for k in range(nc // 2):
            basis[k] = vec[:, 128 * k : 128 * k + 128]
        chunk = basis[pl.ds(q // 2, 1)][0]
        return jnp.where(q % 2 == 0, chunk[:, :64], chunk[:, 64:])

    with scope("wait_v"):
        landed(v_recv.at[far], recvs.at[0])
    top, bottom = [], []
    for k in range(0, nc, 2):
        a, b = v_recv[k], v_recv[k + 1]
        top += [a[:, :64], b[:, :64]]
        bottom += [a[:, 64:], b[:, 64:]]
    vec = jnp.concatenate(
        [jnp.concatenate(top, axis=1), jnp.concatenate(bottom, axis=1)], axis=0
    )
    image_start(vec, 0)
    with scope("ring_start"):
        ring_start()
    gram_start(0)
    walk_start(0)
    with scope("wait_block"):
        block_landed()
    squares = jnp.zeros((8, wide), F32)
    for k in range(0, walkers, 16):
        part = block[k : k + 16].astype(F32)
        part = part * part
        squares = squares + part[:8] + part[8:]
    inverse_diag = 1.0 / (
        jnp.sum(squares, axis=0, keepdims=True) * (1.0 / walkers) + STABILIZER
    )
    gram = gram_landed(0)
    with scope("ring_0"):
        ring_advance(0)
    l_val, e_val = walk_landed(0)
    vec, _ = residual(vec, l_val, e_val, gram, inverse_diag * ENLARGED)

    image_start(vec, 1)
    with scope("ring_1"):
        ring_advance(1)
    gram_start(1)
    with scope("tiles_a"):
        multiply_own()
    walk_start(1)
    with scope("tiles_b"):
        multiply_step(0)
    with scope("ring_2"):
        ring_advance(2)
    gram = gram_landed(1)
    norms = jnp.sum(jnp.where(eye, gram, 0.0), axis=1, keepdims=True)
    norms = norms * (1.0 / ENLARGED) * (1.0 / ENLARGED)
    scale = (1.0 / ENLARGED) / jnp.sqrt(norms * (1.0 / params) + EPSILON)
    gram = gram * scale * to_row(scale, eye)
    vec = vec * scale
    one_ref[...] = own_part(vec)
    l_val, e_val = walk_landed(1)
    vec, coeffs = residual(vec, l_val * scale, e_val * scale, gram, inverse_diag)
    norms = to_row(jnp.sum(vec * vec, axis=1, keepdims=True), eye)
    norm_send[...] = jnp.concatenate([norms, jnp.zeros((1, 96), F32)], axis=1)
    norm_recv[pl.ds(p, 1)] = norm_send[...][None]

    for row in rows:
        push(norm_send, norm_recv.at[p], sends.at[3], recvs.at[3], {"prow": row})
    block_sent()
    ray_ref[...] = coeffs
    two_ref[...] = own_part(vec)
    with scope("tiles_c"):
        multiply_step(1)
        multiply_step(2)
    with scope("ring_3"):
        ring_advance(3)
    with scope("tiles_d"):
        multiply_step(3)
    ring_sent()
    sent(gathered.at[0, pl.ds(0, 32 * (nc - 1))], sends.at[1])
    for turn in range(2):
        sent(pair_send.at[turn], sends.at[4 + turn])
        sent(gram_pair_send.at[turn], sends.at[15 + turn])
        sent(image_recv.at[turn, pl.ds(0, nz - 1)], sends.at[6 + turn])
        sent(gram_recv.at[turn, pl.ds(0, nz - 1)], sends.at[13 + turn])
        sent(walk_recv.at[turn, far], sends.at[8 + turn])
    with scope("wait_norm"):
        landed(norm_recv.at[pl.ds(0, nr - 1)], recvs.at[3])
    norms_ref[...] = jnp.sum(norm_recv[...], axis=0)
    sent(norm_recv.at[pl.ds(0, nr - 1)], sends.at[3])


def write(
    params,
    tiles,
    one,
    two,
    ray,
    norms,
    corr_ref,
    ham_ref,
    one_ref,
    two_ref,
    ray_ref,
    scaled,
    sems,
):
    rows = tiles.shape[1] // 4
    pairs = []
    for k in range(4):
        part = pl.ds(k * rows, rows)
        pairs.append((tiles.at[0, part], corr_ref.at[0, part]))
        pairs.append((tiles.at[1, part], ham_ref.at[0, part]))
    pairs += [(one, one_ref), (ray, ray_ref), (scaled, two_ref)]
    writes = [
        pltpu.make_async_copy(src, dst, sems.at[i])
        for i, (src, dst) in enumerate(pairs)
    ]
    for copy in writes[:-1]:
        copy.start()
    eye = lax.broadcasted_iota(jnp.int32, (32, 32), 0) == lax.broadcasted_iota(
        jnp.int32, (32, 32), 1
    )
    squares = to_column(norms[:, :32], eye)
    scaled[...] = two[...] * (1.0 / jnp.sqrt(squares * (1.0 / params) + EPSILON))
    writes[-1].start()
    for copy in writes:
        copy.wait()


def local(nr, nc, log_derivs, energy_derivs, start_block):
    wide, walkers, narrow = 64 * nc, 32 * nc, 64 * nr
    nz = nr // 2
    vmem = pl.BlockSpec(memory_space=pltpu.VMEM)
    full = nz // 2 - 1
    hbm = pl.BlockSpec(memory_space=pltpu.HBM)
    small = (
        jax.ShapeDtypeStruct((32, 64), F32),
        jax.ShapeDtypeStruct((32, 64), F32),
        jax.ShapeDtypeStruct((32, 32), F32),
    )
    arguments = (log_derivs, energy_derivs, start_block.T)
    results = pl.pallas_call(
        functools.partial(davidson, nr, nc),
        out_shape=(
            pltpu.VMEM((2, wide, narrow), F32),
            *(pltpu.VMEM(x.shape, F32) for x in small),
            pltpu.VMEM((1, 128), F32),
        ),
        in_specs=[hbm] * 3,
        out_specs=(vmem,) * 5,
        scratch_shapes=[
            pltpu.VMEM((32, wide), BF16),
            pltpu.VMEM((32, wide), BF16),
            pltpu.VMEM((32, 64), F32),
            pltpu.VMEM((walkers, wide), BF16),
            pltpu.VMEM((wide, walkers), BF16),
            pltpu.VMEM((nc, 32, 128), BF16),
            pltpu.VMEM((nr, walkers, 128), BF16),
            pltpu.VMEM((16, 128), F32),
            pltpu.VMEM((nc, 16, 128), F32),
            pltpu.VMEM((wide, 64), BF16),
            pltpu.VMEM((96, wide), BF16),
            pltpu.VMEM((nc // 2, 32, 128), F32),
            pltpu.VMEM((2, 16, 128), F32),
            pltpu.VMEM((2, 16, 128), F32),
            pltpu.VMEM((2, 16, 128), F32),
            pltpu.VMEM((2, nz, 16, 128), F32),
            pltpu.VMEM((2, 8, 128), F32),
            pltpu.VMEM((2, 8, 128), F32),
            pltpu.VMEM((2, 8, 128), F32),
            pltpu.VMEM((2, nz, 8, 128), F32),
            pltpu.VMEM((2, 16, 128), F32),
            pltpu.VMEM((2, nc, 16, 128), F32),
            pltpu.VMEM((1, 128), F32),
            pltpu.VMEM((nr, 1, 128), F32),
            pltpu.SemaphoreType.DMA((3,)),
            pltpu.SemaphoreType.DMA((17,)),
            pltpu.SemaphoreType.DMA((17,)),
            pltpu.SemaphoreType.DMA((4, 2, full + 2)),
        ],
        compiler_params=pltpu.CompilerParams(
            collective_id=0, has_side_effects=True, vmem_limit_bytes=24 * 1024 * 1024
        ),
        name="davidson",
    )(*(pltpu.with_memory_space_constraint(x, pltpu.HBM) for x in arguments))

    corr, ham, one, two, ray = pl.pallas_call(
        functools.partial(write, 64 * nc * nr),
        out_shape=(
            jax.ShapeDtypeStruct((1, wide, narrow), F32),
            jax.ShapeDtypeStruct((1, wide, narrow), F32),
            *small,
        ),
        in_specs=[vmem] * 5,
        out_specs=(hbm,) * 5,
        scratch_shapes=[pltpu.VMEM((32, 64), F32), pltpu.SemaphoreType.DMA((11,))],
        compiler_params=pltpu.CompilerParams(vmem_limit_bytes=24 * 1024 * 1024),
        name="tiles",
    )(*(pltpu.with_memory_space_constraint(x, pltpu.VMEM) for x in results))
    return one.T, two.T, ray, corr, ham


def solution(mesh):
    return jax.shard_map(
        functools.partial(local, mesh.shape["prow"], mesh.shape["pcol"]),
        mesh=mesh,
        in_specs=(P("pcol", "prow"), P("pcol", "prow"), P(("prow", "pcol"), None)),
        out_specs=(
            P(("prow", "pcol"), None),
            P(("prow", "pcol"), None),
            P(),
            P("pcol", "prow", None),
            P("pcol", "prow", None),
        ),
        check_vma=False,
    )
```

```python
import contextlib
import functools

import jax
import jax.numpy as jnp
from jax import lax
from jax.experimental import pallas as pl
from jax.experimental.pallas import tpu as pltpu
from jax.sharding import PartitionSpec as P

STABILIZER = 0.5
EPSILON = 1e-6
ENLARGED = 2.0**30
F32 = jnp.float32
BF16 = jnp.bfloat16
HIGHEST = lax.Precision.HIGHEST
MESH = pl.DeviceIdType.MESH
NT = (((1,), (1,)), ((), ()))
TN = (((0,), (0,)), ((), ()))


def scope(name):
    return contextlib.nullcontext()


def pieces(x):
    high = x.astype(BF16)
    rest = x - high.astype(F32)
    middle = rest.astype(BF16)
    low = (rest - middle.astype(F32)).astype(BF16)
    return jnp.concatenate([high, middle, low], axis=0)


def sum_rows(x, n):
    return x[:n] + x[n : 2 * n] + x[2 * n : 3 * n]


def to_row(column, eye):
    return jnp.sum(jnp.where(eye, column, 0.0), axis=0, keepdims=True)


def to_column(row, eye):
    return jnp.sum(jnp.where(eye, row, 0.0), axis=1, keepdims=True)


def fold(x):
    return jnp.concatenate([x[8 * g : 8 * g + 8] for g in range(4)], axis=1)


def unfold(folded):
    return jnp.concatenate(
        [
            jnp.concatenate([x[:, 32 * g : 32 * g + 32] for x in folded], axis=1)
            for g in range(4)
        ],
        axis=0,
    )


def inverse_of_two(a, b, d):
    scale = 1.0 / (a * d - b * b)
    return d * scale, -b * scale, a * scale


def solver_of_four(columns, k):
    g = [[columns[j][k + i : k + i + 1] for j in range(4)] for i in range(4)]
    p0, p1, p2 = inverse_of_two(g[0][0], g[1][0], g[1][1])
    t02, t12 = p0 * g[2][0] + p1 * g[2][1], p1 * g[2][0] + p2 * g[2][1]
    t03, t13 = p0 * g[3][0] + p1 * g[3][1], p1 * g[3][0] + p2 * g[3][1]
    w0, w1, w2 = inverse_of_two(
        g[2][2] - g[2][0] * t02 - g[2][1] * t12,
        g[3][2] - g[3][0] * t02 - g[3][1] * t12,
        g[3][3] - g[3][0] * t03 - g[3][1] * t13,
    )

    def solve(array):
        r = [array[k + i : k + i + 1] for i in range(4)]
        u0, u1 = p0 * r[0] + p1 * r[1], p1 * r[0] + p2 * r[1]
        v2 = r[2] - t02 * r[0] - t12 * r[1]
        v3 = r[3] - t03 * r[0] - t13 * r[1]
        x2, x3 = w0 * v2 + w1 * v3, w1 * v2 + w2 * v3
        return u0 - t02 * x2 - t03 * x3, u1 - t12 * x2 - t13 * x3, x2, x3

    return solve


def eliminate(matrix, right, eye):
    n = matrix.shape[0]
    diagonal = jnp.where(eye, matrix, 0.0)
    unit = lax.rsqrt(jnp.sum(diagonal, axis=1, keepdims=True))
    unit_row = lax.rsqrt(jnp.sum(diagonal, axis=0, keepdims=True))
    both = jnp.concatenate([matrix * unit * unit_row, right * unit], axis=1)
    rows = lax.broadcasted_iota(jnp.int32, both.shape, 0)

    def spread(at):
        return [
            jnp.broadcast_to(both[:, at + j : at + j + 1], both.shape)
            for j in range(4 if at < n else 0)
        ]

    now, later = spread(0), spread(4)
    for k in range(0, n, 4):
        solve = solver_of_four(now, k)
        pivots = (rows >= k) & (rows < k + 4)
        c = [
            jnp.where(rows == k + j, -1.0, jnp.where(pivots, 0.0, now[j]))
            for j in range(4)
        ]

        def step(array):
            x = solve(array)
            rest = jnp.where(pivots, 0.0, array)
            return (rest - c[0] * x[0] - c[1] * x[1]) - (c[2] * x[2] + c[3] * x[3])

        now = [step(array) for array in later]
        both = step(both)
        later = spread(k + 8)
    return both[:, n:] * unit


def farthest_first(m, n):
    steps = [(i, j) for i in range(m) for j in range(n) if i or j]
    return sorted(steps, key=lambda s: -min(s[0], m - s[0]) - min(s[1], n - s[1]))


def davidson(
    nr,
    nc,
    l_hbm,
    e_hbm,
    v_hbm,
    tiles_ref,
    one_ref,
    two_ref,
    ray_ref,
    norms_ref,
    l_ref,
    e_ref,
    v_ref,
    block,
    own_t,
    slabs,
    gathered,
    v_send,
    v_recv,
    weights,
    split_all,
    basis,
    pair_send,
    pair_recv,
    image_send,
    image_recv,
    gram_pair_send,
    gram_pair_recv,
    gram_send,
    gram_recv,
    walk_send,
    walk_recv,
    norm_send,
    norm_recv,
    loads,
    sends,
    recvs,
    ring_sems,
):
    p = lax.axis_index("prow")
    q = lax.axis_index("pcol")
    z = p // 2
    core = p % 2
    nz = nr // 2
    wide = 64 * nc
    walkers = 32 * nc
    params = wide * nr

    def row_of(zz, cc):
        return lax.rem(zz + nz, nz) * 2 + cc

    sibling = z * 2 + 1 - core

    def push(src, dst, send_sem, recv_sem, device):
        pltpu.make_async_remote_copy(
            src_ref=src,
            dst_ref=dst,
            send_sem=send_sem,
            recv_sem=recv_sem,
            device_id=device,
            device_id_type=MESH,
        ).start()

    def sent(ref, sem):
        pltpu.make_async_remote_copy(
            src_ref=ref,
            dst_ref=ref,
            send_sem=sem,
            recv_sem=sem,
            device_id={"prow": sibling},
            device_id_type=MESH,
        ).wait_send()

    def landed(ref, sem):
        pltpu.make_async_remote_copy(
            src_ref=ref,
            dst_ref=ref,
            send_sem=sem,
            recv_sem=sem,
            device_id={"prow": sibling},
            device_id_type=MESH,
        ).wait_recv()

    barrier = pltpu.get_barrier_semaphore()

    nx = 4
    ny = nc // nx
    x, y = q % nx, q // nx

    def along_x(i):
        return y * nx + lax.rem(x + i, nx)

    def along_y(i):
        return lax.rem(y + i, ny) * nx + x

    plane = [
        lax.rem(y + j, ny) * nx + lax.rem(x + i, nx)
        for i, j in farthest_first(nx, ny)
    ]
    chips = [row_of(z + i, core) for i, _ in farthest_first(nz, 1)]
    rows = [
        row_of(z + i, lax.rem(core + j, 2)) for i, j in farthest_first(nz, 2)
    ]
    far_rows = len(rows) // 3
    for axis, members in (
        ("pcol", plane[: nc // 3]),
        ("prow", rows[:far_rows]),
        ("pcol", plane[nc // 3 :]),
        ("prow", rows[far_rows:]),
    ):
        for member in members:
            pl.semaphore_signal(
                barrier, inc=1, device_id={axis: member}, device_id_type=MESH
            )
    reads = [
        pltpu.make_async_copy(src, dst, loads.at[i])
        for i, (src, dst) in enumerate(((v_hbm, v_ref), (l_hbm, l_ref), (e_hbm, e_ref)))
    ]
    for read in reads:
        read.start()


    def to_plane(copy):
        for peer in plane:
            copy(peer)

    reads[0].wait()
    v_own = v_ref[...]
    v_send[...] = jnp.concatenate([v_own[:16], v_own[16:]], axis=1)
    v_recv[pl.ds(q, 1)] = v_send[...][None]
    reads[1].wait()
    reads[2].wait()
    l_own = l_ref[...]
    e_own = e_ref[...]
    for j in range(nc):
        slabs[j] = jnp.concatenate(
            [l_own[:, 64 * j : 64 * j + 64], e_own[:, 64 * j : 64 * j + 64]], axis=1
        )
    own_rows = pl.ds(pl.multiple_of(q * 32, 32), 32)
    gathered[pl.ds(p, 1), own_rows, :] = slabs[pl.ds(q, 1)]
    block[own_rows, :] = l_own
    weights[...] = jnp.concatenate([l_own, e_own], axis=0).T
    with scope("barrier"):
        pl.semaphore_wait(barrier, nc - 1 + nr - 1)
    to_plane(
        lambda peer: push(
            v_send, v_recv.at[q], sends.at[0], recvs.at[0], {"pcol": peer}
        )
    )
    def half_of(member, part):
        return block.at[pl.ds(pl.multiple_of(member * 32 + 16 * part, 16), 16)]

    def block_first():
        for i in range(1, nx):
            ref = half_of(q, 0)
            push(ref, ref, sends.at[2], recvs.at[2], {"pcol": along_x(i)})
        for i in range(1, ny):
            ref = half_of(q, 1)
            push(ref, ref, sends.at[10], recvs.at[10], {"pcol": along_y(i)})

    def block_second():
        landed(block.at[pl.ds(0, 16 * (nx - 1))], recvs.at[2])
        landed(block.at[pl.ds(0, 16 * (ny - 1))], recvs.at[10])

        for i, _ in farthest_first(ny, 1):
            for k in range(nx):
                ref = half_of(along_x(k), 0)
                push(ref, ref, sends.at[11], recvs.at[11], {"pcol": along_y(i)})
        for i, _ in farthest_first(nx, 1):
            for k in range(ny):
                ref = half_of(along_y(k), 1)
                push(ref, ref, sends.at[12], recvs.at[12], {"pcol": along_x(i)})

    counts = (nx - 1, ny - 1, nx * (ny - 1), ny * (nx - 1))

    def block_landed():
        for sem, count in zip((11, 12), counts[2:], strict=True):
            landed(block.at[pl.ds(0, 16 * count)], recvs.at[sem])

    def block_sent():
        for sem, count in zip((2, 10, 11, 12), counts, strict=True):
            sent(block.at[pl.ds(0, 16 * count)], sends.at[sem])

    block_first()
    to_plane(
        lambda peer: push(
            slabs.at[peer],
            gathered.at[p, own_rows],
            sends.at[1],
            recvs.at[1],
            {"pcol": peer},
        )
    )

    eye = lax.broadcasted_iota(jnp.int32, (32, 32), 0) == lax.broadcasted_iota(
        jnp.int32, (32, 32), 1
    )
    far = pl.ds(0, nc - 1)

    full = nz // 2 - 1
    half = walkers // 2
    everything, lower, upper = pl.ds(0, walkers), pl.ds(0, half), pl.ds(half, half)

    def part_of(way, step):
        return everything if step < full else (lower, upper)[way]

    def ring_start():
        landed(gathered.at[0, pl.ds(0, 32 * (nc - 1))], recvs.at[1])
        ring_send(0)
        own = gathered.at[p]
        push(
            own,
            own,
            ring_sems.at[2, 0, full + 1],
            ring_sems.at[3, 0, full + 1],
            {"prow": sibling},
        )

    def ring_send(step):
        for way, sign in ((0, 1), (1, -1)):
            ref = gathered.at[row_of(z - sign * step, core), part_of(way, step)]
            push(
                ref,
                ref,
                ring_sems.at[0, way, step],
                ring_sems.at[1, way, step],
                {"prow": row_of(z + sign, core)},
            )

    def ring_landed(step):
        for way, sign in ((0, 1), (1, -1)):
            ref = gathered.at[row_of(z - sign * (step + 1), core), part_of(way, step)]
            landed(ref, ring_sems.at[1, way, step])
            push(
                ref,
                ref,
                ring_sems.at[2, way, step],
                ring_sems.at[3, way, step],
                {"prow": sibling},
            )

    def ring_advance(step):
        if step <= full:
            ring_landed(step)
        if step < full:
            ring_send(step + 1)

    def sibling_landed(step):
        for way, sign in ((0, 1), (1, -1)):
            chunk = row_of(z - sign * (step + 1), 1 - core)
            landed(gathered.at[chunk, part_of(way, step)], ring_sems.at[3, way, step])

    def ring_sent():
        sent(gathered.at[p], ring_sems.at[2, 0, full + 1])
        for step in range(full + 1):
            for way in range(2):
                ref = gathered.at[p, part_of(way, step)]
                sent(ref, ring_sems.at[0, way, step])
                sent(ref, ring_sems.at[2, way, step])

    def multiply(chunk):
        a = gathered[pl.ds(2 * chunk, 1)][0]
        b = gathered[pl.ds(2 * chunk + 1, 1)][0]
        right = jnp.concatenate(
            [a[:, :64], b[:, :64], a[:, 64:], b[:, 64:]], axis=1
        )
        out = jnp.dot(own_t[...], right, preferred_element_type=F32) * (1.0 / walkers)
        columns = pl.ds(pl.multiple_of(chunk * 128, 128), 128)
        tiles_ref[0, :, columns] = out[:, :128]
        tiles_ref[1, :, columns] = out[:, 128:]

    def multiply_own():
        own_t[...] = block[...].T
        landed(gathered.at[sibling], ring_sems.at[3, 0, full + 1])
        multiply(z)
        row = lax.broadcasted_iota(jnp.int32, (64, 128), 0)
        column = lax.broadcasted_iota(jnp.int32, (64, 128), 1)
        mine = pl.ds(pl.multiple_of(q * 64, 64), 64)
        columns = pl.ds(pl.multiple_of(z * 128, 128), 128)
        tiles_ref[0, mine, columns] += jnp.where(
            column == row + core * 64, STABILIZER, 0.0
        )

    def multiply_step(step):
        if step > full:
            return
        sibling_landed(step)

        def body(way, carry):
            multiply(lax.rem(z + (2 * way - 1) * (step + 1) + nz, nz))
            return carry

        lax.fori_loop(0, 2 if step < full else 1, body, 0)

    def both_cores(src, dst, turn, sem):
        push(
            src.at[turn],
            dst.at[turn],
            sends.at[sem + turn],
            recvs.at[sem + turn],
            {"prow": sibling},
        )

    def along_z(src, dst, turn, sem):
        for chip in chips:
            push(
                src.at[turn],
                dst.at[turn, z],
                sends.at[sem + turn],
                recvs.at[sem + turn],
                {"prow": chip},
            )

    def image_start(vec, turn):
        with scope("values"):
            split = pieces(vec)
            out = sum_rows(jnp.dot(split, weights[...], preferred_element_type=F32), 32)
            pair_send[turn] = jnp.concatenate(
                [fold(out[:, :32]), fold(out[:, 32:])], axis=0
            )
        both_cores(pair_send, pair_recv, turn, 4)
        if turn == 0:
            with scope("block_second"):
                block_second()
        with scope("wait_pair"):
            landed(pair_recv.at[turn], recvs.at[4 + turn])
        with scope("pair_sum"):
            mine = pair_send[turn] + pair_recv[turn]
            image_send[turn] = mine
            image_recv[turn, pl.ds(z, 1)] = mine[None]
        along_z(image_send, image_recv, turn, 6)
        if turn == 1:
            sent(v_recv.at[far], sends.at[0])
        with scope("gram"):
            split_all[...] = split
            out = lax.dot_general(
                split, split_all[...], NT, preferred_element_type=F32
            )
            out = sum_rows(out, 32)
            gram_pair_send[turn] = fold(out[:, :32] + out[:, 32:64] + out[:, 64:])
        both_cores(gram_pair_send, gram_pair_recv, turn, 15)

    def gram_start(turn):
        landed(gram_pair_recv.at[turn], recvs.at[15 + turn])
        mine = gram_pair_send[turn] + gram_pair_recv[turn]
        gram_send[turn] = mine
        gram_recv[turn, pl.ds(z, 1)] = mine[None]
        along_z(gram_send, gram_recv, turn, 13)

    def walk_start(turn):
        with scope("wait_image"):
            landed(image_recv.at[turn, pl.ds(0, nz - 1)], recvs.at[6 + turn])
        with scope("image_sum"):
            mine = jnp.sum(image_recv[turn], axis=0)
            walk_send[turn] = mine
        walk_recv[turn, pl.ds(q, 1)] = mine[None]
        to_plane(
            lambda peer: push(
                walk_send.at[turn],
                walk_recv.at[turn, q],
                sends.at[8 + turn],
                recvs.at[8 + turn],
                {"pcol": peer},
            )
        )

    def gram_landed(turn):
        landed(gram_recv.at[turn, pl.ds(0, nz - 1)], recvs.at[13 + turn])
        return unfold([jnp.sum(gram_recv[turn], axis=0)])

    def walk_landed(turn):
        with scope("wait_walk"):
            landed(walk_recv.at[turn, far], recvs.at[8 + turn])
        return [
            jnp.concatenate(
                [
                    unfold([walk_recv[turn, k + j, rows] for j in range(4)])
                    for k in range(0, nc, 4)
                ],
                axis=1,
            )
            for rows in (slice(0, 8), slice(8, 16))
        ]

    def residual(vec, l_val, e_val, gram, inverse_diag):
        with scope("products"):
            l_split = pieces(l_val)
            both = jnp.concatenate([l_split, pieces(e_val)], axis=0)
            out = sum_rows(
                lax.dot_general(l_split, both, NT, preferred_element_type=F32), 32
            )
        ray_s = out[:, :32] + out[:, 32:64] + out[:, 64:96]
        ray_h = out[:, 96:128] + out[:, 128:160] + out[:, 160:192]
        with scope("images"):
            image = jnp.dot(both, block[...], preferred_element_type=F32)
            image_s = sum_rows(image[:96], 32) * (1.0 / walkers) + STABILIZER * vec
            image_h = sum_rows(image[96:], 32) * (1.0 / walkers) * inverse_diag
            s = pieces(image_s * inverse_diag)
            right = jnp.concatenate(
                [s[:32], s[32:64], s[:32], s[64:], s[32:64], s[:32]], axis=0
            )
        with scope("eliminate"):
            coeffs = eliminate(
                ray_s * (1.0 / walkers) + STABILIZER * gram,
                ray_h * (1.0 / walkers),
                eye,
            )
        with scope("mix"):
            c = pieces(coeffs)
            left = jnp.concatenate(
                [c[:32], c[:32], c[32:64], c[:32], c[32:64], c[64:]], axis=0
            )
            out = lax.dot_general(left, right, TN, preferred_element_type=F32)
            result = image_h - out
        return result, coeffs

    def own_part(vec):
        for k in range(nc // 2):
            basis[k] = vec[:, 128 * k : 128 * k + 128]
        chunk = basis[pl.ds(q // 2, 1)][0]
        return jnp.where(q % 2 == 0, chunk[:, :64], chunk[:, 64:])

    with scope("wait_v"):
        landed(v_recv.at[far], recvs.at[0])
    top, bottom = [], []
    for k in range(0, nc, 2):
        a, b = v_recv[k], v_recv[k + 1]
        top += [a[:, :64], b[:, :64]]
        bottom += [a[:, 64:], b[:, 64:]]
    vec = jnp.concatenate(
        [jnp.concatenate(top, axis=1), jnp.concatenate(bottom, axis=1)], axis=0
    )
    image_start(vec, 0)
    with scope("ring_start"):
        ring_start()
    gram_start(0)
    walk_start(0)
    with scope("wait_block"):
        block_landed()
    squares = jnp.zeros((8, wide), F32)
    for k in range(0, walkers, 16):
        part = block[k : k + 16].astype(F32)
        part = part * part
        squares = squares + part[:8] + part[8:]
    inverse_diag = 1.0 / (
        jnp.sum(squares, axis=0, keepdims=True) * (1.0 / walkers) + STABILIZER
    )
    gram = gram_landed(0)
    with scope("ring_0"):
        ring_advance(0)
    l_val, e_val = walk_landed(0)
    vec, _ = residual(vec, l_val, e_val, gram, inverse_diag * ENLARGED)

    image_start(vec, 1)
    with scope("ring_1"):
        ring_advance(1)
    gram_start(1)
    with scope("tiles_a"):
        multiply_own()
    walk_start(1)
    with scope("tiles_b"):
        multiply_step(0)
    with scope("ring_2"):
        ring_advance(2)
    gram = gram_landed(1)
    norms = jnp.sum(jnp.where(eye, gram, 0.0), axis=1, keepdims=True)
    norms = norms * (1.0 / ENLARGED) * (1.0 / ENLARGED)
    scale = (1.0 / ENLARGED) / jnp.sqrt(norms * (1.0 / params) + EPSILON)
    gram = gram * scale * to_row(scale, eye)
    vec = vec * scale
    one_ref[...] = own_part(vec)
    l_val, e_val = walk_landed(1)
    vec, coeffs = residual(vec, l_val * scale, e_val * scale, gram, inverse_diag)
    norms = to_row(jnp.sum(vec * vec, axis=1, keepdims=True), eye)
    norm_send[...] = jnp.concatenate([norms, jnp.zeros((1, 96), F32)], axis=1)
    norm_recv[pl.ds(p, 1)] = norm_send[...][None]

    for row in rows:
        push(norm_send, norm_recv.at[p], sends.at[3], recvs.at[3], {"prow": row})
    block_sent()
    ray_ref[...] = coeffs
    two_ref[...] = own_part(vec)
    with scope("tiles_c"):
        multiply_step(1)
        multiply_step(2)
    with scope("ring_3"):
        ring_advance(3)
    with scope("tiles_d"):
        multiply_step(3)
    ring_sent()
    sent(gathered.at[0, pl.ds(0, 32 * (nc - 1))], sends.at[1])
    for turn in range(2):
        sent(pair_send.at[turn], sends.at[4 + turn])
        sent(gram_pair_send.at[turn], sends.at[15 + turn])
        sent(image_recv.at[turn, pl.ds(0, nz - 1)], sends.at[6 + turn])
        sent(gram_recv.at[turn, pl.ds(0, nz - 1)], sends.at[13 + turn])
        sent(walk_recv.at[turn, far], sends.at[8 + turn])
    with scope("wait_norm"):
        landed(norm_recv.at[pl.ds(0, nr - 1)], recvs.at[3])
    norms_ref[...] = jnp.sum(norm_recv[...], axis=0)
    sent(norm_recv.at[pl.ds(0, nr - 1)], sends.at[3])


def write(
    params,
    tiles,
    one,
    two,
    ray,
    norms,
    corr_ref,
    ham_ref,
    one_ref,
    two_ref,
    ray_ref,
    scaled,
    sems,
):
    rows = tiles.shape[1] // 4
    pairs = []
    for k in range(4):
        part = pl.ds(k * rows, rows)
        pairs.append((tiles.at[0, part], corr_ref.at[0, part]))
        pairs.append((tiles.at[1, part], ham_ref.at[0, part]))
    pairs += [(one, one_ref), (ray, ray_ref), (scaled, two_ref)]
    writes = [
        pltpu.make_async_copy(src, dst, sems.at[i])
        for i, (src, dst) in enumerate(pairs)
    ]
    for copy in writes[:-1]:
        copy.start()
    eye = lax.broadcasted_iota(jnp.int32, (32, 32), 0) == lax.broadcasted_iota(
        jnp.int32, (32, 32), 1
    )
    squares = to_column(norms[:, :32], eye)
    scaled[...] = two[...] * (1.0 / jnp.sqrt(squares * (1.0 / params) + EPSILON))
    writes[-1].start()
    for copy in writes:
        copy.wait()


def local(nr, nc, log_derivs, energy_derivs, start_block):
    wide, walkers, narrow = 64 * nc, 32 * nc, 64 * nr
    nz = nr // 2
    vmem = pl.BlockSpec(memory_space=pltpu.VMEM)
    full = nz // 2 - 1
    hbm = pl.BlockSpec(memory_space=pltpu.HBM)
    small = (
        jax.ShapeDtypeStruct((32, 64), F32),
        jax.ShapeDtypeStruct((32, 64), F32),
        jax.ShapeDtypeStruct((32, 32), F32),
    )
    arguments = (log_derivs, energy_derivs, start_block.T)
    results = pl.pallas_call(
        functools.partial(davidson, nr, nc),
        out_shape=(
            pltpu.VMEM((2, wide, narrow), F32),
            *(pltpu.VMEM(x.shape, F32) for x in small),
            pltpu.VMEM((1, 128), F32),
        ),
        in_specs=[hbm] * 3,
        out_specs=(vmem,) * 5,
        scratch_shapes=[
            pltpu.VMEM((32, wide), BF16),
            pltpu.VMEM((32, wide), BF16),
            pltpu.VMEM((32, 64), F32),
            pltpu.VMEM((walkers, wide), BF16),
            pltpu.VMEM((wide, walkers), BF16),
            pltpu.VMEM((nc, 32, 128), BF16),
            pltpu.VMEM((nr, walkers, 128), BF16),
            pltpu.VMEM((16, 128), F32),
            pltpu.VMEM((nc, 16, 128), F32),
            pltpu.VMEM((wide, 64), BF16),
            pltpu.VMEM((96, wide), BF16),
            pltpu.VMEM((nc // 2, 32, 128), F32),
            pltpu.VMEM((2, 16, 128), F32),
            pltpu.VMEM((2, 16, 128), F32),
            pltpu.VMEM((2, 16, 128), F32),
            pltpu.VMEM((2, nz, 16, 128), F32),
            pltpu.VMEM((2, 8, 128), F32),
            pltpu.VMEM((2, 8, 128), F32),
            pltpu.VMEM((2, 8, 128), F32),
            pltpu.VMEM((2, nz, 8, 128), F32),
            pltpu.VMEM((2, 16, 128), F32),
            pltpu.VMEM((2, nc, 16, 128), F32),
            pltpu.VMEM((1, 128), F32),
            pltpu.VMEM((nr, 1, 128), F32),
            pltpu.SemaphoreType.DMA((3,)),
            pltpu.SemaphoreType.DMA((17,)),
            pltpu.SemaphoreType.DMA((17,)),
            pltpu.SemaphoreType.DMA((4, 2, full + 2)),
        ],
        compiler_params=pltpu.CompilerParams(
            collective_id=0, has_side_effects=True, vmem_limit_bytes=24 * 1024 * 1024
        ),
        name="davidson",
    )(*(pltpu.with_memory_space_constraint(x, pltpu.HBM) for x in arguments))

    corr, ham, one, two, ray = pl.pallas_call(
        functools.partial(write, 64 * nc * nr),
        out_shape=(
            jax.ShapeDtypeStruct((1, wide, narrow), F32),
            jax.ShapeDtypeStruct((1, wide, narrow), F32),
            *small,
        ),
        in_specs=[vmem] * 5,
        out_specs=(hbm,) * 5,
        scratch_shapes=[pltpu.VMEM((32, 64), F32), pltpu.SemaphoreType.DMA((11,))],
        compiler_params=pltpu.CompilerParams(vmem_limit_bytes=24 * 1024 * 1024),
        name="tiles",
    )(*(pltpu.with_memory_space_constraint(x, pltpu.VMEM) for x in results))
    return one.T, two.T, ray, corr, ham


def solution(mesh):
    return jax.shard_map(
        functools.partial(local, mesh.shape["prow"], mesh.shape["pcol"]),
        mesh=mesh,
        in_specs=(P("pcol", "prow"), P("pcol", "prow"), P(("prow", "pcol"), None)),
        out_specs=(
            P(("prow", "pcol"), None),
            P(("prow", "pcol"), None),
            P(),
            P("pcol", "prow", None),
            P("pcol", "prow", None),
        ),
        check_vma=False,
    )
```

```python
import contextlib
import functools

import jax
import jax.numpy as jnp
from jax import lax
from jax.experimental import pallas as pl
from jax.experimental.pallas import tpu as pltpu
from jax.sharding import PartitionSpec as P

STABILIZER = 0.5
EPSILON = 1e-6
ENLARGED = 2.0**30
F32 = jnp.float32
BF16 = jnp.bfloat16
HIGHEST = lax.Precision.HIGHEST
MESH = pl.DeviceIdType.MESH
NT = (((1,), (1,)), ((), ()))
TN = (((0,), (0,)), ((), ()))


def scope(name):
    return contextlib.nullcontext()


def pieces(x):
    high = x.astype(BF16)
    rest = x - high.astype(F32)
    middle = rest.astype(BF16)
    low = (rest - middle.astype(F32)).astype(BF16)
    return jnp.concatenate([high, middle, low], axis=0)


def sum_rows(x, n):
    return x[:n] + x[n : 2 * n] + x[2 * n : 3 * n]


def to_row(column, eye):
    return jnp.sum(jnp.where(eye, column, 0.0), axis=0, keepdims=True)


def to_column(row, eye):
    return jnp.sum(jnp.where(eye, row, 0.0), axis=1, keepdims=True)


def fold(x):
    return jnp.concatenate([x[8 * g : 8 * g + 8] for g in range(4)], axis=1)


def unfold(folded):
    return jnp.concatenate(
        [
            jnp.concatenate([x[:, 32 * g : 32 * g + 32] for x in folded], axis=1)
            for g in range(4)
        ],
        axis=0,
    )


def inverse_of_two(a, b, d):
    scale = 1.0 / (a * d - b * b)
    return d * scale, -b * scale, a * scale


def solver_of_four(columns, k):
    g = [[columns[j][k + i : k + i + 1] for j in range(4)] for i in range(4)]
    p0, p1, p2 = inverse_of_two(g[0][0], g[1][0], g[1][1])
    t02, t12 = p0 * g[2][0] + p1 * g[2][1], p1 * g[2][0] + p2 * g[2][1]
    t03, t13 = p0 * g[3][0] + p1 * g[3][1], p1 * g[3][0] + p2 * g[3][1]
    w0, w1, w2 = inverse_of_two(
        g[2][2] - g[2][0] * t02 - g[2][1] * t12,
        g[3][2] - g[3][0] * t02 - g[3][1] * t12,
        g[3][3] - g[3][0] * t03 - g[3][1] * t13,
    )

    def solve(array):
        r = [array[k + i : k + i + 1] for i in range(4)]
        u0, u1 = p0 * r[0] + p1 * r[1], p1 * r[0] + p2 * r[1]
        v2 = r[2] - t02 * r[0] - t12 * r[1]
        v3 = r[3] - t03 * r[0] - t13 * r[1]
        x2, x3 = w0 * v2 + w1 * v3, w1 * v2 + w2 * v3
        return u0 - t02 * x2 - t03 * x3, u1 - t12 * x2 - t13 * x3, x2, x3

    return solve


def eliminate(matrix, right, eye):
    n = matrix.shape[0]
    diagonal = jnp.where(eye, matrix, 0.0)
    unit = lax.rsqrt(jnp.sum(diagonal, axis=1, keepdims=True))
    unit_row = lax.rsqrt(jnp.sum(diagonal, axis=0, keepdims=True))
    both = jnp.concatenate([matrix * unit * unit_row, right * unit], axis=1)
    rows = lax.broadcasted_iota(jnp.int32, both.shape, 0)

    def spread(at):
        return [
            jnp.broadcast_to(both[:, at + j : at + j + 1], both.shape)
            for j in range(4 if at < n else 0)
        ]

    now, later = spread(0), spread(4)
    for k in range(0, n, 4):
        solve = solver_of_four(now, k)
        pivots = (rows >= k) & (rows < k + 4)
        c = [
            jnp.where(rows == k + j, -1.0, jnp.where(pivots, 0.0, now[j]))
            for j in range(4)
        ]

        def step(array):
            x = solve(array)
            rest = jnp.where(pivots, 0.0, array)
            return (rest - c[0] * x[0] - c[1] * x[1]) - (c[2] * x[2] + c[3] * x[3])

        now = [step(array) for array in later]
        both = step(both)
        later = spread(k + 8)
    return both[:, n:] * unit


def farthest_first(m, n):
    steps = [(i, j) for i in range(m) for j in range(n) if i or j]
    return sorted(steps, key=lambda s: -min(s[0], m - s[0]) - min(s[1], n - s[1]))


def davidson(
    nr,
    nc,
    l_hbm,
    e_hbm,
    v_hbm,
    tiles_ref,
    one_ref,
    two_ref,
    ray_ref,
    norms_ref,
    l_ref,
    e_ref,
    v_ref,
    block,
    own_t,
    slabs,
    gathered,
    v_send,
    v_recv,
    weights,
    split_all,
    basis,
    pair_send,
    pair_recv,
    image_send,
    image_recv,
    gram_pair_send,
    gram_pair_recv,
    gram_send,
    gram_recv,
    walk_send,
    walk_recv,
    norm_send,
    norm_recv,
    loads,
    sends,
    recvs,
    ring_sems,
):
    p = lax.axis_index("prow")
    q = lax.axis_index("pcol")
    z = p // 2
    core = p % 2
    nz = nr // 2
    wide = 64 * nc
    walkers = 32 * nc
    params = wide * nr

    def row_of(zz, cc):
        return lax.rem(zz + nz, nz) * 2 + cc

    sibling = z * 2 + 1 - core

    def push(src, dst, send_sem, recv_sem, device):
        pltpu.make_async_remote_copy(
            src_ref=src,
            dst_ref=dst,
            send_sem=send_sem,
            recv_sem=recv_sem,
            device_id=device,
            device_id_type=MESH,
        ).start()

    def sent(ref, sem):
        pltpu.make_async_remote_copy(
            src_ref=ref,
            dst_ref=ref,
            send_sem=sem,
            recv_sem=sem,
            device_id={"prow": sibling},
            device_id_type=MESH,
        ).wait_send()

    def landed(ref, sem):
        pltpu.make_async_remote_copy(
            src_ref=ref,
            dst_ref=ref,
            send_sem=sem,
            recv_sem=sem,
            device_id={"prow": sibling},
            device_id_type=MESH,
        ).wait_recv()

    barrier = pltpu.get_barrier_semaphore()

    nx = 4
    ny = nc // nx
    x, y = q % nx, q // nx

    def along_x(i):
        return y * nx + lax.rem(x + i, nx)

    def along_y(i):
        return lax.rem(y + i, ny) * nx + x

    plane = [
        lax.rem(y + j, ny) * nx + lax.rem(x + i, nx)
        for i, j in farthest_first(nx, ny)
    ]
    chips = [row_of(z + i, core) for i, _ in farthest_first(nz, 1)]
    rows = [
        row_of(z + i, lax.rem(core + j, 2)) for i, j in farthest_first(nz, 2)
    ]
    far_rows = len(rows) // 3
    for axis, members in (
        ("pcol", plane[: nc // 3]),
        ("prow", rows[:far_rows]),
        ("pcol", plane[nc // 3 :]),
        ("prow", rows[far_rows:]),
    ):
        for member in members:
            pl.semaphore_signal(
                barrier, inc=1, device_id={axis: member}, device_id_type=MESH
            )
    reads = [
        pltpu.make_async_copy(src, dst, loads.at[i])
        for i, (src, dst) in enumerate(((v_hbm, v_ref), (l_hbm, l_ref), (e_hbm, e_ref)))
    ]
    for read in reads:
        read.start()


    def to_plane(copy):
        for peer in plane:
            copy(peer)

    reads[0].wait()
    v_own = v_ref[...]
    v_send[...] = jnp.concatenate([v_own[:16], v_own[16:]], axis=1)
    v_recv[pl.ds(q, 1)] = v_send[...][None]
    reads[1].wait()
    reads[2].wait()
    l_own = l_ref[...]
    e_own = e_ref[...]
    for j in range(nc):
        slabs[j] = jnp.concatenate(
            [l_own[:, 64 * j : 64 * j + 64], e_own[:, 64 * j : 64 * j + 64]], axis=1
        )
    own_rows = pl.ds(pl.multiple_of(q * 32, 32), 32)
    gathered[pl.ds(p, 1), own_rows, :] = slabs[pl.ds(q, 1)]
    block[own_rows, :] = l_own
    weights[...] = jnp.concatenate([l_own, e_own], axis=0).T
    with scope("barrier"):
        pl.semaphore_wait(barrier, nc - 1 + nr - 1)
    to_plane(
        lambda peer: push(
            v_send, v_recv.at[q], sends.at[0], recvs.at[0], {"pcol": peer}
        )
    )
    def half_of(member, part):
        return block.at[pl.ds(pl.multiple_of(member * 32 + 16 * part, 16), 16)]

    def block_first():
        for i in range(1, nx):
            ref = half_of(q, 0)
            push(ref, ref, sends.at[2], recvs.at[2], {"pcol": along_x(i)})
        for i in range(1, ny):
            ref = half_of(q, 1)
            push(ref, ref, sends.at[10], recvs.at[10], {"pcol": along_y(i)})

    def block_second():
        landed(block.at[pl.ds(0, 16 * (nx - 1))], recvs.at[2])
        landed(block.at[pl.ds(0, 16 * (ny - 1))], recvs.at[10])

        for i, _ in farthest_first(ny, 1):
            for k in range(nx):
                ref = half_of(along_x(k), 0)
                push(ref, ref, sends.at[11], recvs.at[11], {"pcol": along_y(i)})
        for i, _ in farthest_first(nx, 1):
            for k in range(ny):
                ref = half_of(along_y(k), 1)
                push(ref, ref, sends.at[12], recvs.at[12], {"pcol": along_x(i)})

    counts = (nx - 1, ny - 1, nx * (ny - 1), ny * (nx - 1))

    def block_landed():
        for sem, count in zip((11, 12), counts[2:], strict=True):
            landed(block.at[pl.ds(0, 16 * count)], recvs.at[sem])

    def block_sent():
        for sem, count in zip((2, 10, 11, 12), counts, strict=True):
            sent(block.at[pl.ds(0, 16 * count)], sends.at[sem])

    block_first()
    to_plane(
        lambda peer: push(
            slabs.at[peer],
            gathered.at[p, own_rows],
            sends.at[1],
            recvs.at[1],
            {"pcol": peer},
        )
    )

    eye = lax.broadcasted_iota(jnp.int32, (32, 32), 0) == lax.broadcasted_iota(
        jnp.int32, (32, 32), 1
    )
    far = pl.ds(0, nc - 1)

    full = nz // 2 - 1
    half = walkers // 2
    everything, lower, upper = pl.ds(0, walkers), pl.ds(0, half), pl.ds(half, half)

    def part_of(way, step):
        return everything if step < full else (lower, upper)[way]

    def ring_start():
        landed(gathered.at[0, pl.ds(0, 32 * (nc - 1))], recvs.at[1])
        ring_send(0)
        own = gathered.at[p]
        push(
            own,
            own,
            ring_sems.at[2, 0, full + 1],
            ring_sems.at[3, 0, full + 1],
            {"prow": sibling},
        )

    def ring_send(step):
        for way, sign in ((0, 1), (1, -1)):
            ref = gathered.at[row_of(z - sign * step, core), part_of(way, step)]
            push(
                ref,
                ref,
                ring_sems.at[0, way, step],
                ring_sems.at[1, way, step],
                {"prow": row_of(z + sign, core)},
            )

    def ring_landed(step):
        for way, sign in ((0, 1), (1, -1)):
            ref = gathered.at[row_of(z - sign * (step + 1), core), part_of(way, step)]
            landed(ref, ring_sems.at[1, way, step])
            push(
                ref,
                ref,
                ring_sems.at[2, way, step],
                ring_sems.at[3, way, step],
                {"prow": sibling},
            )

    def ring_advance(step):
        if step <= full:
            ring_landed(step)
        if step < full:
            ring_send(step + 1)

    def sibling_landed(step):
        for way, sign in ((0, 1), (1, -1)):
            chunk = row_of(z - sign * (step + 1), 1 - core)
            landed(gathered.at[chunk, part_of(way, step)], ring_sems.at[3, way, step])

    def ring_sent():
        sent(gathered.at[p], ring_sems.at[2, 0, full + 1])
        for step in range(full + 1):
            for way in range(2):
                ref = gathered.at[p, part_of(way, step)]
                sent(ref, ring_sems.at[0, way, step])
                sent(ref, ring_sems.at[2, way, step])

    def multiply(chunk):
        a = gathered[pl.ds(2 * chunk, 1)][0]
        b = gathered[pl.ds(2 * chunk + 1, 1)][0]
        right = jnp.concatenate(
            [a[:, :64], b[:, :64], a[:, 64:], b[:, 64:]], axis=1
        )
        out = jnp.dot(own_t[...], right, preferred_element_type=F32) * (1.0 / walkers)
        columns = pl.ds(pl.multiple_of(chunk * 128, 128), 128)
        tiles_ref[0, :, columns] = out[:, :128]
        tiles_ref[1, :, columns] = out[:, 128:]

    def multiply_own():
        own_t[...] = block[...].T
        landed(gathered.at[sibling], ring_sems.at[3, 0, full + 1])
        multiply(z)
        row = lax.broadcasted_iota(jnp.int32, (64, 128), 0)
        column = lax.broadcasted_iota(jnp.int32, (64, 128), 1)
        mine = pl.ds(pl.multiple_of(q * 64, 64), 64)
        columns = pl.ds(pl.multiple_of(z * 128, 128), 128)
        tiles_ref[0, mine, columns] += jnp.where(
            column == row + core * 64, STABILIZER, 0.0
        )

    def multiply_step(step):
        if step > full:
            return
        sibling_landed(step)

        def body(way, carry):
            multiply(lax.rem(z + (2 * way - 1) * (step + 1) + nz, nz))
            return carry

        lax.fori_loop(0, 2 if step < full else 1, body, 0)

    def both_cores(src, dst, turn, sem):
        push(
            src.at[turn],
            dst.at[turn],
            sends.at[sem + turn],
            recvs.at[sem + turn],
            {"prow": sibling},
        )

    def along_z(src, dst, turn, sem):
        for chip in chips:
            push(
                src.at[turn],
                dst.at[turn, z],
                sends.at[sem + turn],
                recvs.at[sem + turn],
                {"prow": chip},
            )

    def image_start(vec, turn):
        with scope("values"):
            split = pieces(vec)
            out = sum_rows(jnp.dot(split, weights[...], preferred_element_type=F32), 32)
            pair_send[turn] = jnp.concatenate(
                [fold(out[:, :32]), fold(out[:, 32:])], axis=0
            )
        both_cores(pair_send, pair_recv, turn, 4)
        if turn == 0:
            with scope("block_second"):
                block_second()
        with scope("wait_pair"):
            landed(pair_recv.at[turn], recvs.at[4 + turn])
        with scope("pair_sum"):
            mine = pair_send[turn] + pair_recv[turn]
            image_send[turn] = mine
            image_recv[turn, pl.ds(z, 1)] = mine[None]
        along_z(image_send, image_recv, turn, 6)
        if turn == 1:
            sent(v_recv.at[far], sends.at[0])
        with scope("gram"):
            split_all[...] = split
            out = lax.dot_general(
                split, split_all[...], NT, preferred_element_type=F32
            )
            out = sum_rows(out, 32)
            gram_pair_send[turn] = fold(out[:, :32] + out[:, 32:64] + out[:, 64:])
        both_cores(gram_pair_send, gram_pair_recv, turn, 15)

    def gram_start(turn):
        landed(gram_pair_recv.at[turn], recvs.at[15 + turn])
        mine = gram_pair_send[turn] + gram_pair_recv[turn]
        gram_send[turn] = mine
        gram_recv[turn, pl.ds(z, 1)] = mine[None]
        along_z(gram_send, gram_recv, turn, 13)

    def walk_start(turn):
        with scope("wait_image"):
            landed(image_recv.at[turn, pl.ds(0, nz - 1)], recvs.at[6 + turn])
        with scope("image_sum"):
            mine = jnp.sum(image_recv[turn], axis=0)
            walk_send[turn] = mine
        walk_recv[turn, pl.ds(q, 1)] = mine[None]
        to_plane(
            lambda peer: push(
                walk_send.at[turn],
                walk_recv.at[turn, q],
                sends.at[8 + turn],
                recvs.at[8 + turn],
                {"pcol": peer},
            )
        )

    def gram_landed(turn):
        landed(gram_recv.at[turn, pl.ds(0, nz - 1)], recvs.at[13 + turn])
        return unfold([jnp.sum(gram_recv[turn], axis=0)])

    def walk_landed(turn):
        with scope("wait_walk"):
            landed(walk_recv.at[turn, far], recvs.at[8 + turn])
        return [
            jnp.concatenate(
                [
                    unfold([walk_recv[turn, k + j, rows] for j in range(4)])
                    for k in range(0, nc, 4)
                ],
                axis=1,
            )
            for rows in (slice(0, 8), slice(8, 16))
        ]

    def residual(vec, l_val, e_val, gram, inverse_diag):
        with scope("products"):
            l_split = pieces(l_val)
            both = jnp.concatenate([l_split, pieces(e_val)], axis=0)
            out = sum_rows(
                lax.dot_general(l_split, both, NT, preferred_element_type=F32), 32
            )
        ray_s = out[:, :32] + out[:, 32:64] + out[:, 64:96]
        ray_h = out[:, 96:128] + out[:, 128:160] + out[:, 160:192]
        with scope("images"):
            image = jnp.dot(both, block[...], preferred_element_type=F32)
            image_s = sum_rows(image[:96], 32) * (1.0 / walkers) + STABILIZER * vec
            image_h = sum_rows(image[96:], 32) * (1.0 / walkers) * inverse_diag
            s = pieces(image_s * inverse_diag)
            right = jnp.concatenate(
                [s[:32], s[32:64], s[:32], s[64:], s[32:64], s[:32]], axis=0
            )
        with scope("eliminate"):
            coeffs = eliminate(
                ray_s * (1.0 / walkers) + STABILIZER * gram,
                ray_h * (1.0 / walkers),
                eye,
            )
        with scope("mix"):
            c = pieces(coeffs)
            left = jnp.concatenate(
                [c[:32], c[:32], c[32:64], c[:32], c[32:64], c[64:]], axis=0
            )
            out = lax.dot_general(left, right, TN, preferred_element_type=F32)
            result = image_h - out
        return result, coeffs

    def own_part(vec):
        for k in range(nc // 2):
            basis[k] = vec[:, 128 * k : 128 * k + 128]
        chunk = basis[pl.ds(q // 2, 1)][0]
        return jnp.where(q % 2 == 0, chunk[:, :64], chunk[:, 64:])

    with scope("wait_v"):
        landed(v_recv.at[far], recvs.at[0])
    top, bottom = [], []
    for k in range(0, nc, 2):
        a, b = v_recv[k], v_recv[k + 1]
        top += [a[:, :64], b[:, :64]]
        bottom += [a[:, 64:], b[:, 64:]]
    vec = jnp.concatenate(
        [jnp.concatenate(top, axis=1), jnp.concatenate(bottom, axis=1)], axis=0
    )
    image_start(vec, 0)
    with scope("ring_start"):
        ring_start()
    gram_start(0)
    walk_start(0)
    with scope("wait_block"):
        block_landed()
    squares = jnp.zeros((8, wide), F32)
    for k in range(0, walkers, 16):
        part = block[k : k + 16].astype(F32)
        part = part * part
        squares = squares + part[:8] + part[8:]
    inverse_diag = 1.0 / (
        jnp.sum(squares, axis=0, keepdims=True) * (1.0 / walkers) + STABILIZER
    )
    gram = gram_landed(0)
    with scope("ring_0"):
        ring_advance(0)
    l_val, e_val = walk_landed(0)
    vec, _ = residual(vec, l_val, e_val, gram, inverse_diag * ENLARGED)

    image_start(vec, 1)
    gram_start(1)
    with scope("ring_1"):
        ring_advance(1)
    with scope("tiles_a"):
        multiply_own()
    walk_start(1)
    with scope("tiles_b"):
        multiply_step(0)
    gram = gram_landed(1)
    norms = jnp.sum(jnp.where(eye, gram, 0.0), axis=1, keepdims=True)
    norms = norms * (1.0 / ENLARGED) * (1.0 / ENLARGED)
    scale = (1.0 / ENLARGED) / jnp.sqrt(norms * (1.0 / params) + EPSILON)
    gram = gram * scale * to_row(scale, eye)
    vec = vec * scale
    one_ref[...] = own_part(vec)
    with scope("ring_2"):
        ring_advance(2)
    l_val, e_val = walk_landed(1)
    vec, coeffs = residual(vec, l_val * scale, e_val * scale, gram, inverse_diag)
    norms = to_row(jnp.sum(vec * vec, axis=1, keepdims=True), eye)
    norm_send[...] = jnp.concatenate([norms, jnp.zeros((1, 96), F32)], axis=1)
    norm_recv[pl.ds(p, 1)] = norm_send[...][None]

    for row in rows:
        push(norm_send, norm_recv.at[p], sends.at[3], recvs.at[3], {"prow": row})
    block_sent()
    ray_ref[...] = coeffs
    two_ref[...] = own_part(vec)
    with scope("tiles_c"):
        multiply_step(1)
        multiply_step(2)
    with scope("ring_3"):
        ring_advance(3)
    with scope("tiles_d"):
        multiply_step(3)
    ring_sent()
    sent(gathered.at[0, pl.ds(0, 32 * (nc - 1))], sends.at[1])
    for turn in range(2):
        sent(pair_send.at[turn], sends.at[4 + turn])
        sent(gram_pair_send.at[turn], sends.at[15 + turn])
        sent(image_recv.at[turn, pl.ds(0, nz - 1)], sends.at[6 + turn])
        sent(gram_recv.at[turn, pl.ds(0, nz - 1)], sends.at[13 + turn])
        sent(walk_recv.at[turn, far], sends.at[8 + turn])
    with scope("wait_norm"):
        landed(norm_recv.at[pl.ds(0, nr - 1)], recvs.at[3])
    norms_ref[...] = jnp.sum(norm_recv[...], axis=0)
    sent(norm_recv.at[pl.ds(0, nr - 1)], sends.at[3])


def write(
    params,
    tiles,
    one,
    two,
    ray,
    norms,
    corr_ref,
    ham_ref,
    one_ref,
    two_ref,
    ray_ref,
    scaled,
    sems,
):
    rows = tiles.shape[1] // 4
    pairs = []
    for k in range(4):
        part = pl.ds(k * rows, rows)
        pairs.append((tiles.at[0, part], corr_ref.at[0, part]))
        pairs.append((tiles.at[1, part], ham_ref.at[0, part]))
    pairs += [(one, one_ref), (ray, ray_ref), (scaled, two_ref)]
    writes = [
        pltpu.make_async_copy(src, dst, sems.at[i])
        for i, (src, dst) in enumerate(pairs)
    ]
    for copy in writes[:-1]:
        copy.start()
    eye = lax.broadcasted_iota(jnp.int32, (32, 32), 0) == lax.broadcasted_iota(
        jnp.int32, (32, 32), 1
    )
    squares = to_column(norms[:, :32], eye)
    scaled[...] = two[...] * (1.0 / jnp.sqrt(squares * (1.0 / params) + EPSILON))
    writes[-1].start()
    for copy in writes:
        copy.wait()


def local(nr, nc, log_derivs, energy_derivs, start_block):
    wide, walkers, narrow = 64 * nc, 32 * nc, 64 * nr
    nz = nr // 2
    vmem = pl.BlockSpec(memory_space=pltpu.VMEM)
    full = nz // 2 - 1
    hbm = pl.BlockSpec(memory_space=pltpu.HBM)
    small = (
        jax.ShapeDtypeStruct((32, 64), F32),
        jax.ShapeDtypeStruct((32, 64), F32),
        jax.ShapeDtypeStruct((32, 32), F32),
    )
    arguments = (log_derivs, energy_derivs, start_block.T)
    results = pl.pallas_call(
        functools.partial(davidson, nr, nc),
        out_shape=(
            pltpu.VMEM((2, wide, narrow), F32),
            *(pltpu.VMEM(x.shape, F32) for x in small),
            pltpu.VMEM((1, 128), F32),
        ),
        in_specs=[hbm] * 3,
        out_specs=(vmem,) * 5,
        scratch_shapes=[
            pltpu.VMEM((32, wide), BF16),
            pltpu.VMEM((32, wide), BF16),
            pltpu.VMEM((32, 64), F32),
            pltpu.VMEM((walkers, wide), BF16),
            pltpu.VMEM((wide, walkers), BF16),
            pltpu.VMEM((nc, 32, 128), BF16),
            pltpu.VMEM((nr, walkers, 128), BF16),
            pltpu.VMEM((16, 128), F32),
            pltpu.VMEM((nc, 16, 128), F32),
            pltpu.VMEM((wide, 64), BF16),
            pltpu.VMEM((96, wide), BF16),
            pltpu.VMEM((nc // 2, 32, 128), F32),
            pltpu.VMEM((2, 16, 128), F32),
            pltpu.VMEM((2, 16, 128), F32),
            pltpu.VMEM((2, 16, 128), F32),
            pltpu.VMEM((2, nz, 16, 128), F32),
            pltpu.VMEM((2, 8, 128), F32),
            pltpu.VMEM((2, 8, 128), F32),
            pltpu.VMEM((2, 8, 128), F32),
            pltpu.VMEM((2, nz, 8, 128), F32),
            pltpu.VMEM((2, 16, 128), F32),
            pltpu.VMEM((2, nc, 16, 128), F32),
            pltpu.VMEM((1, 128), F32),
            pltpu.VMEM((nr, 1, 128), F32),
            pltpu.SemaphoreType.DMA((3,)),
            pltpu.SemaphoreType.DMA((17,)),
            pltpu.SemaphoreType.DMA((17,)),
            pltpu.SemaphoreType.DMA((4, 2, full + 2)),
        ],
        compiler_params=pltpu.CompilerParams(
            collective_id=0, has_side_effects=True, vmem_limit_bytes=24 * 1024 * 1024
        ),
        name="davidson",
    )(*(pltpu.with_memory_space_constraint(x, pltpu.HBM) for x in arguments))

    corr, ham, one, two, ray = pl.pallas_call(
        functools.partial(write, 64 * nc * nr),
        out_shape=(
            jax.ShapeDtypeStruct((1, wide, narrow), F32),
            jax.ShapeDtypeStruct((1, wide, narrow), F32),
            *small,
        ),
        in_specs=[vmem] * 5,
        out_specs=(hbm,) * 5,
        scratch_shapes=[pltpu.VMEM((32, 64), F32), pltpu.SemaphoreType.DMA((11,))],
        compiler_params=pltpu.CompilerParams(vmem_limit_bytes=24 * 1024 * 1024),
        name="tiles",
    )(*(pltpu.with_memory_space_constraint(x, pltpu.VMEM) for x in results))
    return one.T, two.T, ray, corr, ham


def solution(mesh):
    return jax.shard_map(
        functools.partial(local, mesh.shape["prow"], mesh.shape["pcol"]),
        mesh=mesh,
        in_specs=(P("pcol", "prow"), P("pcol", "prow"), P(("prow", "pcol"), None)),
        out_specs=(
            P(("prow", "pcol"), None),
            P(("prow", "pcol"), None),
            P(),
            P("pcol", "prow", None),
            P("pcol", "prow", None),
        ),
        check_vma=False,
    )
```

```python
import contextlib
import functools

import jax
import jax.numpy as jnp
from jax import lax
from jax.experimental import pallas as pl
from jax.experimental.pallas import tpu as pltpu
from jax.sharding import PartitionSpec as P

STABILIZER = 0.5
EPSILON = 1e-6
ENLARGED = 2.0**30
F32 = jnp.float32
BF16 = jnp.bfloat16
HIGHEST = lax.Precision.HIGHEST
MESH = pl.DeviceIdType.MESH
NT = (((1,), (1,)), ((), ()))
TN = (((0,), (0,)), ((), ()))


def scope(name):
    return contextlib.nullcontext()


def pieces(x):
    high = x.astype(BF16)
    rest = x - high.astype(F32)
    middle = rest.astype(BF16)
    low = (rest - middle.astype(F32)).astype(BF16)
    return jnp.concatenate([high, middle, low], axis=0)


def sum_rows(x, n):
    return x[:n] + x[n : 2 * n] + x[2 * n : 3 * n]


def to_row(column, eye):
    return jnp.sum(jnp.where(eye, column, 0.0), axis=0, keepdims=True)


def to_column(row, eye):
    return jnp.sum(jnp.where(eye, row, 0.0), axis=1, keepdims=True)


def fold(x):
    return jnp.concatenate([x[8 * g : 8 * g + 8] for g in range(4)], axis=1)


def unfold(folded):
    return jnp.concatenate(
        [
            jnp.concatenate([x[:, 32 * g : 32 * g + 32] for x in folded], axis=1)
            for g in range(4)
        ],
        axis=0,
    )


def inverse_of_two(a, b, d):
    scale = 1.0 / (a * d - b * b)
    return d * scale, -b * scale, a * scale


def solver_of_four(columns, k):
    g = [[columns[j][k + i : k + i + 1] for j in range(4)] for i in range(4)]
    p0, p1, p2 = inverse_of_two(g[0][0], g[1][0], g[1][1])
    t02, t12 = p0 * g[2][0] + p1 * g[2][1], p1 * g[2][0] + p2 * g[2][1]
    t03, t13 = p0 * g[3][0] + p1 * g[3][1], p1 * g[3][0] + p2 * g[3][1]
    w0, w1, w2 = inverse_of_two(
        g[2][2] - g[2][0] * t02 - g[2][1] * t12,
        g[3][2] - g[3][0] * t02 - g[3][1] * t12,
        g[3][3] - g[3][0] * t03 - g[3][1] * t13,
    )

    def solve(array):
        r = [array[k + i : k + i + 1] for i in range(4)]
        u0, u1 = p0 * r[0] + p1 * r[1], p1 * r[0] + p2 * r[1]
        v2 = r[2] - t02 * r[0] - t12 * r[1]
        v3 = r[3] - t03 * r[0] - t13 * r[1]
        x2, x3 = w0 * v2 + w1 * v3, w1 * v2 + w2 * v3
        return u0 - t02 * x2 - t03 * x3, u1 - t12 * x2 - t13 * x3, x2, x3

    return solve


def eliminate(matrix, right, eye):
    n = matrix.shape[0]
    diagonal = jnp.where(eye, matrix, 0.0)
    unit = lax.rsqrt(jnp.sum(diagonal, axis=1, keepdims=True))
    unit_row = lax.rsqrt(jnp.sum(diagonal, axis=0, keepdims=True))
    both = jnp.concatenate([matrix * unit * unit_row, right * unit], axis=1)
    rows = lax.broadcasted_iota(jnp.int32, both.shape, 0)

    def spread(at):
        return [
            jnp.broadcast_to(both[:, at + j : at + j + 1], both.shape)
            for j in range(4 if at < n else 0)
        ]

    now, later = spread(0), spread(4)
    for k in range(0, n, 4):
        solve = solver_of_four(now, k)
        pivots = (rows >= k) & (rows < k + 4)
        c = [
            jnp.where(rows == k + j, -1.0, jnp.where(pivots, 0.0, now[j]))
            for j in range(4)
        ]

        def step(array):
            x = solve(array)
            rest = jnp.where(pivots, 0.0, array)
            return (rest - c[0] * x[0] - c[1] * x[1]) - (c[2] * x[2] + c[3] * x[3])

        now = [step(array) for array in later]
        both = step(both)
        later = spread(k + 8)
    return both[:, n:] * unit


def farthest_first(m, n):
    steps = [(i, j) for i in range(m) for j in range(n) if i or j]
    return sorted(steps, key=lambda s: -min(s[0], m - s[0]) - min(s[1], n - s[1]))


def davidson(
    nr,
    nc,
    l_hbm,
    e_hbm,
    v_hbm,
    tiles_ref,
    one_ref,
    two_ref,
    ray_ref,
    norms_ref,
    l_ref,
    e_ref,
    v_ref,
    block,
    own_t,
    slabs,
    gathered,
    v_send,
    v_recv,
    weights,
    split_all,
    basis,
    pair_send,
    pair_recv,
    image_send,
    image_recv,
    gram_pair_send,
    gram_pair_recv,
    gram_send,
    gram_recv,
    walk_send,
    walk_recv,
    norm_send,
    norm_recv,
    loads,
    sends,
    recvs,
    ring_sems,
):
    p = lax.axis_index("prow")
    q = lax.axis_index("pcol")
    z = p // 2
    core = p % 2
    nz = nr // 2
    wide = 64 * nc
    walkers = 32 * nc
    params = wide * nr

    def row_of(zz, cc):
        return lax.rem(zz + nz, nz) * 2 + cc

    sibling = z * 2 + 1 - core

    def push(src, dst, send_sem, recv_sem, device):
        pltpu.make_async_remote_copy(
            src_ref=src,
            dst_ref=dst,
            send_sem=send_sem,
            recv_sem=recv_sem,
            device_id=device,
            device_id_type=MESH,
        ).start()

    def sent(ref, sem):
        pltpu.make_async_remote_copy(
            src_ref=ref,
            dst_ref=ref,
            send_sem=sem,
            recv_sem=sem,
            device_id={"prow": sibling},
            device_id_type=MESH,
        ).wait_send()

    def landed(ref, sem):
        pltpu.make_async_remote_copy(
            src_ref=ref,
            dst_ref=ref,
            send_sem=sem,
            recv_sem=sem,
            device_id={"prow": sibling},
            device_id_type=MESH,
        ).wait_recv()

    barrier = pltpu.get_barrier_semaphore()

    nx = 4
    ny = nc // nx
    x, y = q % nx, q // nx

    def along_x(i):
        return y * nx + lax.rem(x + i, nx)

    def along_y(i):
        return lax.rem(y + i, ny) * nx + x

    plane = [
        lax.rem(y + j, ny) * nx + lax.rem(x + i, nx)
        for i, j in farthest_first(nx, ny)
    ]
    chips = [row_of(z + i, core) for i, _ in farthest_first(nz, 1)]
    rows = [
        row_of(z + i, lax.rem(core + j, 2)) for i, j in farthest_first(nz, 2)
    ]
    far_rows = len(rows) // 3
    for axis, members in (
        ("pcol", plane[: nc // 3]),
        ("prow", rows[:far_rows]),
        ("pcol", plane[nc // 3 :]),
        ("prow", rows[far_rows:]),
    ):
        for member in members:
            pl.semaphore_signal(
                barrier, inc=1, device_id={axis: member}, device_id_type=MESH
            )
    reads = [
        pltpu.make_async_copy(src, dst, loads.at[i])
        for i, (src, dst) in enumerate(((v_hbm, v_ref), (l_hbm, l_ref), (e_hbm, e_ref)))
    ]
    for read in reads:
        read.start()


    def to_plane(copy):
        for peer in plane:
            copy(peer)

    reads[0].wait()
    v_own = v_ref[...]
    v_send[...] = jnp.concatenate([v_own[:16], v_own[16:]], axis=1)
    v_recv[pl.ds(q, 1)] = v_send[...][None]
    reads[1].wait()
    reads[2].wait()
    l_own = l_ref[...]
    e_own = e_ref[...]
    for j in range(nc):
        slabs[j] = jnp.concatenate(
            [l_own[:, 64 * j : 64 * j + 64], e_own[:, 64 * j : 64 * j + 64]], axis=1
        )
    own_rows = pl.ds(pl.multiple_of(q * 32, 32), 32)
    gathered[pl.ds(p, 1), own_rows, :] = slabs[pl.ds(q, 1)]
    block[own_rows, :] = l_own
    weights[...] = jnp.concatenate([l_own, e_own], axis=0).T
    with scope("barrier"):
        pl.semaphore_wait(barrier, nc - 1 + nr - 1)
    to_plane(
        lambda peer: push(
            v_send, v_recv.at[q], sends.at[0], recvs.at[0], {"pcol": peer}
        )
    )
    def half_of(member, part):
        return block.at[pl.ds(pl.multiple_of(member * 32 + 16 * part, 16), 16)]

    def block_first():
        for i in range(1, nx):
            ref = half_of(q, 0)
            push(ref, ref, sends.at[2], recvs.at[2], {"pcol": along_x(i)})
        for i in range(1, ny):
            ref = half_of(q, 1)
            push(ref, ref, sends.at[10], recvs.at[10], {"pcol": along_y(i)})

    def block_second():
        landed(block.at[pl.ds(0, 16 * (nx - 1))], recvs.at[2])
        landed(block.at[pl.ds(0, 16 * (ny - 1))], recvs.at[10])

        for i, _ in farthest_first(ny, 1):
            for k in range(nx):
                ref = half_of(along_x(k), 0)
                push(ref, ref, sends.at[11], recvs.at[11], {"pcol": along_y(i)})
        for i, _ in farthest_first(nx, 1):
            for k in range(ny):
                ref = half_of(along_y(k), 1)
                push(ref, ref, sends.at[12], recvs.at[12], {"pcol": along_x(i)})

    counts = (nx - 1, ny - 1, nx * (ny - 1), ny * (nx - 1))

    def block_landed():
        for sem, count in zip((11, 12), counts[2:], strict=True):
            landed(block.at[pl.ds(0, 16 * count)], recvs.at[sem])

    def block_sent():
        for sem, count in zip((2, 10, 11, 12), counts, strict=True):
            sent(block.at[pl.ds(0, 16 * count)], sends.at[sem])

    block_first()
    to_plane(
        lambda peer: push(
            slabs.at[peer],
            gathered.at[p, own_rows],
            sends.at[1],
            recvs.at[1],
            {"pcol": peer},
        )
    )

    eye = lax.broadcasted_iota(jnp.int32, (32, 32), 0) == lax.broadcasted_iota(
        jnp.int32, (32, 32), 1
    )
    far = pl.ds(0, nc - 1)

    full = nz // 2 - 1
    half = walkers // 2
    everything, lower, upper = pl.ds(0, walkers), pl.ds(0, half), pl.ds(half, half)

    def part_of(way, step):
        return everything if step < full else (lower, upper)[way]

    def ring_start():
        landed(gathered.at[0, pl.ds(0, 32 * (nc - 1))], recvs.at[1])
        ring_send(0)
        own = gathered.at[p]
        push(
            own,
            own,
            ring_sems.at[2, 0, full + 1],
            ring_sems.at[3, 0, full + 1],
            {"prow": sibling},
        )

    def ring_send(step):
        for way, sign in ((0, 1), (1, -1)):
            ref = gathered.at[row_of(z - sign * step, core), part_of(way, step)]
            push(
                ref,
                ref,
                ring_sems.at[0, way, step],
                ring_sems.at[1, way, step],
                {"prow": row_of(z + sign, core)},
            )

    def ring_landed(step):
        for way, sign in ((0, 1), (1, -1)):
            ref = gathered.at[row_of(z - sign * (step + 1), core), part_of(way, step)]
            landed(ref, ring_sems.at[1, way, step])
            push(
                ref,
                ref,
                ring_sems.at[2, way, step],
                ring_sems.at[3, way, step],
                {"prow": sibling},
            )

    def ring_advance(step):
        if step <= full:
            ring_landed(step)
        if step < full:
            ring_send(step + 1)

    def sibling_landed(step):
        for way, sign in ((0, 1), (1, -1)):
            chunk = row_of(z - sign * (step + 1), 1 - core)
            landed(gathered.at[chunk, part_of(way, step)], ring_sems.at[3, way, step])

    def ring_sent():
        sent(gathered.at[p], ring_sems.at[2, 0, full + 1])
        for step in range(full + 1):
            for way in range(2):
                ref = gathered.at[p, part_of(way, step)]
                sent(ref, ring_sems.at[0, way, step])
                sent(ref, ring_sems.at[2, way, step])

    def multiply(chunk):
        a = gathered[pl.ds(2 * chunk, 1)][0]
        b = gathered[pl.ds(2 * chunk + 1, 1)][0]
        right = jnp.concatenate(
            [a[:, :64], b[:, :64], a[:, 64:], b[:, 64:]], axis=1
        )
        out = jnp.dot(own_t[...], right, preferred_element_type=F32) * (1.0 / walkers)
        columns = pl.ds(pl.multiple_of(chunk * 128, 128), 128)
        tiles_ref[0, :, columns] = out[:, :128]
        tiles_ref[1, :, columns] = out[:, 128:]

    def multiply_own():
        own_t[...] = block[...].T
        landed(gathered.at[sibling], ring_sems.at[3, 0, full + 1])
        multiply(z)
        row = lax.broadcasted_iota(jnp.int32, (64, 128), 0)
        column = lax.broadcasted_iota(jnp.int32, (64, 128), 1)
        mine = pl.ds(pl.multiple_of(q * 64, 64), 64)
        columns = pl.ds(pl.multiple_of(z * 128, 128), 128)
        tiles_ref[0, mine, columns] += jnp.where(
            column == row + core * 64, STABILIZER, 0.0
        )

    def multiply_step(step):
        if step > full:
            return
        sibling_landed(step)

        def body(way, carry):
            multiply(lax.rem(z + (2 * way - 1) * (step + 1) + nz, nz))
            return carry

        lax.fori_loop(0, 2 if step < full else 1, body, 0)

    def both_cores(src, dst, turn, sem):
        push(
            src.at[turn],
            dst.at[turn],
            sends.at[sem + turn],
            recvs.at[sem + turn],
            {"prow": sibling},
        )

    def along_z(src, dst, turn, sem):
        for chip in chips:
            push(
                src.at[turn],
                dst.at[turn, z],
                sends.at[sem + turn],
                recvs.at[sem + turn],
                {"prow": chip},
            )

    def image_start(vec, turn):
        with scope("values"):
            split = pieces(vec)
            out = sum_rows(jnp.dot(split, weights[...], preferred_element_type=F32), 32)
            pair_send[turn] = jnp.concatenate(
                [fold(out[:, :32]), fold(out[:, 32:])], axis=0
            )
        both_cores(pair_send, pair_recv, turn, 4)
        if turn == 0:
            with scope("block_second"):
                block_second()
        with scope("wait_pair"):
            landed(pair_recv.at[turn], recvs.at[4 + turn])
        with scope("pair_sum"):
            mine = pair_send[turn] + pair_recv[turn]
            image_send[turn] = mine
            image_recv[turn, pl.ds(z, 1)] = mine[None]
        along_z(image_send, image_recv, turn, 6)
        if turn == 1:
            sent(v_recv.at[far], sends.at[0])
        with scope("gram"):
            split_all[...] = split
            out = lax.dot_general(
                split, split_all[...], NT, preferred_element_type=F32
            )
            out = sum_rows(out, 32)
            gram_pair_send[turn] = fold(out[:, :32] + out[:, 32:64] + out[:, 64:])
        both_cores(gram_pair_send, gram_pair_recv, turn, 15)

    def gram_start(turn):
        landed(gram_pair_recv.at[turn], recvs.at[15 + turn])
        mine = gram_pair_send[turn] + gram_pair_recv[turn]
        gram_send[turn] = mine
        gram_recv[turn, pl.ds(z, 1)] = mine[None]
        along_z(gram_send, gram_recv, turn, 13)

    def walk_start(turn):
        with scope("wait_image"):
            landed(image_recv.at[turn, pl.ds(0, nz - 1)], recvs.at[6 + turn])
        with scope("image_sum"):
            mine = jnp.sum(image_recv[turn], axis=0)
            walk_send[turn] = mine
        walk_recv[turn, pl.ds(q, 1)] = mine[None]
        to_plane(
            lambda peer: push(
                walk_send.at[turn],
                walk_recv.at[turn, q],
                sends.at[8 + turn],
                recvs.at[8 + turn],
                {"pcol": peer},
            )
        )

    def gram_landed(turn):
        landed(gram_recv.at[turn, pl.ds(0, nz - 1)], recvs.at[13 + turn])
        return unfold([jnp.sum(gram_recv[turn], axis=0)])

    def walk_landed(turn):
        with scope("wait_walk"):
            landed(walk_recv.at[turn, far], recvs.at[8 + turn])
        return [
            jnp.concatenate(
                [
                    unfold([walk_recv[turn, k + j, rows] for j in range(4)])
                    for k in range(0, nc, 4)
                ],
                axis=1,
            )
            for rows in (slice(0, 8), slice(8, 16))
        ]

    def residual(vec, l_val, e_val, gram, inverse_diag):
        with scope("products"):
            l_split = pieces(l_val)
            both = jnp.concatenate([l_split, pieces(e_val)], axis=0)
            out = sum_rows(
                lax.dot_general(l_split, both, NT, preferred_element_type=F32), 32
            )
        ray_s = out[:, :32] + out[:, 32:64] + out[:, 64:96]
        ray_h = out[:, 96:128] + out[:, 128:160] + out[:, 160:192]
        with scope("images"):
            image = jnp.dot(both, block[...], preferred_element_type=F32)
            image_s = sum_rows(image[:96], 32) * (1.0 / walkers) + STABILIZER * vec
            image_h = sum_rows(image[96:], 32) * (1.0 / walkers) * inverse_diag
            s = pieces(image_s * inverse_diag)
            right = jnp.concatenate(
                [s[:32], s[32:64], s[:32], s[64:], s[32:64], s[:32]], axis=0
            )
        with scope("eliminate"):
            coeffs = eliminate(
                ray_s * (1.0 / walkers) + STABILIZER * gram,
                ray_h * (1.0 / walkers),
                eye,
            )
        with scope("mix"):
            c = pieces(coeffs)
            left = jnp.concatenate(
                [c[:32], c[:32], c[32:64], c[:32], c[32:64], c[64:]], axis=0
            )
            out = lax.dot_general(left, right, TN, preferred_element_type=F32)
            result = image_h - out
        return result, coeffs

    def own_part(vec):
        for k in range(nc // 2):
            basis[k] = vec[:, 128 * k : 128 * k + 128]
        chunk = basis[pl.ds(q // 2, 1)][0]
        return jnp.where(q % 2 == 0, chunk[:, :64], chunk[:, 64:])

    with scope("wait_v"):
        landed(v_recv.at[far], recvs.at[0])
    top, bottom = [], []
    for k in range(0, nc, 2):
        a, b = v_recv[k], v_recv[k + 1]
        top += [a[:, :64], b[:, :64]]
        bottom += [a[:, 64:], b[:, 64:]]
    vec = jnp.concatenate(
        [jnp.concatenate(top, axis=1), jnp.concatenate(bottom, axis=1)], axis=0
    )
    image_start(vec, 0)
    with scope("ring_start"):
        ring_start()
    gram_start(0)
    walk_start(0)
    with scope("wait_block"):
        block_landed()
    squares = jnp.zeros((8, wide), F32)
    for k in range(0, walkers, 16):
        part = block[k : k + 16].astype(F32)
        part = part * part
        squares = squares + part[:8] + part[8:]
    inverse_diag = 1.0 / (
        jnp.sum(squares, axis=0, keepdims=True) * (1.0 / walkers) + STABILIZER
    )
    gram = gram_landed(0)
    with scope("ring_0"):
        ring_advance(0)
    l_val, e_val = walk_landed(0)
    vec, _ = residual(vec, l_val, e_val, gram, inverse_diag * ENLARGED)

    image_start(vec, 1)
    gram_start(1)
    with scope("ring_1"):
        ring_advance(1)
    with scope("tiles_a"):
        multiply_own()
    walk_start(1)
    with scope("tiles_b"):
        multiply_step(0)
    gram = gram_landed(1)
    norms = jnp.sum(jnp.where(eye, gram, 0.0), axis=1, keepdims=True)
    norms = norms * (1.0 / ENLARGED) * (1.0 / ENLARGED)
    scale = (1.0 / ENLARGED) / jnp.sqrt(norms * (1.0 / params) + EPSILON)
    gram = gram * scale * to_row(scale, eye)
    vec = vec * scale
    first_block = vec
    with scope("ring_2"):
        ring_advance(2)
    l_val, e_val = walk_landed(1)
    vec, coeffs = residual(vec, l_val * scale, e_val * scale, gram, inverse_diag)
    norms = to_row(jnp.sum(vec * vec, axis=1, keepdims=True), eye)
    norm_send[...] = jnp.concatenate([norms, jnp.zeros((1, 96), F32)], axis=1)
    norm_recv[pl.ds(p, 1)] = norm_send[...][None]

    for row in rows:
        push(norm_send, norm_recv.at[p], sends.at[3], recvs.at[3], {"prow": row})
    block_sent()
    ray_ref[...] = coeffs
    two_ref[...] = own_part(vec)
    one_ref[...] = own_part(first_block)
    with scope("tiles_c"):
        multiply_step(1)
        multiply_step(2)
    with scope("ring_3"):
        ring_advance(3)
    with scope("tiles_d"):
        multiply_step(3)
    ring_sent()
    sent(gathered.at[0, pl.ds(0, 32 * (nc - 1))], sends.at[1])
    for turn in range(2):
        sent(pair_send.at[turn], sends.at[4 + turn])
        sent(gram_pair_send.at[turn], sends.at[15 + turn])
        sent(image_recv.at[turn, pl.ds(0, nz - 1)], sends.at[6 + turn])
        sent(gram_recv.at[turn, pl.ds(0, nz - 1)], sends.at[13 + turn])
        sent(walk_recv.at[turn, far], sends.at[8 + turn])
    with scope("wait_norm"):
        landed(norm_recv.at[pl.ds(0, nr - 1)], recvs.at[3])
    norms_ref[...] = jnp.sum(norm_recv[...], axis=0)
    sent(norm_recv.at[pl.ds(0, nr - 1)], sends.at[3])


def write(
    params,
    tiles,
    one,
    two,
    ray,
    norms,
    corr_ref,
    ham_ref,
    one_ref,
    two_ref,
    ray_ref,
    scaled,
    sems,
):
    rows = tiles.shape[1] // 4
    pairs = []
    for k in range(4):
        part = pl.ds(k * rows, rows)
        pairs.append((tiles.at[0, part], corr_ref.at[0, part]))
        pairs.append((tiles.at[1, part], ham_ref.at[0, part]))
    pairs += [(one, one_ref), (ray, ray_ref), (scaled, two_ref)]
    writes = [
        pltpu.make_async_copy(src, dst, sems.at[i])
        for i, (src, dst) in enumerate(pairs)
    ]
    for copy in writes[:-1]:
        copy.start()
    eye = lax.broadcasted_iota(jnp.int32, (32, 32), 0) == lax.broadcasted_iota(
        jnp.int32, (32, 32), 1
    )
    squares = to_column(norms[:, :32], eye)
    scaled[...] = two[...] * (1.0 / jnp.sqrt(squares * (1.0 / params) + EPSILON))
    writes[-1].start()
    for copy in writes:
        copy.wait()


def local(nr, nc, log_derivs, energy_derivs, start_block):
    wide, walkers, narrow = 64 * nc, 32 * nc, 64 * nr
    nz = nr // 2
    vmem = pl.BlockSpec(memory_space=pltpu.VMEM)
    full = nz // 2 - 1
    hbm = pl.BlockSpec(memory_space=pltpu.HBM)
    small = (
        jax.ShapeDtypeStruct((32, 64), F32),
        jax.ShapeDtypeStruct((32, 64), F32),
        jax.ShapeDtypeStruct((32, 32), F32),
    )
    arguments = (log_derivs, energy_derivs, start_block.T)
    results = pl.pallas_call(
        functools.partial(davidson, nr, nc),
        out_shape=(
            pltpu.VMEM((2, wide, narrow), F32),
            *(pltpu.VMEM(x.shape, F32) for x in small),
            pltpu.VMEM((1, 128), F32),
        ),
        in_specs=[hbm] * 3,
        out_specs=(vmem,) * 5,
        scratch_shapes=[
            pltpu.VMEM((32, wide), BF16),
            pltpu.VMEM((32, wide), BF16),
            pltpu.VMEM((32, 64), F32),
            pltpu.VMEM((walkers, wide), BF16),
            pltpu.VMEM((wide, walkers), BF16),
            pltpu.VMEM((nc, 32, 128), BF16),
            pltpu.VMEM((nr, walkers, 128), BF16),
            pltpu.VMEM((16, 128), F32),
            pltpu.VMEM((nc, 16, 128), F32),
            pltpu.VMEM((wide, 64), BF16),
            pltpu.VMEM((96, wide), BF16),
            pltpu.VMEM((nc // 2, 32, 128), F32),
            pltpu.VMEM((2, 16, 128), F32),
            pltpu.VMEM((2, 16, 128), F32),
            pltpu.VMEM((2, 16, 128), F32),
            pltpu.VMEM((2, nz, 16, 128), F32),
            pltpu.VMEM((2, 8, 128), F32),
            pltpu.VMEM((2, 8, 128), F32),
            pltpu.VMEM((2, 8, 128), F32),
            pltpu.VMEM((2, nz, 8, 128), F32),
            pltpu.VMEM((2, 16, 128), F32),
            pltpu.VMEM((2, nc, 16, 128), F32),
            pltpu.VMEM((1, 128), F32),
            pltpu.VMEM((nr, 1, 128), F32),
            pltpu.SemaphoreType.DMA((3,)),
            pltpu.SemaphoreType.DMA((17,)),
            pltpu.SemaphoreType.DMA((17,)),
            pltpu.SemaphoreType.DMA((4, 2, full + 2)),
        ],
        compiler_params=pltpu.CompilerParams(
            collective_id=0, has_side_effects=True, vmem_limit_bytes=24 * 1024 * 1024
        ),
        name="davidson",
    )(*(pltpu.with_memory_space_constraint(x, pltpu.HBM) for x in arguments))

    corr, ham, one, two, ray = pl.pallas_call(
        functools.partial(write, 64 * nc * nr),
        out_shape=(
            jax.ShapeDtypeStruct((1, wide, narrow), F32),
            jax.ShapeDtypeStruct((1, wide, narrow), F32),
            *small,
        ),
        in_specs=[vmem] * 5,
        out_specs=(hbm,) * 5,
        scratch_shapes=[pltpu.VMEM((32, 64), F32), pltpu.SemaphoreType.DMA((11,))],
        compiler_params=pltpu.CompilerParams(vmem_limit_bytes=24 * 1024 * 1024),
        name="tiles",
    )(*(pltpu.with_memory_space_constraint(x, pltpu.VMEM) for x in results))
    return one.T, two.T, ray, corr, ham


def solution(mesh):
    return jax.shard_map(
        functools.partial(local, mesh.shape["prow"], mesh.shape["pcol"]),
        mesh=mesh,
        in_specs=(P("pcol", "prow"), P("pcol", "prow"), P(("prow", "pcol"), None)),
        out_specs=(
            P(("prow", "pcol"), None),
            P(("prow", "pcol"), None),
            P(),
            P("pcol", "prow", None),
            P("pcol", "prow", None),
        ),
        check_vma=False,
    )
```
